32 devices in a mesh: leaf: 8 (over z, y), level: 4 (over x, core).
Axes of the slice: x: 2, y: 2, z: 4, core: 2. Of those that a mesh axis runs over, the one named last changes fastest.
Arguments:
- points_x: bfloat16 [256, 16384], P(None, ('leaf', 'level')), may hold values from -6 to 6
- leaf_basis: bfloat16 [32, 512, 256], P(('leaf', 'level')), may hold values from -0.25 to 0.25
- near_tiles: bfloat16 [32, 4, 512, 512], P(('leaf', 'level')), may hold values from -0.25 to 0.25
- near_cols: int32 [32, 4], P(('leaf', 'level')), may hold values from 0 to 11, as said below
- near_count: int32 [32], P(('leaf', 'level')), may hold values from 3 to 4, as said below
- transfer: bfloat16 [2, 256, 256], replicated, may hold values from -0.3125 to 0.3125
- coupling: bfloat16 [6, 2, 256, 256], replicated, may hold values from -0.375 to 0.375
- couple_mask: int32 [6, 8, 2], replicated, may hold values 0 or 1
Outputs:
- kernel_product: bfloat16 [256, 16384], P(None, ('leaf', 'level'))
The draws below stay inside these ranges and needn't reach their ends.
Inputs may be any that keep to these rules, and one draw needn't show every extreme that they name: Slots 0, 1 and 2 of leaf L name L itself, L - 1 and L + 1 (near_cols 4 + L mod 4, one less, one more); slot 3 names any leaf of the previous, own or next group; some leaf's slot 3 names 0 and some names 11. The live slots of a leaf are its first near_count slots; in every draw some leaf has 3 and some has 4 live slots.
All inputs are finite; a program needn't handle non-finite values.
Results may differ from the reference program's by a relative error of at most 0.015.
Values may be sent and summed in bfloat16 or wider, within the bound.
No kernel may reach another device: no remote copies, remote signals or barrier semaphores. Data moves between devices by JAX's collectives and lax.ppermute only.
A program may use at most 64 MiB of HBM per device.

```python
import jax
import jax.numpy as jnp
from jax import lax

LEAF_PTS = 512
RANK = 256
VECS = 256
NEAR_SLOTS = 4
LEVELS = 6
GROUPS = 8
NLEAF = 32
NPTS = 16384
N_LEAF = 8
N_LEVEL = 4


def draw_near_count(key, part):
    key_busy, key_forced = jax.random.split(jax.random.fold_in(key, 17), 2)
    busy_flag = jax.random.randint(key_busy, (NLEAF,), 0, 5) == 0
    tile_count = jnp.where(busy_flag, NEAR_SLOTS, 3)
    forced_at = jax.random.randint(key_forced, (), 0, NLEAF)
    tile_count = tile_count.at[forced_at].set(NEAR_SLOTS)
    tile_count = tile_count.at[(forced_at + NLEAF // 2) % NLEAF].set(3)
    return tile_count.astype(jnp.int32)


def draw_near_cols(key, part):
    key_extra, key_forced = jax.random.split(jax.random.fold_in(key, 29), 2)
    leaf_ids = jnp.arange(NLEAF, dtype=jnp.int32)
    own_col = N_LEVEL + leaf_ids % N_LEVEL
    extra = jax.random.randint(key_extra, (NLEAF,), 0, 3 * N_LEVEL)
    forced_at = jax.random.randint(key_forced, (), 0, NLEAF)
    extra = extra.at[forced_at].set(0)
    extra = extra.at[(forced_at + NLEAF // 2) % NLEAF].set(3 * N_LEVEL - 1)
    return jnp.stack([own_col, own_col - 1, own_col + 1, extra], axis=1).astype(jnp.int32)


def set_ends(result, rng, smallest, top_value):
    longest = result.shape.index(max(result.shape))
    spots = []
    for shift in (0, 1):
        where = [jax.random.randint(jax.random.fold_in(rng, axis), (), 0, length) for axis, length in enumerate(result.shape)]
        where[longest] = (where[longest] + shift) % result.shape[longest]
        spots.append(tuple(where))
    return result.at[spots[0]].set(smallest).at[spots[1]].set(top_value)


def levels(key, dims, cuts, least, top_value):
    level, own = 1.0, jax.random.fold_in(key, 6)
    for dim, parts in cuts:
        steps = jnp.exp(jax.random.uniform(jax.random.fold_in(own, dim), (parts,), jnp.float32, least / len(cuts), top_value / len(cuts)))
        level = level * jnp.repeat(steps, dims[dim] // parts).reshape([-1 if axis == dim else 1 for axis in range(len(dims))])
    return level


def noise(stream_key, shape, width, reach, cuts=(), kind=jnp.bfloat16):
    drawn = width * jax.random.normal(stream_key, shape, jnp.float32)
    if cuts:
        drawn = drawn * levels(stream_key, shape, cuts, -0.22, 0.18)
    return jnp.clip(drawn, -reach, reach).astype(kind)


def setup_inputs(seed: int = 0) -> dict:
    splits = jax.random.split(jax.random.key(seed), 9)
    return {
        "points_x": noise(splits[0], (VECS, NPTS), 1.0, 6.0, ((1, 32),)),
        "leaf_basis": noise(splits[1], (NLEAF, LEAF_PTS, RANK), LEAF_PTS ** -0.5, 0.25, ((0, 32),)),
        "near_tiles": noise(splits[2], (NLEAF, NEAR_SLOTS, LEAF_PTS, LEAF_PTS), LEAF_PTS ** -0.5, 0.25, ((0, 32),)),
        "near_cols": draw_near_cols(jax.random.fold_in(splits[8], 71), 0),
        "near_count": draw_near_count(jax.random.fold_in(splits[8], 71), 0),
        "transfer": noise(splits[5], (2, RANK, RANK), (RANK * 3 // 2) ** -0.5, 0.3125),
        "coupling": noise(splits[6], (LEVELS, 2, RANK, RANK), RANK ** -0.5, 0.375),
        "couple_mask": set_ends((jax.random.randint(splits[7], (LEVELS, GROUPS, 2), 0, 2) < 1).astype(jnp.int32), jax.random.fold_in(splits[7], 1), 0, 1),
    }


def pair_up(coefs, transfer):
    lower_coef = coefs[0::2].astype(jnp.float32)
    upper_coef = coefs[1::2].astype(jnp.float32)
    summed = jnp.einsum("kvr,rs->kvs", lower_coef, transfer[0].astype(jnp.float32))
    summed = summed + jnp.einsum("kvr,rs->kvs", upper_coef, transfer[1].astype(jnp.float32))
    return summed.astype(jnp.bfloat16)


def split_down(fields, transfer):
    parent = fields.astype(jnp.float32)
    toward_lower = jnp.einsum("kvs,rs->kvr", parent, transfer[0].astype(jnp.float32))
    toward_upper = jnp.einsum("kvs,rs->kvr", parent, transfer[1].astype(jnp.float32))
    stacked = jnp.stack([toward_lower, toward_upper], axis=1)
    return stacked.reshape((2 * fields.shape[0],) + fields.shape[1:])


def couple_level(coefs, matrices, mask_rows):
    cluster_count = coefs.shape[0]
    coupled = jnp.zeros(coefs.shape, jnp.float32)
    wide_coefs = coefs.astype(jnp.float32)
    for pick_idx, offset in enumerate((2, 3)):
        if offset < cluster_count:
            matrix = matrices[pick_idx].astype(jnp.float32)
            zero_pad = jnp.zeros((offset,) + coefs.shape[1:], jnp.float32)
            ahead_coef = jnp.concatenate([wide_coefs[offset:], zero_pad], axis=0)
            behind = jnp.concatenate([zero_pad, wide_coefs[:cluster_count - offset]], axis=0)
            ahead_mask = mask_rows[:cluster_count, pick_idx].astype(jnp.float32)
            behind_mask = jnp.concatenate([jnp.zeros((offset,), jnp.float32), mask_rows[:cluster_count - offset, pick_idx].astype(jnp.float32)])
            coupled = coupled + ahead_mask[:, None, None] * jnp.einsum("kvr,rs->kvs", ahead_coef, matrix)
            coupled = coupled + behind_mask[:, None, None] * jnp.einsum("kvs,rs->kvr", behind, matrix)
    return coupled


def reference(points_x, leaf_basis, near_tiles, near_cols, near_count, transfer, coupling, couple_mask):
    vectors = points_x.shape[0]
    leaves = leaf_basis.shape[0]
    points = leaf_basis.shape[1]
    by_leaf = points_x.reshape(vectors, leaves, points).transpose(1, 0, 2)

    def leaf_coef(operands):
        return jnp.dot(operands[0], operands[1], preferred_element_type=jnp.float32).astype(jnp.bfloat16)

    level_coefs = lax.map(leaf_coef, (by_leaf, leaf_basis))
    group_bits = N_LEVEL.bit_length() - 1
    leaf_bits = N_LEAF.bit_length() - 1
    active = min(LEVELS, leaf_bits + 1)
    for step_idx in range(group_bits):
        level_coefs = pair_up(level_coefs, transfer)
    coarse = [level_coefs]
    for level_idx in range(1, active):
        coarse.append(pair_up(coarse[-1], transfer))
    couplings = [couple_level(coarse[level_idx], coupling[level_idx], couple_mask[level_idx]) for level_idx in range(active)]
    fields = couplings[active - 1].astype(jnp.bfloat16)
    for level_idx in range(active - 2, -1, -1):
        fields = (split_down(fields, transfer) + couplings[level_idx]).astype(jnp.bfloat16)
    for step_idx in range(group_bits):
        fields = split_down(fields, transfer).astype(jnp.bfloat16)

    group_width = N_LEVEL * points
    padded_x = jnp.pad(points_x, ((0, 0), (group_width, group_width)))

    def finish(leaf_items):
        tile_set, columns, tile_count, fields_leaf, leaf_map, leaf_id = leaf_items
        window_start = (leaf_id // N_LEVEL) * group_width
        window_x = lax.dynamic_slice_in_dim(padded_x, window_start.astype(jnp.int32), 3 * group_width, 1)
        running_sum = jnp.dot(fields_leaf, leaf_map.T, preferred_element_type=jnp.float32)
        for slot_idx in range(NEAR_SLOTS):
            column_x = lax.dynamic_slice_in_dim(window_x, (columns[slot_idx] * points).astype(jnp.int32), points, 1)
            tile_block = tile_set[slot_idx]
            running_sum = lax.cond(slot_idx < tile_count,
                                   lambda running: running + jnp.dot(column_x, tile_block, preferred_element_type=jnp.float32),
                                   lambda running: running, running_sum)
        return running_sum.astype(jnp.bfloat16)

    leaf_ids = jnp.arange(leaves, dtype=jnp.int32)
    blocks = lax.map(finish, (near_tiles, near_cols, near_count, fields, leaf_basis, leaf_ids))
    return blocks.transpose(1, 0, 2).reshape(vectors, leaves * points)
```

```python
from functools import partial

import jax
import jax.numpy as jnp
from jax import lax
from jax.experimental import pallas as pl
from jax.experimental.pallas import tpu as pltpu
from jax.sharding import PartitionSpec as P

VMEM_LIMIT = 48 * 1024 * 1024
F32 = jnp.float32
BF16 = jnp.bfloat16


def dot(a, b):
    return jnp.dot(a, b, preferred_element_type=F32)


def dot_t(a, b):
    return lax.dot_general(a, b, (((1,), (1,)), ((), ())), preferred_element_type=F32)


def vmem(count):
    return [pl.BlockSpec(memory_space=pltpu.VMEM)] * count


def smem(count):
    return [pl.BlockSpec(memory_space=pltpu.SMEM)] * count


def params():
    return pltpu.CompilerParams(vmem_limit_bytes=VMEM_LIMIT)


def up_kernel(bits, x_ref, basis_ref, transfer_ref, z_ref, w_ref):
    pos = lax.axis_index("level")
    w = basis_ref[0]
    for bit in range(bits):
        w = dot(w, transfer_ref[pos >> bit & 1]).astype(BF16)
    w_ref[...] = w
    z_ref[...] = dot(x_ref[...], w).astype(BF16)


def up(x, basis, transfer, bits):
    vectors, points = x.shape
    rank = basis.shape[2]
    return pl.pallas_call(
        partial(up_kernel, bits),
        out_shape=(
            jax.ShapeDtypeStruct((vectors, rank), BF16),
            jax.ShapeDtypeStruct((points, rank), BF16),
        ),
        in_specs=vmem(3),
        out_specs=tuple(vmem(2)),
        compiler_params=params(),
        name="up",
    )(x, basis, transfer)


def level_plan(leaf_count, levels):
    active = min(levels, leaf_count.bit_length())
    coupled = [lev for lev in range(active) if 2 < (leaf_count >> lev)]
    return coupled


def far_kernel(plan, coef_ref, coupling_ref, transfer_ref, mask_ref, field_ref, *scratch):
    leaf_pos = lax.axis_index("leaf")
    count, rows, rank = coef_ref.shape
    level_refs = [coef_ref, *scratch]
    chunk = 8
    for lev in range(1, len(plan)):
        source, target = level_refs[lev - 1], level_refs[lev]
        parents = count >> lev
        step = min(chunk, parents)

        def join(at, source=source, target=target, step=step):
            lower = jnp.concatenate([source[2 * (at + i)] for i in range(step)], axis=0)
            upper = jnp.concatenate([source[2 * (at + i) + 1] for i in range(step)], axis=0)
            made = (dot(lower, transfer_ref[0]) + dot(upper, transfer_ref[1])).astype(BF16)
            for i in range(step):
                target[at + i] = made[i * rows : (i + 1) * rows]

        if parents <= step:
            join(0)
        else:
            pl.loop(0, parents // step)(lambda i, join=join, step=step: join(i * step))
    field = None
    for lev in reversed(plan):
        coefs = level_refs[lev]
        clusters = count >> lev
        cluster = leaf_pos >> lev
        total = jnp.zeros((rows, rank), F32)
        if field is not None:
            total = dot_t(field, transfer_ref[leaf_pos >> lev & 1])
        for pick, offset in enumerate((2, 3)):
            if offset < clusters:
                matrix = coupling_ref[lev, pick]
                ahead = jnp.minimum(cluster + offset, clusters - 1)
                behind = jnp.maximum(cluster - offset, 0)
                ahead_on = jnp.where(cluster + offset < clusters, mask_ref[lev, cluster, pick], 0)
                behind_on = jnp.where(cluster >= offset, mask_ref[lev, behind, pick], 0)
                total = total + ahead_on.astype(F32) * dot(coefs[ahead], matrix)
                total = total + behind_on.astype(F32) * dot_t(coefs[behind], matrix)
        field = total.astype(BF16)
    if field is None:
        field = jnp.zeros((rows, rank), BF16)
    field_ref[...] = field


def far(coefs, coupling, transfer, mask):
    count, rows, rank = coefs.shape
    plan = level_plan(count, coupling.shape[0])
    used = max(1, len(plan))
    scratch = [pltpu.VMEM((count >> lev, rows, rank), BF16) for lev in range(1, len(plan))]
    return pl.pallas_call(
        partial(far_kernel, plan),
        out_shape=jax.ShapeDtypeStruct((rows, rank), BF16),
        grid=(1,),
        in_specs=[
            pl.BlockSpec(coefs.shape, lambda i: (0, 0, 0)),
            pl.BlockSpec((used,) + coupling.shape[1:], lambda i: (0, 0, 0, 0)),
            pl.BlockSpec(transfer.shape, lambda i: (0, 0, 0)),
        ]
        + smem(1),
        out_specs=pl.BlockSpec((rows, rank), lambda i: (0, 0)),
        scratch_shapes=scratch,
        compiler_params=params(),
        name="far",
    )(coefs, coupling, transfer, mask)


def finish_kernel(
    group_size, x_ref, left_ref, right_ref, mate_ref, cross_ref, tiles_ref, field_ref, w_ref,
    cols_ref, count_ref, out_ref, acc_ref
):
    pos = lax.axis_index("level")
    odd = pos & 1
    acc = dot(x_ref[...], tiles_ref[0, 0])
    acc = acc + dot(mate_ref[1], tiles_ref[0, 2 - odd])
    acc = acc + dot(cross_ref[0], tiles_ref[0, 1 + odd])
    acc_ref[...] = acc + dot_t(field_ref[...], w_ref[...])
    col = cols_ref[0, 3]
    group, place = col // group_size, lax.rem(col, group_size)
    live = count_ref[0] > 3
    tile = tiles_ref.at[0, 3]
    own = jnp.logical_and(live, place == pos)

    for at, block in enumerate((left_ref, x_ref, right_ref)):
        @pl.when(jnp.logical_and(own, group == at))
        def _(block=block):
            acc_ref[...] += dot(block[...], tile[...])

    @pl.when(jnp.logical_and(live, place == (pos ^ 1)))
    def _():
        acc_ref[...] += dot(mate_ref[group], tile[...])

    @pl.when(jnp.logical_and(live, (place >> 1) != (pos >> 1)))
    def _():
        acc_ref[...] += dot(cross_ref[1], tile[...])

    out_ref[...] = acc_ref[...].astype(BF16)


def finish(group_size, x, left, right, mate, cross, tiles, field, w, cols, count):
    vectors, points = x.shape
    return pl.pallas_call(
        partial(finish_kernel, group_size),
        out_shape=jax.ShapeDtypeStruct((vectors, points), BF16),
        in_specs=vmem(8) + smem(2),
        out_specs=vmem(1)[0],
        scratch_shapes=[pltpu.VMEM((vectors, points), F32)],
        compiler_params=params(),
        name="finish",
    )(x, left, right, mate, cross, tiles, field, w, cols, count)


def per_device(
    points_x, leaf_basis, near_tiles, near_cols, near_count, transfer, coupling, couple_mask
):
    group_size = lax.axis_size("level")
    leaf_count = lax.axis_size("leaf")
    pos = lax.axis_index("level")
    vectors, points = points_x.shape
    rank = leaf_basis.shape[2]
    assert group_size == 4
    group_bits = group_size.bit_length() - 1
    rows = vectors // group_size

    ahead = [(i, i + 1) for i in range(leaf_count - 1)]
    left = lax.ppermute(points_x, "leaf", ahead)
    right = lax.ppermute(points_x, "leaf", [(b, a) for a, b in ahead])
    far_col = lax.ppermute(near_cols[0, 3:], "level", [(i, i ^ 2) for i in range(group_size)])[0]

    z, w = up(points_x, leaf_basis, transfer, group_bits)
    parts = lax.all_to_all(z.reshape(group_size, rows, rank), "level", 0, 0)
    coef = parts.astype(F32).sum(0).astype(BF16)
    coefs = lax.all_gather(coef, "leaf", axis=0)
    field = far(coefs, coupling, transfer, couple_mask)
    field = lax.all_gather(field, "level", axis=0, tiled=True)

    mine = jnp.stack([left, points_x, right])
    mate = lax.ppermute(mine, "level", [(i, i ^ 1) for i in range(group_size)])
    beside = mate[jnp.where(pos == 1, 2, jnp.where(pos == 2, 0, 1))]
    group, place = far_col // group_size, far_col % group_size
    picked = jnp.where(place == pos, mine[group], mate[group])
    cross = lax.ppermute(
        jnp.stack([beside, picked]), "level", [(i, i ^ 2) for i in range(group_size)]
    )
    return finish(
        group_size, points_x, left, right, mate, cross, near_tiles, field, w, near_cols, near_count
    )


def solution(mesh):
    in_specs = (
        P(None, ("leaf", "level")),
        P(("leaf", "level"), None, None),
        P(("leaf", "level"), None, None, None),
        P(("leaf", "level"), None),
        P(("leaf", "level")),
        P(),
        P(),
        P(),
    )
    out_specs = P(None, ("leaf", "level"))
    return jax.shard_map(
        per_device, mesh=mesh, in_specs=in_specs, out_specs=out_specs, check_vma=False
    )
```

```python
from functools import partial

import jax
import jax.numpy as jnp
from jax import lax
from jax.experimental import pallas as pl
from jax.experimental.pallas import tpu as pltpu
from jax.sharding import PartitionSpec as P

VMEM_LIMIT = 32 * 1024 * 1024
F32 = jnp.float32
BF16 = jnp.bfloat16
GROUP = 4


def dot(a, b):
    return jnp.dot(a, b, preferred_element_type=F32)


def dot_t(a, b):
    return lax.dot_general(a, b, (((1,), (1,)), ((), ())), preferred_element_type=F32)


def call(kernel, name, flops, inputs, scalars, outputs, scratch=()):
    shapes = [jax.ShapeDtypeStruct(shape, dtype) for shape, dtype in outputs]
    moved = sum(a.size * a.dtype.itemsize for a in inputs) + sum(
        s.size * s.dtype.itemsize for s in shapes
    )
    return pl.pallas_call(
        kernel,
        out_shape=shapes,
        in_specs=[pl.BlockSpec(memory_space=pltpu.VMEM)] * len(inputs)
        + [pl.BlockSpec(memory_space=pltpu.SMEM)] * len(scalars),
        out_specs=[pl.BlockSpec(memory_space=pltpu.VMEM)] * len(outputs),
        scratch_shapes=list(scratch),
        compiler_params=pltpu.CompilerParams(vmem_limit_bytes=VMEM_LIMIT),
        cost_estimate=pl.CostEstimate(flops=flops, bytes_accessed=moved, transcendentals=0),
        name=name,
    )(*inputs, *scalars)


def up_kernel(bits, x_ref, basis_ref, transfer_ref, *refs):
    *share_refs, w_ref, z_ref = refs
    pos = lax.axis_index("level")
    w = basis_ref[0]
    for bit in range(bits):
        w = dot(w, transfer_ref[pos >> bit & 1]).astype(BF16)
    w_ref[...] = w
    z = dot(x_ref[...], w).astype(BF16)
    rows = z_ref.shape[1]
    for member in range(GROUP):
        z_ref[member] = z[member * rows : (member + 1) * rows]
    for turn, share_ref in enumerate(share_refs):
        share_ref[...] = z_ref[pos ^ turn]


def push_kernel(
    turns, pairs, clusters, own_ref, mate_ref, coupling_ref, transfer_ref, mask_ref, *refs
):
    *push_refs, both_ref, pair_ref = refs
    leaf_pos = lax.axis_index("leaf")
    pair, side = leaf_pos >> 1, leaf_pos & 1
    both_ref[side] = own_ref[...]
    both_ref[1 - side] = mate_ref[...]
    total = dot(both_ref[0], transfer_ref[0]) + dot(both_ref[1], transfer_ref[1])
    pair_ref[...] = total.astype(BF16)

    def term(lev, coef, gap, source, target):
        pick = abs(gap) - 2
        matrix = coupling_ref[lev, pick]
        switch = mask_ref[lev, source if gap > 0 else target, pick].astype(F32)
        return switch * (dot_t(coef, matrix) if gap > 0 else dot(coef, matrix))

    def fill(push_ref, distance, to_side):
        target_pair = pair + distance
        total = None
        if abs(distance) in (2, 3) and clusters[1]:
            coupled = term(1, pair_ref[...], distance, pair, target_pair).astype(BF16)
            total = dot_t(coupled, transfer_ref[to_side])
        for from_side in (0, 1):
            gap = 2 * distance + to_side - from_side
            if abs(gap) in (2, 3) and clusters[0]:
                more = term(
                    0, both_ref[from_side], gap, 2 * pair + from_side, 2 * target_pair + to_side
                )
                total = more if total is None else total + more
        if total is None:
            total = jnp.zeros(push_ref.shape, F32)
        push_ref[...] = total.astype(BF16)

    for turn, push_ref in zip(turns, push_refs):
        for distance in (turn, turn - pairs) if len(turns) < 6 else (turn,):
            target_pair = pair + distance
            inside = jnp.logical_and(target_pair >= 0, target_pair < pairs)
            for to_side in (0, 1):
                @pl.when(jnp.logical_and(inside, side == to_side))
                def _(push_ref=push_ref, distance=distance, to_side=to_side):
                    fill(push_ref, distance, to_side)


def pick_kernel(x_ref, mate_ref, across_ref, corner_ref, left_cols, right_cols, to_left, to_right):
    pos = lax.axis_index("level")
    for cols, out in ((left_cols, to_left), (right_cols, to_right)):
        turn = lax.rem(cols[0, 3], GROUP) ^ pos
        for at, block in enumerate((x_ref, mate_ref, across_ref, corner_ref)):
            @pl.when(turn == at)
            def _(block=block, out=out):
                out[...] = block[...]


def near_kernel(
    x_ref, mate_ref, across_ref, corner_ref, edge_ref, tiles_ref, cols_ref, count_ref, acc_ref
):
    pos = lax.axis_index("level")
    odd = pos & 1
    inner = jnp.logical_or(pos == 1, pos == 2)
    acc = dot(x_ref[...], tiles_ref[0, 0]) + dot(mate_ref[...], tiles_ref[0, 2 - odd])
    beside = jnp.where(inner, corner_ref[...], edge_ref[...])
    acc_ref[...] = acc + dot(beside, tiles_ref[0, 1 + odd])
    col = cols_ref[0, 3]
    turn = lax.rem(col, GROUP) ^ pos
    here = jnp.logical_and(count_ref[0] > 3, col // GROUP == 1)
    for at, block in enumerate((x_ref, mate_ref, across_ref, corner_ref)):
        @pl.when(jnp.logical_and(here, turn == at))
        def _(block=block):
            acc_ref[...] += dot(block[...], tiles_ref[0, 3])


def finish_kernel(
    acc_ref, left_ref, right_ref, tiles_ref, w_ref, field0, field1, field2, field3,
    cols_ref, count_ref, out_ref, total_ref, field_ref
):
    pos = lax.axis_index("level")
    for turn, share_ref in enumerate((field0, field1, field2, field3)):
        field_ref[pos ^ turn] = share_ref[...]
    field = jnp.concatenate([field_ref[member] for member in range(GROUP)], axis=0)
    total_ref[...] = acc_ref[...] + dot_t(field, w_ref[...])
    group = cols_ref[0, 3] // GROUP
    live = count_ref[0] > 3
    for at, block in ((0, left_ref), (2, right_ref)):
        @pl.when(jnp.logical_and(live, group == at))
        def _(block=block):
            total_ref[...] += dot(block[...], tiles_ref[0, 3])
    out_ref[...] = total_ref[...].astype(BF16)


def turned(value, turn):
    return lax.ppermute(value, "level", [(i, i ^ turn) for i in range(GROUP)])


def shifted(value, steps):
    count = lax.axis_size("leaf")
    route = [(i, i + steps) for i in range(count) if 0 <= i + steps < count]
    return lax.ppermute(value, "leaf", route)


def swapped(value, distance):
    count = lax.axis_size("leaf")
    return lax.ppermute(value, "leaf", [(i, i ^ 1 << distance) for i in range(count)])


def upper_field(coef, coupling, transfer, couple_mask):
    leaf_count = lax.axis_size("leaf")
    leaf_pos = lax.axis_index("leaf")
    couplings = []
    levels = range(2, min(coupling.shape[0], leaf_count.bit_length()))
    for lev in levels:
        other = swapped(coef, lev - 1)
        is_upper = (leaf_pos >> lev - 1 & 1) == 1
        total = dot(jnp.where(is_upper, other, coef), transfer[0])
        total = total + dot(jnp.where(is_upper, coef, other), transfer[1])
        coef = total.astype(BF16)
        cluster = leaf_pos >> lev
        coupled = jnp.zeros(coef.shape, F32)
        for pick, offset in enumerate((2, 3)):
            if offset < leaf_count >> lev:
                matrix = coupling[lev, pick]
                ahead = shifted(coef, -(offset << lev))
                behind = shifted(coef, offset << lev)
                ahead_mask = couple_mask[lev, cluster, pick].astype(F32)
                behind_mask = couple_mask[lev, jnp.maximum(cluster - offset, 0), pick].astype(F32)
                coupled = coupled + ahead_mask * dot(ahead, matrix)
                coupled = coupled + behind_mask * dot_t(behind, matrix)
        couplings.append(coupled)
    field = jnp.zeros(coef.shape, F32)
    for lev, coupled in zip(reversed(levels), reversed(couplings)):
        if lev + 1 in levels:
            field = dot_t(field.astype(BF16), transfer[leaf_pos >> lev & 1])
        field = field + coupled
    for lev in (1, 0):
        field = dot_t(field.astype(BF16), transfer[leaf_pos >> lev & 1])
    return field


def per_device(
    points_x, leaf_basis, near_tiles, near_cols, near_count, transfer, coupling, couple_mask
):
    assert lax.axis_size("level") == GROUP
    leaf_count = lax.axis_size("leaf")
    vectors, points = points_x.shape
    rank = leaf_basis.shape[2]
    rows = vectors // GROUP
    bits = GROUP.bit_length() - 1
    block = ((vectors, points), BF16)
    share = ((rows, rank), BF16)
    cube = 2 * rank * rank

    across = turned(points_x, 2)
    mate = turned(points_x, 1)
    joints = [(GROUP * g - 1, GROUP * g) for g in range(1, leaf_count)]
    edge = lax.ppermute(points_x, ("leaf", "level"), joints + [(b, a) for a, b in joints])
    left_cols = shifted(near_cols, 1)
    right_cols = shifted(near_cols, -1)
    corner = turned(across, 1)

    *shares, w = call(
        partial(up_kernel, bits), "up", cube * (vectors + bits * points) * 2,
        [points_x, leaf_basis, transfer], [], [share] * GROUP + [((points, rank), BF16)],
        [pltpu.VMEM((GROUP, rows, rank), BF16)],
    )
    coef = shares[0].astype(F32)
    for turn in range(1, GROUP):
        coef = coef + turned(shares[turn], turn).astype(F32)
    coef = coef.astype(BF16)

    levels = coupling.shape[0]
    active = min(levels, leaf_count.bit_length())
    pairs = leaf_count // 2
    turns = [1, 2, 3] if pairs == 4 else [1, 2, 3, -1, -2, -3]
    clusters = [lev < active and (leaf_count >> lev) > 2 for lev in (0, 1)]
    *pushes, _, pair_coef = call(
        partial(push_kernel, turns, pairs, clusters), "push", cube * rows * 10,
        [coef, swapped(coef, 0), coupling, transfer], [couple_mask],
        [share] * len(turns) + [((2, rows, rank), BF16), share],
    )
    field = None
    for turn, push in zip(turns, pushes):
        if len(turns) < 6:
            route = [(i, (i + 2 * turn) % leaf_count) for i in range(leaf_count)]
            came = lax.ppermute(push, "leaf", route)
        else:
            came = shifted(push, 2 * turn)
        field = came.astype(F32) if field is None else field + came.astype(F32)
    if active > 2 and (leaf_count >> 2) > 2:
        field = field + upper_field(pair_coef, coupling, transfer, couple_mask)
    field = field.astype(BF16)
    fields = [field] + [turned(field, turn) for turn in range(1, GROUP)]

    to_left, to_right = call(
        pick_kernel, "pick", 0, [points_x, mate, across, corner], [left_cols, right_cols],
        [block] * 2,
    )
    from_left = shifted(to_right, 1)
    from_right = shifted(to_left, -1)
    (acc,) = call(
        near_kernel, "near", 8 * vectors * points * points,
        [points_x, mate, across, corner, edge, near_tiles], [near_cols, near_count],
        [((vectors, points), F32)],
    )
    (out,) = call(
        finish_kernel, "finish", 4 * vectors * points * points,
        [acc, from_left, from_right, near_tiles, w, *fields], [near_cols, near_count],
        [block], [pltpu.VMEM((vectors, points), F32), pltpu.VMEM((GROUP, rows, rank), BF16)],
    )
    return out


def solution(mesh):
    in_specs = (
        P(None, ("leaf", "level")),
        P(("leaf", "level"), None, None),
        P(("leaf", "level"), None, None, None),
        P(("leaf", "level"), None),
        P(("leaf", "level")),
        P(),
        P(),
        P(),
    )
    out_specs = P(None, ("leaf", "level"))
    return jax.shard_map(
        per_device, mesh=mesh, in_specs=in_specs, out_specs=out_specs, check_vma=False
    )
```

```python
from functools import partial

import jax
import jax.numpy as jnp
from jax import lax
from jax.experimental import pallas as pl
from jax.experimental.pallas import tpu as pltpu
from jax.sharding import PartitionSpec as P

VMEM_LIMIT = 32 * 1024 * 1024
F32 = jnp.float32
BF16 = jnp.bfloat16
GROUP = 4


def dot(a, b):
    return jnp.dot(a, b, preferred_element_type=F32)


def dot_t(a, b):
    return lax.dot_general(a, b, (((1,), (1,)), ((), ())), preferred_element_type=F32)


def call(kernel, name, flops, inputs, scalars, outputs, scratch=(), inputs_in=pltpu.VMEM):
    shapes = [jax.ShapeDtypeStruct(shape, dtype) for shape, dtype in outputs]
    moved = sum(a.size * a.dtype.itemsize for a in inputs) + sum(
        s.size * s.dtype.itemsize for s in shapes
    )
    return pl.pallas_call(
        kernel,
        out_shape=shapes,
        in_specs=[pl.BlockSpec(memory_space=inputs_in)] * len(inputs)
        + [pl.BlockSpec(memory_space=pltpu.SMEM)] * len(scalars),
        out_specs=[pl.BlockSpec(memory_space=pltpu.VMEM)] * len(outputs),
        scratch_shapes=list(scratch),
        compiler_params=pltpu.CompilerParams(vmem_limit_bytes=VMEM_LIMIT),
        cost_estimate=pl.CostEstimate(flops=0, bytes_accessed=0, transcendentals=0),
        name=name,
    )(*(pltpu.with_memory_space_constraint(a, inputs_in) for a in inputs), *scalars)


def up_kernel(
    bits, x_hbm, basis_hbm, transfer_hbm, coupling_hbm,
    keep_ref, send_ref, w_ref, x_ref, transfer_ref, coupling_ref, basis_ref, z_ref, sems
):
    pos = lax.axis_index("level")
    core = pos & 1
    pairs = (
        (basis_hbm.at[0], basis_ref), (transfer_hbm, transfer_ref), (x_hbm, x_ref),
        (coupling_hbm.at[:2], coupling_ref),
    )
    copies = [pltpu.make_async_copy(a, b, sems.at[i]) for i, (a, b) in enumerate(pairs)]
    for copy in copies:
        copy.start()
    copies[0].wait()
    copies[1].wait()
    w = basis_ref[...]
    for bit in range(bits):
        w = dot(w, transfer_ref[pos >> bit & 1]).astype(BF16)
    w_ref[...] = w
    copies[2].wait()
    z = dot(x_ref[...], w).astype(BF16)
    rows = z_ref.shape[1]
    z_ref[0] = z[:rows]
    z_ref[1] = z[rows:]
    keep_ref[...] = z_ref[core]
    send_ref[...] = z_ref[1 - core]
    copies[3].wait()


def push_kernel(
    turns, pairs, clusters, own_ref, mate_ref, coupling_ref, transfer_ref, mask_ref, *refs
):
    *push_refs, pair_ref, both_ref = refs
    leaf_pos = lax.axis_index("leaf")
    pair, side = leaf_pos >> 1, leaf_pos & 1
    both_ref[side] = own_ref[...]
    both_ref[1 - side] = mate_ref[...]
    total = dot(both_ref[0], transfer_ref[0]) + dot(both_ref[1], transfer_ref[1])
    pair_ref[...] = total.astype(BF16)

    def term(lev, coef, gap, source, target):
        pick = abs(gap) - 2
        matrix = coupling_ref[lev, pick]
        switch = mask_ref[lev, pick, source if gap > 0 else target].astype(F32)
        return switch * (dot_t(coef, matrix) if gap > 0 else dot(coef, matrix))

    def fill(push_ref, distance, to_side):
        target_pair = pair + distance
        total = None
        if abs(distance) in (2, 3) and clusters[1]:
            coupled = term(1, pair_ref[...], distance, pair, target_pair).astype(BF16)
            total = dot_t(coupled, transfer_ref[to_side])
        for from_side in (0, 1):
            gap = 2 * distance + to_side - from_side
            if abs(gap) in (2, 3) and clusters[0]:
                more = term(
                    0, both_ref[from_side], gap, 2 * pair + from_side, 2 * target_pair + to_side
                )
                total = more if total is None else total + more
        if total is None:
            total = jnp.zeros(push_ref.shape, F32)
        push_ref[...] = total.astype(BF16)

    for turn, push_ref in zip(turns, push_refs):
        for distance in reached(turn, pairs):
            if pairs == 4:
                inside = (pair ^ turn) == pair + distance
            else:
                inside = jnp.logical_and(pair + distance >= 0, pair + distance < pairs)
            for to_side in (0, 1):
                @pl.when(jnp.logical_and(inside, side == to_side))
                def _(push_ref=push_ref, distance=distance, to_side=to_side):
                    fill(push_ref, distance, to_side)


def reached(turn, pairs):
    return sorted({(i ^ turn) - i for i in range(pairs)}) if pairs == 4 else [turn]


def pick_kernel(x_ref, mate_ref, across_ref, corner_ref, even_cols, odd_cols, to_even, to_odd):
    pos = lax.axis_index("level")
    for cols, out in ((even_cols, to_even), (odd_cols, to_odd)):
        turn = lax.rem(cols[0, 3], GROUP) ^ pos
        for at, block in enumerate((x_ref, mate_ref, across_ref, corner_ref)):
            @pl.when(turn == at)
            def _(block=block, out=out):
                out[...] = block[...]


def near_kernel(
    x_ref, mate_ref, across_ref, corner_ref, edge_ref, tiles_ref, cols_ref, count_ref, acc_ref
):
    pos = lax.axis_index("level")
    odd = pos & 1
    inner = jnp.logical_or(pos == 1, pos == 2)
    acc = dot(x_ref[...], tiles_ref[0, 0]) + dot(mate_ref[...], tiles_ref[0, 2 - odd])
    beside = jnp.where(inner, corner_ref[...], edge_ref[...])
    acc_ref[...] = acc + dot(beside, tiles_ref[0, 1 + odd])
    col = cols_ref[0, 3]
    turn = lax.rem(col, GROUP) ^ pos
    here = jnp.logical_and(count_ref[0] > 3, col // GROUP == 1)
    for at, block in enumerate((x_ref, mate_ref, across_ref, corner_ref)):
        @pl.when(jnp.logical_and(here, turn == at))
        def _(block=block):
            acc_ref[...] += dot(block[...], tiles_ref[0, 3])


def finish_kernel(
    acc_ref, even_ref, odd_ref, tiles_ref, w_ref, own_field, mate_field,
    cols_ref, count_ref, out_ref, total_ref, field_ref
):
    core = lax.axis_index("level") & 1
    side = lax.axis_index("leaf") & 1
    field_ref[core] = own_field[...]
    field_ref[1 - core] = mate_field[...]
    field = jnp.concatenate([field_ref[0], field_ref[1]], axis=0)
    total_ref[...] = acc_ref[...] + dot_t(field, w_ref[...])
    group = cols_ref[0, 3] // GROUP
    live = jnp.logical_and(count_ref[0] > 3, group != 1)
    from_even = (group == 0) == (side == 1)

    @pl.when(jnp.logical_and(live, from_even))
    def _():
        total_ref[...] += dot(even_ref[...], tiles_ref[0, 3])

    @pl.when(jnp.logical_and(live, jnp.logical_not(from_even)))
    def _():
        total_ref[...] += dot(odd_ref[...], tiles_ref[0, 3])

    out_ref[...] = total_ref[...].astype(BF16)


def turned(value, turn):
    return lax.ppermute(value, "level", [(i, i ^ turn) for i in range(GROUP)])


def shifted(value, steps):
    count = lax.axis_size("leaf")
    route = [(i, i + steps) for i in range(count) if 0 <= i + steps < count]
    return lax.ppermute(value, "leaf", route)


def swapped(value, distance):
    count = lax.axis_size("leaf")
    return lax.ppermute(value, "leaf", [(i, i ^ 1 << distance) for i in range(count)])


def neighbours(value, odd):
    count = lax.axis_size("leaf")
    route = [(i, i + 1) for i in range(odd, count - 1, 2)]
    return lax.ppermute(value, "leaf", route + [(b, a) for a, b in route])


def upper_field(coef, coupling, transfer, couple_mask):
    leaf_count = lax.axis_size("leaf")
    leaf_pos = lax.axis_index("leaf")
    couplings = []
    levels = range(2, min(coupling.shape[0], leaf_count.bit_length()))
    for lev in levels:
        other = swapped(coef, lev - 1)
        is_upper = (leaf_pos >> lev - 1 & 1) == 1
        total = dot(jnp.where(is_upper, other, coef), transfer[0])
        total = total + dot(jnp.where(is_upper, coef, other), transfer[1])
        coef = total.astype(BF16)
        cluster = leaf_pos >> lev
        coupled = jnp.zeros(coef.shape, F32)
        for pick, offset in enumerate((2, 3)):
            if offset < leaf_count >> lev:
                matrix = coupling[lev, pick]
                ahead = shifted(coef, -(offset << lev))
                behind = shifted(coef, offset << lev)
                ahead_mask = couple_mask[lev, cluster, pick].astype(F32)
                behind_mask = couple_mask[lev, jnp.maximum(cluster - offset, 0), pick].astype(F32)
                coupled = coupled + ahead_mask * dot(ahead, matrix)
                coupled = coupled + behind_mask * dot_t(behind, matrix)
        couplings.append(coupled)
    field = jnp.zeros(coef.shape, F32)
    for lev, coupled in zip(reversed(levels), reversed(couplings)):
        if lev + 1 in levels:
            field = dot_t(field.astype(BF16), transfer[leaf_pos >> lev & 1])
        field = field + coupled
    for lev in (1, 0):
        field = dot_t(field.astype(BF16), transfer[leaf_pos >> lev & 1])
    return field


def per_device(
    points_x, leaf_basis, near_tiles, near_cols, near_count, transfer, coupling, couple_mask
):
    assert lax.axis_size("level") == GROUP
    leaf_count = lax.axis_size("leaf")
    vectors, points = points_x.shape
    rank = leaf_basis.shape[2]
    rows = vectors // 2
    bits = GROUP.bit_length() - 1
    block = ((vectors, points), BF16)
    half = ((rows, rank), BF16)
    cube = 2 * rank * rank

    across = turned(points_x, 2)
    mate = turned(points_x, 1)
    joints = [(GROUP * g - 1, GROUP * g) for g in range(1, leaf_count)]
    edge = lax.ppermute(points_x, ("leaf", "level"), joints + [(b, a) for a, b in joints])
    even_cols = neighbours(near_cols, 0)
    odd_cols = neighbours(near_cols, 1)
    corner = turned(across, 1)

    keep, send, w, own_x, transfer_in, coupling_in = call(
        partial(up_kernel, bits), "up", cube * (vectors + bits * points) * 2,
        [points_x, leaf_basis, transfer, coupling], [],
        [half, half, ((points, rank), BF16), block, (transfer.shape, BF16),
         ((2,) + coupling.shape[1:], BF16)],
        [pltpu.VMEM((points, rank), BF16), pltpu.VMEM((2, rows, rank), BF16),
         pltpu.SemaphoreType.DMA((4,))],
        pltpu.HBM,
    )
    coef = (keep.astype(F32) + turned(send, 1).astype(F32)).astype(BF16)
    coef = (coef.astype(F32) + turned(coef, 2).astype(F32)).astype(BF16)
    edge, corner = lax.optimization_barrier((edge, corner))
    to_even, to_odd = call(
        pick_kernel, "pick", 0, [own_x, mate, across, corner], [even_cols, odd_cols], [block] * 2
    )
    coef, to_even, to_odd = lax.optimization_barrier((coef, to_even, to_odd))
    beside = swapped(coef, 0)
    from_even = neighbours(to_even, 0)
    from_odd = neighbours(to_odd, 1)

    (acc,) = call(
        near_kernel, "near", 8 * vectors * points * points,
        [own_x, mate, across, corner, edge, near_tiles], [near_cols, near_count],
        [((vectors, points), F32)],
    )
    beside, acc = lax.optimization_barrier((beside, acc))
    active = min(coupling.shape[0], leaf_count.bit_length())
    pairs = leaf_count // 2
    turns = [1, 2, 3] if pairs == 4 else [1, 2, 3, -1, -2, -3]
    clusters = [lev < active and (leaf_count >> lev) > 2 for lev in (0, 1)]
    *pushes, pair_coef = call(
        partial(push_kernel, turns, pairs, clusters), "push", cube * rows * 10,
        [coef, beside, coupling_in, transfer_in], [couple_mask.transpose(0, 2, 1)],
        [half] * (len(turns) + 1), [pltpu.VMEM((2, rows, rank), BF16)],
    )
    field = None
    for turn, push in zip(turns, pushes):
        if pairs == 4:
            came = lax.ppermute(push, "leaf", [(i, i ^ 2 * turn) for i in range(leaf_count)])
        else:
            came = shifted(push, 2 * turn)
        field = came.astype(F32) if field is None else field + came.astype(F32)
    if active > 2 and (leaf_count >> 2) > 2:
        field = field + upper_field(pair_coef, coupling, transfer, couple_mask)
    field = field.astype(BF16)
    mate_field = turned(field, 1)

    (out,) = call(
        finish_kernel, "finish", 4 * vectors * points * points,
        [acc, from_even, from_odd, near_tiles, w, field, mate_field], [near_cols, near_count],
        [block], [pltpu.VMEM((vectors, points), F32), pltpu.VMEM((2, rows, rank), BF16)],
    )
    return out


def solution(mesh):
    in_specs = (
        P(None, ("leaf", "level")),
        P(("leaf", "level"), None, None),
        P(("leaf", "level"), None, None, None),
        P(("leaf", "level"), None),
        P(("leaf", "level")),
        P(),
        P(),
        P(),
    )
    out_specs = P(None, ("leaf", "level"))
    return jax.shard_map(
        per_device, mesh=mesh, in_specs=in_specs, out_specs=out_specs, check_vma=False
    )
```

```python
from functools import partial

import jax
import jax.numpy as jnp
from jax import lax
from jax.experimental import pallas as pl
from jax.experimental.pallas import tpu as pltpu
from jax.sharding import PartitionSpec as P

VMEM_LIMIT = 32 * 1024 * 1024
F32 = jnp.float32
BF16 = jnp.bfloat16
GROUP = 4


def dot(a, b):
    return jnp.dot(a, b, preferred_element_type=F32)


def dot_t(a, b):
    return lax.dot_general(a, b, (((1,), (1,)), ((), ())), preferred_element_type=F32)


def call(kernel, name, flops, inputs, scalars, outputs, scratch=(), inputs_in=pltpu.VMEM):
    shapes = [jax.ShapeDtypeStruct(shape, dtype) for shape, dtype in outputs]
    moved = sum(a.size * a.dtype.itemsize for a in inputs) + sum(
        s.size * s.dtype.itemsize for s in shapes
    )
    return pl.pallas_call(
        kernel,
        out_shape=shapes,
        in_specs=[pl.BlockSpec(memory_space=inputs_in)] * len(inputs)
        + [pl.BlockSpec(memory_space=pltpu.SMEM)] * len(scalars),
        out_specs=[pl.BlockSpec(memory_space=pltpu.VMEM)] * len(outputs),
        scratch_shapes=list(scratch),
        compiler_params=pltpu.CompilerParams(vmem_limit_bytes=VMEM_LIMIT),
        cost_estimate=pl.CostEstimate(flops=0, bytes_accessed=0, transcendentals=0),
        name=name,
    )(*(pltpu.with_memory_space_constraint(a, inputs_in) for a in inputs), *scalars)


def up_kernel(
    bits, x_hbm, basis_hbm, transfer_hbm, coupling_hbm,
    keep_ref, send_ref, w_ref, x_ref, transfer_ref, coupling_ref, basis_ref, z_ref, sems
):
    pos = lax.axis_index("level")
    core = pos & 1
    pairs = (
        (basis_hbm.at[0], basis_ref), (transfer_hbm, transfer_ref), (x_hbm, x_ref),
        (coupling_hbm.at[:2], coupling_ref),
    )
    copies = [pltpu.make_async_copy(a, b, sems.at[i]) for i, (a, b) in enumerate(pairs)]
    for copy in copies:
        copy.start()
    copies[0].wait()
    copies[1].wait()
    w = basis_ref[...]
    for bit in range(bits):
        w = dot(w, transfer_ref[pos >> bit & 1]).astype(BF16)
    w_ref[...] = w
    copies[2].wait()
    z = dot(x_ref[...], w).astype(BF16)
    rows = z_ref.shape[1]
    z_ref[0] = z[:rows]
    z_ref[1] = z[rows:]
    keep_ref[...] = z_ref[core]
    send_ref[...] = z_ref[1 - core]
    copies[3].wait()


def push_kernel(
    turns, pairs, clusters, own_ref, mate_ref, coupling_ref, transfer_ref, mask_ref, *refs
):
    *push_refs, pair_ref, both_ref = refs
    leaf_pos = lax.axis_index("leaf")
    pair, side = leaf_pos >> 1, leaf_pos & 1
    both_ref[side] = own_ref[...]
    both_ref[1 - side] = mate_ref[...]
    total = dot(both_ref[0], transfer_ref[0]) + dot(both_ref[1], transfer_ref[1])
    pair_ref[...] = total.astype(BF16)

    def term(lev, coef, gap, source, target):
        pick = abs(gap) - 2
        matrix = coupling_ref[lev, pick]
        switch = mask_ref[lev, pick, source if gap > 0 else target].astype(F32)
        return switch * (dot_t(coef, matrix) if gap > 0 else dot(coef, matrix))

    def fill(push_ref, distance, to_side):
        target_pair = pair + distance
        total = None
        if abs(distance) in (2, 3) and clusters[1]:
            coupled = term(1, pair_ref[...], distance, pair, target_pair).astype(BF16)
            total = dot_t(coupled, transfer_ref[to_side])
        for from_side in (0, 1):
            gap = 2 * distance + to_side - from_side
            if abs(gap) in (2, 3) and clusters[0]:
                more = term(
                    0, both_ref[from_side], gap, 2 * pair + from_side, 2 * target_pair + to_side
                )
                total = more if total is None else total + more
        if total is None:
            total = jnp.zeros(push_ref.shape, F32)
        push_ref[...] = total.astype(BF16)

    for turn, push_ref in zip(turns, push_refs):
        for distance in reached(turn, pairs):
            if pairs == 4:
                inside = (pair ^ turn) == pair + distance
            else:
                inside = jnp.logical_and(pair + distance >= 0, pair + distance < pairs)
            for to_side in (0, 1):
                @pl.when(jnp.logical_and(inside, side == to_side))
                def _(push_ref=push_ref, distance=distance, to_side=to_side):
                    fill(push_ref, distance, to_side)


def reached(turn, pairs):
    return sorted({(i ^ turn) - i for i in range(pairs)}) if pairs == 4 else [turn]


def pick_kernel(x_ref, mate_ref, across_ref, corner_ref, even_cols, odd_cols, to_even, to_odd):
    pos = lax.axis_index("level")
    for cols, out in ((even_cols, to_even), (odd_cols, to_odd)):
        turn = lax.rem(cols[0, 3], GROUP) ^ pos
        for at, block in enumerate((x_ref, mate_ref, across_ref, corner_ref)):
            @pl.when(turn == at)
            def _(block=block, out=out):
                out[...] = block[...]


def near_kernel(
    x_ref, mate_ref, across_ref, corner_ref, edge_ref, tiles_ref, cols_ref, count_ref, acc_ref
):
    pos = lax.axis_index("level")
    odd = pos & 1
    inner = jnp.logical_or(pos == 1, pos == 2)
    acc = dot(x_ref[...], tiles_ref[0, 0]) + dot(mate_ref[...], tiles_ref[0, 2 - odd])
    beside = jnp.where(inner, corner_ref[...], edge_ref[...])
    acc_ref[...] = acc + dot(beside, tiles_ref[0, 1 + odd])
    col = cols_ref[0, 3]
    turn = lax.rem(col, GROUP) ^ pos
    here = jnp.logical_and(count_ref[0] > 3, col // GROUP == 1)
    for at, block in enumerate((x_ref, mate_ref, across_ref, corner_ref)):
        @pl.when(jnp.logical_and(here, turn == at))
        def _(block=block):
            acc_ref[...] += dot(block[...], tiles_ref[0, 3])


def finish_kernel(
    acc_ref, even_ref, odd_ref, tiles_ref, w_ref, own_field, mate_field,
    cols_ref, count_ref, out_ref, total_ref, field_ref
):
    core = lax.axis_index("level") & 1
    side = lax.axis_index("leaf") & 1
    field_ref[core] = own_field[...]
    field_ref[1 - core] = mate_field[...]
    field = jnp.concatenate([field_ref[0], field_ref[1]], axis=0)
    total_ref[...] = acc_ref[...] + dot_t(field, w_ref[...])
    group = cols_ref[0, 3] // GROUP
    live = jnp.logical_and(count_ref[0] > 3, group != 1)
    from_even = (group == 0) == (side == 1)

    @pl.when(jnp.logical_and(live, from_even))
    def _():
        total_ref[...] += dot(even_ref[...], tiles_ref[0, 3])

    @pl.when(jnp.logical_and(live, jnp.logical_not(from_even)))
    def _():
        total_ref[...] += dot(odd_ref[...], tiles_ref[0, 3])

    out_ref[...] = total_ref[...].astype(BF16)


def turned(value, turn):
    return lax.ppermute(value, "level", [(i, i ^ turn) for i in range(GROUP)])


def shifted(value, steps):
    count = lax.axis_size("leaf")
    route = [(i, i + steps) for i in range(count) if 0 <= i + steps < count]
    return lax.ppermute(value, "leaf", route)


def swapped(value, distance):
    count = lax.axis_size("leaf")
    return lax.ppermute(value, "leaf", [(i, i ^ 1 << distance) for i in range(count)])


def neighbours(value, odd):
    count = lax.axis_size("leaf")
    route = [(i, i + 1) for i in range(odd, count - 1, 2)]
    return lax.ppermute(value, "leaf", route + [(b, a) for a, b in route])


def upper_field(coef, coupling, transfer, couple_mask):
    leaf_count = lax.axis_size("leaf")
    leaf_pos = lax.axis_index("leaf")
    couplings = []
    levels = range(2, min(coupling.shape[0], leaf_count.bit_length()))
    for lev in levels:
        other = swapped(coef, lev - 1)
        is_upper = (leaf_pos >> lev - 1 & 1) == 1
        total = dot(jnp.where(is_upper, other, coef), transfer[0])
        total = total + dot(jnp.where(is_upper, coef, other), transfer[1])
        coef = total.astype(BF16)
        cluster = leaf_pos >> lev
        coupled = jnp.zeros(coef.shape, F32)
        for pick, offset in enumerate((2, 3)):
            if offset < leaf_count >> lev:
                matrix = coupling[lev, pick]
                ahead = shifted(coef, -(offset << lev))
                behind = shifted(coef, offset << lev)
                ahead_mask = couple_mask[lev, cluster, pick].astype(F32)
                behind_mask = couple_mask[lev, jnp.maximum(cluster - offset, 0), pick].astype(F32)
                coupled = coupled + ahead_mask * dot(ahead, matrix)
                coupled = coupled + behind_mask * dot_t(behind, matrix)
        couplings.append(coupled)
    field = jnp.zeros(coef.shape, F32)
    for lev, coupled in zip(reversed(levels), reversed(couplings)):
        if lev + 1 in levels:
            field = dot_t(field.astype(BF16), transfer[leaf_pos >> lev & 1])
        field = field + coupled
    for lev in (1, 0):
        field = dot_t(field.astype(BF16), transfer[leaf_pos >> lev & 1])
    return field


def per_device(
    points_x, leaf_basis, near_tiles, near_cols, near_count, transfer, coupling, couple_mask
):
    assert lax.axis_size("level") == GROUP
    leaf_count = lax.axis_size("leaf")
    vectors, points = points_x.shape
    rank = leaf_basis.shape[2]
    rows = vectors // 2
    bits = GROUP.bit_length() - 1
    block = ((vectors, points), BF16)
    half = ((rows, rank), BF16)
    cube = 2 * rank * rank

    even_cols = neighbours(near_cols, 0)
    odd_cols = neighbours(near_cols, 1)
    across = turned(points_x, 2)
    mate = turned(points_x, 1)
    sent, across, even_cols, odd_cols = lax.optimization_barrier(
        (points_x, across, even_cols, odd_cols)
    )
    joints = [(GROUP * g - 1, GROUP * g) for g in range(1, leaf_count)]
    edge = lax.ppermute(sent, ("leaf", "level"), joints + [(b, a) for a, b in joints])
    corner = turned(across, 1)
    edge, corner = lax.optimization_barrier((edge, corner))

    keep, send, w, own_x, transfer_in, coupling_in = call(
        partial(up_kernel, bits), "up", cube * (vectors + bits * points) * 2,
        [points_x, leaf_basis, transfer, coupling], [],
        [half, half, ((points, rank), BF16), block, (transfer.shape, BF16),
         ((2,) + coupling.shape[1:], BF16)],
        [pltpu.VMEM((points, rank), BF16), pltpu.VMEM((2, rows, rank), BF16),
         pltpu.SemaphoreType.DMA((4,))],
        pltpu.HBM,
    )
    coef = (keep.astype(F32) + turned(send, 1).astype(F32)).astype(BF16)
    coef = (coef.astype(F32) + turned(coef, 2).astype(F32)).astype(BF16)
    beside = swapped(coef, 0)
    to_even, to_odd = call(
        pick_kernel, "pick", 0, [own_x, mate, across, corner], [even_cols, odd_cols], [block] * 2
    )
    from_even = neighbours(to_even, 0)
    from_odd = neighbours(to_odd, 1)

    (acc,) = call(
        near_kernel, "near", 8 * vectors * points * points,
        [own_x, mate, across, corner, edge, near_tiles], [near_cols, near_count],
        [((vectors, points), F32)],
    )
    active = min(coupling.shape[0], leaf_count.bit_length())
    pairs = leaf_count // 2
    turns = [1, 2, 3] if pairs == 4 else [1, 2, 3, -1, -2, -3]
    clusters = [lev < active and (leaf_count >> lev) > 2 for lev in (0, 1)]
    *pushes, pair_coef = call(
        partial(push_kernel, turns, pairs, clusters), "push", cube * rows * 10,
        [coef, beside, coupling_in, transfer_in], [couple_mask.transpose(0, 2, 1)],
        [half] * (len(turns) + 1), [pltpu.VMEM((2, rows, rank), BF16)],
    )
    field = None
    for turn, push in zip(turns, pushes):
        if pairs == 4:
            came = lax.ppermute(push, "leaf", [(i, i ^ 2 * turn) for i in range(leaf_count)])
        else:
            came = shifted(push, 2 * turn)
        field = came.astype(F32) if field is None else field + came.astype(F32)
    if active > 2 and (leaf_count >> 2) > 2:
        field = field + upper_field(pair_coef, coupling, transfer, couple_mask)
    field = field.astype(BF16)
    mate_field = turned(field, 1)

    (out,) = call(
        finish_kernel, "finish", 4 * vectors * points * points,
        [acc, from_even, from_odd, near_tiles, w, field, mate_field], [near_cols, near_count],
        [block], [pltpu.VMEM((vectors, points), F32), pltpu.VMEM((2, rows, rank), BF16)],
    )
    return out


def solution(mesh):
    in_specs = (
        P(None, ("leaf", "level")),
        P(("leaf", "level"), None, None),
        P(("leaf", "level"), None, None, None),
        P(("leaf", "level"), None),
        P(("leaf", "level")),
        P(),
        P(),
        P(),
    )
    out_specs = P(None, ("leaf", "level"))
    return jax.shard_map(
        per_device, mesh=mesh, in_specs=in_specs, out_specs=out_specs, check_vma=False
    )
```

```python
from functools import partial

import jax
import jax.numpy as jnp
from jax import lax
from jax.experimental import pallas as pl
from jax.experimental.pallas import tpu as pltpu
from jax.sharding import PartitionSpec as P

VMEM_LIMIT = 32 * 1024 * 1024
F32 = jnp.float32
BF16 = jnp.bfloat16
GROUP = 4


def dot(a, b):
    return jnp.dot(a, b, preferred_element_type=F32)


def dot_t(a, b):
    return lax.dot_general(a, b, (((1,), (1,)), ((), ())), preferred_element_type=F32)


def call(kernel, name, flops, inputs, scalars, outputs, scratch=(), inputs_in=pltpu.VMEM):
    shapes = [jax.ShapeDtypeStruct(shape, dtype) for shape, dtype in outputs]
    moved = sum(a.size * a.dtype.itemsize for a in inputs) + sum(
        s.size * s.dtype.itemsize for s in shapes
    )
    return pl.pallas_call(
        kernel,
        out_shape=shapes,
        in_specs=[pl.BlockSpec(memory_space=inputs_in)] * len(inputs)
        + [pl.BlockSpec(memory_space=pltpu.SMEM)] * len(scalars),
        out_specs=[pl.BlockSpec(memory_space=pltpu.VMEM)] * len(outputs),
        scratch_shapes=list(scratch),
        compiler_params=pltpu.CompilerParams(vmem_limit_bytes=VMEM_LIMIT),
        cost_estimate=pl.CostEstimate(flops=0, bytes_accessed=0, transcendentals=0),
        name=name,
    )(*(pltpu.with_memory_space_constraint(a, inputs_in) for a in inputs), *scalars)


def up_kernel(
    bits, x_hbm, basis_hbm, transfer_hbm, coupling_hbm,
    keep_ref, send_ref, w_ref, x_ref, transfer_ref, coupling_ref, basis_ref, z_ref, sems
):
    pos = lax.axis_index("level")
    core = pos & 1
    pairs = (
        (basis_hbm.at[0], basis_ref), (transfer_hbm, transfer_ref), (x_hbm, x_ref),
        (coupling_hbm.at[:2], coupling_ref),
    )
    copies = [pltpu.make_async_copy(a, b, sems.at[i]) for i, (a, b) in enumerate(pairs)]
    for copy in copies:
        copy.start()
    copies[0].wait()
    copies[1].wait()
    w = basis_ref[...]
    for bit in range(bits):
        w = dot(w, transfer_ref[pos >> bit & 1]).astype(BF16)
    w_ref[...] = w
    copies[2].wait()
    z = dot(x_ref[...], w).astype(BF16)
    rows = z_ref.shape[1]
    z_ref[0] = z[:rows]
    z_ref[1] = z[rows:]
    keep_ref[...] = z_ref[core]
    send_ref[...] = z_ref[1 - core]
    copies[3].wait()


def push_kernel(
    turns, pairs, clusters, own_ref, mate_ref, coupling_ref, transfer_ref, mask_ref, *refs
):
    *push_refs, pair_ref, both_ref = refs
    leaf_pos = lax.axis_index("leaf")
    pair, side = leaf_pos >> 1, leaf_pos & 1
    both_ref[side] = own_ref[...]
    both_ref[1 - side] = mate_ref[...]
    total = dot(both_ref[0], transfer_ref[0]) + dot(both_ref[1], transfer_ref[1])
    pair_ref[...] = total.astype(BF16)

    def term(lev, coef, gap, source, target):
        pick = abs(gap) - 2
        matrix = coupling_ref[lev, pick]
        switch = mask_ref[lev, pick, source if gap > 0 else target].astype(F32)
        return switch * (dot_t(coef, matrix) if gap > 0 else dot(coef, matrix))

    def fill(push_ref, distance, to_side):
        target_pair = pair + distance
        total = None
        if abs(distance) in (2, 3) and clusters[1]:
            coupled = term(1, pair_ref[...], distance, pair, target_pair).astype(BF16)
            total = dot_t(coupled, transfer_ref[to_side])
        for from_side in (0, 1):
            gap = 2 * distance + to_side - from_side
            if abs(gap) in (2, 3) and clusters[0]:
                more = term(
                    0, both_ref[from_side], gap, 2 * pair + from_side, 2 * target_pair + to_side
                )
                total = more if total is None else total + more
        if total is None:
            total = jnp.zeros(push_ref.shape, F32)
        push_ref[...] = total.astype(BF16)

    for turn, push_ref in zip(turns, push_refs):
        for distance in reached(turn, pairs):
            if pairs == 4:
                inside = (pair ^ turn) == pair + distance
            else:
                inside = jnp.logical_and(pair + distance >= 0, pair + distance < pairs)
            for to_side in (0, 1):
                @pl.when(jnp.logical_and(inside, side == to_side))
                def _(push_ref=push_ref, distance=distance, to_side=to_side):
                    fill(push_ref, distance, to_side)


def reached(turn, pairs):
    return sorted({(i ^ turn) - i for i in range(pairs)}) if pairs == 4 else [turn]


def pick_kernel(x_ref, mate_ref, across_ref, corner_ref, even_cols, odd_cols, to_even, to_odd):
    pos = lax.axis_index("level")
    for cols, out in ((even_cols, to_even), (odd_cols, to_odd)):
        turn = lax.rem(cols[0, 3], GROUP) ^ pos
        for at, block in enumerate((x_ref, mate_ref, across_ref, corner_ref)):
            @pl.when(turn == at)
            def _(block=block, out=out):
                out[...] = block[...]


def near_kernel(
    x_ref, mate_ref, across_ref, corner_ref, edge_ref, tiles_ref, cols_ref, count_ref, acc_ref
):
    pos = lax.axis_index("level")
    odd = pos & 1
    inner = jnp.logical_or(pos == 1, pos == 2)
    acc = dot(x_ref[...], tiles_ref[0, 0]) + dot(mate_ref[...], tiles_ref[0, 2 - odd])
    beside = jnp.where(inner, corner_ref[...], edge_ref[...])
    acc_ref[...] = acc + dot(beside, tiles_ref[0, 1 + odd])
    col = cols_ref[0, 3]
    turn = lax.rem(col, GROUP) ^ pos
    here = jnp.logical_and(count_ref[0] > 3, col // GROUP == 1)
    for at, block in enumerate((x_ref, mate_ref, across_ref, corner_ref)):
        @pl.when(jnp.logical_and(here, turn == at))
        def _(block=block):
            acc_ref[...] += dot(block[...], tiles_ref[0, 3])


def finish_kernel(
    acc_ref, even_ref, odd_ref, tiles_ref, w_ref, own_field, mate_field,
    cols_ref, count_ref, out_ref, total_ref, field_ref
):
    core = lax.axis_index("level") & 1
    side = lax.axis_index("leaf") & 1
    field_ref[core] = own_field[...]
    field_ref[1 - core] = mate_field[...]
    field = jnp.concatenate([field_ref[0], field_ref[1]], axis=0)
    total_ref[...] = acc_ref[...] + dot_t(field, w_ref[...])
    group = cols_ref[0, 3] // GROUP
    live = jnp.logical_and(count_ref[0] > 3, group != 1)
    from_even = (group == 0) == (side == 1)

    @pl.when(jnp.logical_and(live, from_even))
    def _():
        total_ref[...] += dot(even_ref[...], tiles_ref[0, 3])

    @pl.when(jnp.logical_and(live, jnp.logical_not(from_even)))
    def _():
        total_ref[...] += dot(odd_ref[...], tiles_ref[0, 3])

    out_ref[...] = total_ref[...].astype(BF16)


def turned(value, turn):
    return lax.ppermute(value, "level", [(i, i ^ turn) for i in range(GROUP)])


def shifted(value, steps):
    count = lax.axis_size("leaf")
    route = [(i, i + steps) for i in range(count) if 0 <= i + steps < count]
    return lax.ppermute(value, "leaf", route)


def swapped(value, distance):
    count = lax.axis_size("leaf")
    return lax.ppermute(value, "leaf", [(i, i ^ 1 << distance) for i in range(count)])


def neighbours(value, odd):
    count = lax.axis_size("leaf")
    route = [(i, i + 1) for i in range(odd, count - 1, 2)]
    return lax.ppermute(value, "leaf", route + [(b, a) for a, b in route])


def upper_field(coef, coupling, transfer, couple_mask):
    leaf_count = lax.axis_size("leaf")
    leaf_pos = lax.axis_index("leaf")
    couplings = []
    levels = range(2, min(coupling.shape[0], leaf_count.bit_length()))
    for lev in levels:
        other = swapped(coef, lev - 1)
        is_upper = (leaf_pos >> lev - 1 & 1) == 1
        total = dot(jnp.where(is_upper, other, coef), transfer[0])
        total = total + dot(jnp.where(is_upper, coef, other), transfer[1])
        coef = total.astype(BF16)
        cluster = leaf_pos >> lev
        coupled = jnp.zeros(coef.shape, F32)
        for pick, offset in enumerate((2, 3)):
            if offset < leaf_count >> lev:
                matrix = coupling[lev, pick]
                ahead = shifted(coef, -(offset << lev))
                behind = shifted(coef, offset << lev)
                ahead_mask = couple_mask[lev, cluster, pick].astype(F32)
                behind_mask = couple_mask[lev, jnp.maximum(cluster - offset, 0), pick].astype(F32)
                coupled = coupled + ahead_mask * dot(ahead, matrix)
                coupled = coupled + behind_mask * dot_t(behind, matrix)
        couplings.append(coupled)
    field = jnp.zeros(coef.shape, F32)
    for lev, coupled in zip(reversed(levels), reversed(couplings)):
        if lev + 1 in levels:
            field = dot_t(field.astype(BF16), transfer[leaf_pos >> lev & 1])
        field = field + coupled
    for lev in (1, 0):
        field = dot_t(field.astype(BF16), transfer[leaf_pos >> lev & 1])
    return field


def per_device(
    points_x, leaf_basis, near_tiles, near_cols, near_count, transfer, coupling, couple_mask
):
    assert lax.axis_size("level") == GROUP
    leaf_count = lax.axis_size("leaf")
    vectors, points = points_x.shape
    rank = leaf_basis.shape[2]
    rows = vectors // 2
    bits = GROUP.bit_length() - 1
    block = ((vectors, points), BF16)
    half = ((rows, rank), BF16)
    cube = 2 * rank * rank

    even_cols = neighbours(near_cols, 0)
    odd_cols = neighbours(near_cols, 1)
    across = turned(points_x, 2)
    mate = turned(points_x, 1)

    keep, send, w, own_x, transfer_in, coupling_in = call(
        partial(up_kernel, bits), "up", cube * (vectors + bits * points) * 2,
        [points_x, leaf_basis, transfer, coupling], [],
        [half, half, ((points, rank), BF16), block, (transfer.shape, BF16),
         ((2,) + coupling.shape[1:], BF16)],
        [pltpu.VMEM((points, rank), BF16), pltpu.VMEM((2, rows, rank), BF16),
         pltpu.SemaphoreType.DMA((4,))],
        pltpu.HBM,
    )
    coef = (keep.astype(F32) + turned(send, 1).astype(F32)).astype(BF16)
    coef = (coef.astype(F32) + turned(coef, 2).astype(F32)).astype(BF16)
    beside = swapped(coef, 0)

    sent, across, even_cols, odd_cols, beside = lax.optimization_barrier(
        (points_x, across, even_cols, odd_cols, beside)
    )
    joints = [(GROUP * g - 1, GROUP * g) for g in range(1, leaf_count)]
    edge = lax.ppermute(sent, ("leaf", "level"), joints + [(b, a) for a, b in joints])
    corner = turned(across, 1)
    edge, corner = lax.optimization_barrier((edge, corner))
    to_even, to_odd = call(
        pick_kernel, "pick", 0, [own_x, mate, across, corner], [even_cols, odd_cols], [block] * 2
    )
    from_even = neighbours(to_even, 0)
    from_odd = neighbours(to_odd, 1)

    (acc,) = call(
        near_kernel, "near", 8 * vectors * points * points,
        [own_x, mate, across, corner, edge, near_tiles], [near_cols, near_count],
        [((vectors, points), F32)],
    )
    active = min(coupling.shape[0], leaf_count.bit_length())
    pairs = leaf_count // 2
    turns = [1, 2, 3] if pairs == 4 else [1, 2, 3, -1, -2, -3]
    clusters = [lev < active and (leaf_count >> lev) > 2 for lev in (0, 1)]
    *pushes, pair_coef = call(
        partial(push_kernel, turns, pairs, clusters), "push", cube * rows * 10,
        [coef, beside, coupling_in, transfer_in], [couple_mask.transpose(0, 2, 1)],
        [half] * (len(turns) + 1), [pltpu.VMEM((2, rows, rank), BF16)],
    )
    field = None
    for turn, push in zip(turns, pushes):
        if pairs == 4:
            came = lax.ppermute(push, "leaf", [(i, i ^ 2 * turn) for i in range(leaf_count)])
        else:
            came = shifted(push, 2 * turn)
        field = came.astype(F32) if field is None else field + came.astype(F32)
    if active > 2 and (leaf_count >> 2) > 2:
        field = field + upper_field(pair_coef, coupling, transfer, couple_mask)
    field = field.astype(BF16)
    mate_field = turned(field, 1)

    (out,) = call(
        finish_kernel, "finish", 4 * vectors * points * points,
        [acc, from_even, from_odd, near_tiles, w, field, mate_field], [near_cols, near_count],
        [block], [pltpu.VMEM((vectors, points), F32), pltpu.VMEM((2, rows, rank), BF16)],
    )
    return out


def solution(mesh):
    in_specs = (
        P(None, ("leaf", "level")),
        P(("leaf", "level"), None, None),
        P(("leaf", "level"), None, None, None),
        P(("leaf", "level"), None),
        P(("leaf", "level")),
        P(),
        P(),
        P(),
    )
    out_specs = P(None, ("leaf", "level"))
    return jax.shard_map(
        per_device, mesh=mesh, in_specs=in_specs, out_specs=out_specs, check_vma=False
    )
```

```python
from functools import partial

import jax
import jax.numpy as jnp
from jax import lax
from jax.experimental import pallas as pl
from jax.experimental.pallas import tpu as pltpu
from jax.sharding import PartitionSpec as P

VMEM_LIMIT = 32 * 1024 * 1024
F32 = jnp.float32
BF16 = jnp.bfloat16
GROUP = 4
SLOT = 3
TAIL = 16


def dot(a, b):
    return jnp.dot(a, b, preferred_element_type=F32)


def dot_t(a, b):
    return lax.dot_general(a, b, (((1,), (1,)), ((), ())), preferred_element_type=F32)


def call(kernel, name, inputs, scalars, outputs, scratch=(), inputs_in=pltpu.VMEM):
    shapes = [jax.ShapeDtypeStruct(shape, dtype) for shape, dtype in outputs]
    return pl.pallas_call(
        kernel,
        out_shape=shapes,
        in_specs=[pl.BlockSpec(memory_space=inputs_in)] * len(inputs)
        + [pl.BlockSpec(memory_space=pltpu.SMEM)] * len(scalars),
        out_specs=[pl.BlockSpec(memory_space=pltpu.VMEM)] * len(outputs),
        scratch_shapes=list(scratch),
        compiler_params=pltpu.CompilerParams(vmem_limit_bytes=VMEM_LIMIT),
        cost_estimate=pl.CostEstimate(flops=0, bytes_accessed=0, transcendentals=0),
        name=name,
    )(*(pltpu.with_memory_space_constraint(a, inputs_in) for a in inputs), *scalars)


def up_kernel(
    bits, x_hbm, basis_hbm, transfer_hbm, coupling_hbm, cols_hbm,
    keep_ref, send_ref, w_ref, x_ref, transfer_ref, coupling_ref, basis_ref, z_ref, cols_ref, sems
):
    pos = lax.axis_index("level")
    core = pos & 1
    pairs = (
        (basis_hbm.at[0], basis_ref), (transfer_hbm, transfer_ref), (x_hbm, x_ref),
        (coupling_hbm.at[:2], coupling_ref), (cols_hbm, cols_ref),
    )
    copies = [pltpu.make_async_copy(a, b, sems.at[i]) for i, (a, b) in enumerate(pairs)]
    for copy in copies:
        copy.start()
    copies[0].wait()
    copies[1].wait()
    w = basis_ref[...]
    for bit in range(bits):
        w = dot(w, transfer_ref[pos >> bit & 1]).astype(BF16)
    w_ref[...] = w
    copies[2].wait()
    z = dot(x_ref[...], w).astype(BF16)
    rows = z_ref.shape[1]
    z_ref[0] = z[:rows]
    z_ref[1] = z[rows:]
    keep_ref[:rows] = z_ref[core]
    send_ref[:rows] = z_ref[1 - core]
    copies[4].wait()
    tail = keep_ref.shape[0] - rows
    named = cols_ref[0, SLOT].astype(F32)
    keep_ref[rows:] = jnp.full((tail, z.shape[1]), named, F32).astype(BF16)
    send_ref[rows:] = jnp.zeros((tail, z.shape[1]), BF16)
    copies[3].wait()


def push_kernel(
    turns, pairs, clusters, own_ref, mate_ref, coupling_ref, transfer_ref, mask_ref, *refs
):
    *push_refs, pair_ref, both_ref = refs
    leaf_pos = lax.axis_index("leaf")
    pair, side = leaf_pos >> 1, leaf_pos & 1
    both_ref[side] = own_ref[...]
    both_ref[1 - side] = mate_ref[...]
    total = dot(both_ref[0], transfer_ref[0]) + dot(both_ref[1], transfer_ref[1])
    pair_ref[...] = total.astype(BF16)

    def term(lev, coef, gap, source, target):
        pick = abs(gap) - 2
        matrix = coupling_ref[lev, pick]
        switch = mask_ref[lev, pick, source if gap > 0 else target].astype(F32)
        return switch * (dot_t(coef, matrix) if gap > 0 else dot(coef, matrix))

    def fill(push_ref, distance, to_side):
        target_pair = pair + distance
        total = None
        if abs(distance) in (2, 3) and clusters[1]:
            coupled = term(1, pair_ref[...], distance, pair, target_pair).astype(BF16)
            total = dot_t(coupled, transfer_ref[to_side])
        for from_side in (0, 1):
            gap = 2 * distance + to_side - from_side
            if abs(gap) in (2, 3) and clusters[0]:
                more = term(
                    0, both_ref[from_side], gap, 2 * pair + from_side, 2 * target_pair + to_side
                )
                total = more if total is None else total + more
        if total is None:
            total = jnp.zeros(push_ref.shape, F32)
        push_ref[...] = total.astype(BF16)

    for turn, push_ref in zip(turns, push_refs):
        for distance in reached(turn, pairs):
            if pairs == 4:
                inside = (pair ^ turn) == pair + distance
            else:
                inside = jnp.logical_and(pair + distance >= 0, pair + distance < pairs)
            for to_side in (0, 1):
                @pl.when(jnp.logical_and(inside, side == to_side))
                def _(push_ref=push_ref, distance=distance, to_side=to_side):
                    fill(push_ref, distance, to_side)


def reached(turn, pairs):
    return sorted({(i ^ turn) - i for i in range(pairs)}) if pairs == 4 else [turn]


def by_group(side, group, own, even, odd):
    from_even = (group == 0) == (side == 1)
    beyond = group != 1
    return (
        (group == 1, own),
        (jnp.logical_and(beyond, from_even), even),
        (jnp.logical_and(beyond, jnp.logical_not(from_even)), odd),
    )


def pick_kernel(
    rows, named_ref, x_ref, even_ref, odd_ref, mate_ref, mate_even, mate_odd, out_ref
):
    pos = lax.axis_index("level")
    side = lax.axis_index("leaf") & 1
    col = jnp.max(named_ref[rows:].astype(F32)).astype(jnp.int32)
    group, mine = col // GROUP, lax.rem(col, GROUP) == pos
    own_blocks = by_group(side, group, x_ref, even_ref, odd_ref)
    mate_blocks = by_group(side, group, mate_ref, mate_even, mate_odd)
    for (here, own), (_, mate) in zip(own_blocks, mate_blocks):
        @pl.when(jnp.logical_and(here, mine))
        def _(own=own):
            out_ref[...] = own[...]

        @pl.when(jnp.logical_and(here, jnp.logical_not(mine)))
        def _(mate=mate):
            out_ref[...] = mate[...]


def near_kernel(
    x_ref, even_ref, odd_ref, mate_ref, mate_even, mate_odd, beside_ref, tiles_ref,
    cols_ref, count_ref, acc_ref
):
    pos = lax.axis_index("level")
    side = lax.axis_index("leaf") & 1
    upper = pos & 1
    acc = dot(x_ref[...], tiles_ref[0, 0]) + dot(mate_ref[...], tiles_ref[0, 2 - upper])
    acc_ref[...] = acc + dot(beside_ref[...], tiles_ref[0, 1 + upper])
    group, place = cols_ref[0, SLOT] // GROUP, lax.rem(cols_ref[0, SLOT], GROUP)
    live = count_ref[0] > SLOT
    for at, blocks in (
        (pos, by_group(side, group, x_ref, even_ref, odd_ref)),
        (pos ^ 1, by_group(side, group, mate_ref, mate_even, mate_odd)),
    ):
        for here, block in blocks:
            @pl.when(jnp.logical_and(jnp.logical_and(live, place == at), here))
            def _(block=block):
                acc_ref[...] += dot(block[...], tiles_ref[0, SLOT])


def finish_kernel(
    acc_ref, picked_ref, tiles_ref, w_ref, own_field, mate_field,
    cols_ref, count_ref, out_ref, total_ref, field_ref
):
    pos = lax.axis_index("level")
    core = pos & 1
    field_ref[core] = own_field[...]
    field_ref[1 - core] = mate_field[...]
    field = jnp.concatenate([field_ref[0], field_ref[1]], axis=0)
    total_ref[...] = acc_ref[...] + dot_t(field, w_ref[...])
    place = lax.rem(cols_ref[0, SLOT], GROUP)

    @pl.when(jnp.logical_and(count_ref[0] > SLOT, (place >> 1) != (pos >> 1)))
    def _():
        total_ref[...] += dot(picked_ref[...], tiles_ref[0, SLOT])

    out_ref[...] = total_ref[...].astype(BF16)


def turned(value, turn):
    return lax.ppermute(value, "level", [(i, i ^ turn) for i in range(GROUP)])


def shifted(value, steps):
    count = lax.axis_size("leaf")
    route = [(i, i + steps) for i in range(count) if 0 <= i + steps < count]
    return lax.ppermute(value, "leaf", route)


def swapped(value, distance):
    count = lax.axis_size("leaf")
    return lax.ppermute(value, "leaf", [(i, i ^ 1 << distance) for i in range(count)])


def neighbours(value, odd):
    count = lax.axis_size("leaf")
    route = [(i, i + 1) for i in range(odd, count - 1, 2)]
    return lax.ppermute(value, "leaf", route + [(b, a) for a, b in route])


def upper_field(coef, coupling, transfer, couple_mask):
    leaf_count = lax.axis_size("leaf")
    leaf_pos = lax.axis_index("leaf")
    couplings = []
    levels = range(2, min(coupling.shape[0], leaf_count.bit_length()))
    for lev in levels:
        other = swapped(coef, lev - 1)
        is_upper = (leaf_pos >> lev - 1 & 1) == 1
        total = dot(jnp.where(is_upper, other, coef), transfer[0])
        total = total + dot(jnp.where(is_upper, coef, other), transfer[1])
        coef = total.astype(BF16)
        cluster = leaf_pos >> lev
        coupled = jnp.zeros(coef.shape, F32)
        for pick, offset in enumerate((2, 3)):
            if offset < leaf_count >> lev:
                matrix = coupling[lev, pick]
                ahead = shifted(coef, -(offset << lev))
                behind = shifted(coef, offset << lev)
                ahead_mask = couple_mask[lev, cluster, pick].astype(F32)
                behind_mask = couple_mask[lev, jnp.maximum(cluster - offset, 0), pick].astype(F32)
                coupled = coupled + ahead_mask * dot(ahead, matrix)
                coupled = coupled + behind_mask * dot_t(behind, matrix)
        couplings.append(coupled)
    field = jnp.zeros(coef.shape, F32)
    for lev, coupled in zip(reversed(levels), reversed(couplings)):
        if lev + 1 in levels:
            field = dot_t(field.astype(BF16), transfer[leaf_pos >> lev & 1])
        field = field + coupled
    for lev in (1, 0):
        field = dot_t(field.astype(BF16), transfer[leaf_pos >> lev & 1])
    return field


def per_device(
    points_x, leaf_basis, near_tiles, near_cols, near_count, transfer, coupling, couple_mask
):
    assert lax.axis_size("level") == GROUP
    leaf_count = lax.axis_size("leaf")
    vectors, points = points_x.shape
    rank = leaf_basis.shape[2]
    rows = vectors // 2
    bits = GROUP.bit_length() - 1
    block = ((vectors, points), BF16)
    half = ((rows, rank), BF16)

    tailed = ((rows + TAIL, rank), BF16)

    keep, send, w, own_x, transfer_in, coupling_in = call(
        partial(up_kernel, bits), "up",
        [points_x, leaf_basis, transfer, coupling, near_cols], [],
        [tailed, tailed, ((points, rank), BF16), block, (transfer.shape, BF16),
         ((2,) + coupling.shape[1:], BF16)],
        [pltpu.VMEM((points, rank), BF16), pltpu.VMEM((2, rows, rank), BF16),
         pltpu.SMEM(near_cols.shape, jnp.int32), pltpu.SemaphoreType.DMA((5,))],
        pltpu.HBM,
    )
    chip_sum = (keep.astype(F32) + turned(send, 1).astype(F32)).astype(BF16)
    even = neighbours(points_x, 0)
    chip_sum, even = lax.optimization_barrier((chip_sum, even))
    named = turned(chip_sum, 2)
    coef = (chip_sum[:rows].astype(F32) + named[:rows].astype(F32)).astype(BF16)

    mate = turned(points_x, 1)
    sent, even = lax.optimization_barrier((points_x, even))
    odd = neighbours(sent, 1)
    last = GROUP * leaf_count - 1
    joints = [(i, i + 1) for i in range(1, last, 2)]
    sent, coef = lax.optimization_barrier((points_x, coef))
    flat = lax.ppermute(sent, ("leaf", "level"), joints + [(b, a) for a, b in joints])
    mate_even = turned(even, 1)

    active = min(coupling.shape[0], leaf_count.bit_length())
    pairs = leaf_count // 2
    turns = [1, 2, 3] if pairs == 4 else [1, 2, 3, -1, -2, -3]
    clusters = [lev < active and (leaf_count >> lev) > 2 for lev in (0, 1)]
    *pushes, pair_coef = call(
        partial(push_kernel, turns, pairs, clusters), "push",
        [coef, swapped(coef, 0), coupling_in, transfer_in], [couple_mask.transpose(0, 2, 1)],
        [half] * (len(turns) + 1), [pltpu.VMEM((2, rows, rank), BF16)],
    )
    odd, flat, mate, mate_even, pushes = lax.optimization_barrier(
        (odd, flat, mate, mate_even, pushes)
    )
    mate_odd = turned(odd, 1)
    held = [own_x, even, odd, mate, mate_even, mate_odd]
    (pick,) = call(partial(pick_kernel, rows), "pick", [named] + held, [], [block])
    picked = turned(pick, 2)
    (acc,) = call(
        near_kernel, "near", held + [flat, near_tiles], [near_cols, near_count],
        [((vectors, points), F32)],
    )

    field = None
    for turn, push in zip(turns, pushes):
        if pairs == 4:
            came = lax.ppermute(push, "leaf", [(i, i ^ 2 * turn) for i in range(leaf_count)])
        else:
            came = shifted(push, 2 * turn)
        field = came.astype(F32) if field is None else field + came.astype(F32)
    if active > 2 and (leaf_count >> 2) > 2:
        field = field + upper_field(pair_coef, coupling, transfer, couple_mask)
    field = field.astype(BF16)
    mate_field = turned(field, 1)

    (out,) = call(
        finish_kernel, "finish",
        [acc, picked, near_tiles, w, field, mate_field], [near_cols, near_count],
        [block], [pltpu.VMEM((vectors, points), F32), pltpu.VMEM((2, rows, rank), BF16)],
    )
    return out


def solution(mesh):
    in_specs = (
        P(None, ("leaf", "level")),
        P(("leaf", "level"), None, None),
        P(("leaf", "level"), None, None, None),
        P(("leaf", "level"), None),
        P(("leaf", "level")),
        P(),
        P(),
        P(),
    )
    out_specs = P(None, ("leaf", "level"))
    return jax.shard_map(
        per_device, mesh=mesh, in_specs=in_specs, out_specs=out_specs, check_vma=False
    )
```

```python
from functools import partial

import jax
import jax.numpy as jnp
from jax import lax
from jax.experimental import pallas as pl
from jax.experimental.pallas import tpu as pltpu
from jax.sharding import PartitionSpec as P

VMEM_LIMIT = 32 * 1024 * 1024
F32 = jnp.float32
BF16 = jnp.bfloat16
GROUP = 4
SLOT = 3
TAIL = 32


def dot(a, b):
    return jnp.dot(a, b, preferred_element_type=F32)


def dot_t(a, b):
    return lax.dot_general(a, b, (((1,), (1,)), ((), ())), preferred_element_type=F32)


def call(kernel, name, inputs, scalars, outputs, scratch=(), inputs_in=pltpu.VMEM):
    shapes = [jax.ShapeDtypeStruct(shape, dtype) for shape, dtype in outputs]
    return pl.pallas_call(
        kernel,
        out_shape=shapes,
        in_specs=[pl.BlockSpec(memory_space=inputs_in)] * len(inputs)
        + [pl.BlockSpec(memory_space=pltpu.SMEM)] * len(scalars),
        out_specs=[pl.BlockSpec(memory_space=pltpu.VMEM)] * len(outputs),
        scratch_shapes=list(scratch),
        compiler_params=pltpu.CompilerParams(vmem_limit_bytes=VMEM_LIMIT),
        cost_estimate=pl.CostEstimate(flops=0, bytes_accessed=0, transcendentals=0),
        name=name,
    )(*(pltpu.with_memory_space_constraint(a, inputs_in) for a in inputs), *scalars)


def up_kernel(
    bits, x_hbm, basis_hbm, transfer_hbm, coupling_hbm, cols_hbm,
    keep_ref, send_ref, w_ref, x_ref, transfer_ref, coupling_ref, basis_ref, z_ref, cols_ref, sems
):
    pos = lax.axis_index("level")
    core = pos & 1
    pairs = (
        (basis_hbm.at[0], basis_ref), (transfer_hbm, transfer_ref), (x_hbm, x_ref),
        (coupling_hbm.at[:2], coupling_ref), (cols_hbm, cols_ref),
    )
    copies = [pltpu.make_async_copy(a, b, sems.at[i]) for i, (a, b) in enumerate(pairs)]
    for copy in copies:
        copy.start()
    copies[0].wait()
    copies[1].wait()
    w = basis_ref[...]
    for bit in range(bits):
        w = dot(w, transfer_ref[pos >> bit & 1]).astype(BF16)
    w_ref[...] = w
    copies[2].wait()
    z = dot(x_ref[...], w).astype(BF16)
    rows = z_ref.shape[1]
    z_ref[0] = z[:rows]
    z_ref[1] = z[rows:]
    keep_ref[:rows] = z_ref[core]
    send_ref[:rows] = z_ref[1 - core]
    copies[4].wait()
    tail = TAIL // 2
    for chip in range(2):
        named = jnp.where(pos >> 1 == chip, cols_ref[0, SLOT], 0).astype(F32)
        filled = jnp.full((tail, z.shape[1]), named, F32).astype(BF16)
        keep_ref[rows + chip * tail : rows + (chip + 1) * tail] = filled
    send_ref[rows:] = jnp.zeros((TAIL, z.shape[1]), BF16)
    copies[3].wait()


def push_kernel(
    turns, pairs, clusters, own_ref, mate_ref, coupling_ref, transfer_ref, mask_ref, *refs
):
    *push_refs, pair_ref, both_ref = refs
    leaf_pos = lax.axis_index("leaf")
    pair, side = leaf_pos >> 1, leaf_pos & 1
    rows = both_ref.shape[1]
    both_ref[side] = own_ref[:rows]
    both_ref[1 - side] = mate_ref[:rows]
    total = dot(both_ref[0], transfer_ref[0]) + dot(both_ref[1], transfer_ref[1])
    pair_ref[...] = total.astype(BF16)

    def term(lev, coef, gap, source, target):
        pick = abs(gap) - 2
        matrix = coupling_ref[lev, pick]
        switch = mask_ref[lev, pick, source if gap > 0 else target].astype(F32)
        return switch * (dot_t(coef, matrix) if gap > 0 else dot(coef, matrix))

    def fill(push_ref, distance, to_side):
        target_pair = pair + distance
        total = None
        if abs(distance) in (2, 3) and clusters[1]:
            coupled = term(1, pair_ref[...], distance, pair, target_pair).astype(BF16)
            total = dot_t(coupled, transfer_ref[to_side])
        for from_side in (0, 1):
            gap = 2 * distance + to_side - from_side
            if abs(gap) in (2, 3) and clusters[0]:
                more = term(
                    0, both_ref[from_side], gap, 2 * pair + from_side, 2 * target_pair + to_side
                )
                total = more if total is None else total + more
        if total is None:
            total = jnp.zeros(pair_ref.shape, F32)
        push_ref[:rows] = total.astype(BF16)

    for turn, push_ref in zip(turns, push_refs):
        push_ref[rows:] = mate_ref[rows:]
        for distance in reached(turn, pairs):
            if pairs == 4:
                inside = (pair ^ turn) == pair + distance
            else:
                inside = jnp.logical_and(pair + distance >= 0, pair + distance < pairs)
            for to_side in (0, 1):
                @pl.when(jnp.logical_and(inside, side == to_side))
                def _(push_ref=push_ref, distance=distance, to_side=to_side):
                    fill(push_ref, distance, to_side)


def reached(turn, pairs):
    return sorted({(i ^ turn) - i for i in range(pairs)}) if pairs == 4 else [turn]


def named_place(rows, ref):
    tail = TAIL // 2
    cols = [jnp.max(ref[rows + c * tail : rows + (c + 1) * tail].astype(F32)) for c in range(2)]
    col = jnp.where(lax.axis_index("level") >> 1 == 0, cols[0], cols[1]).astype(jnp.int32)
    return lax.rem(col, GROUP)


def pick_block(place, blocks, out_ref):
    turn = place ^ lax.axis_index("level")
    for at, block in enumerate(blocks):
        @pl.when(turn == at)
        def _(block=block):
            out_ref[...] = block[...]


def pick_even_kernel(rows, named_ref, *refs):
    *blocks, out_ref = refs
    pick_block(named_place(rows, named_ref), blocks, out_ref)


def pick_odd_kernel(rows, pairs, named_refs_count, *refs):
    named_refs, blocks, out_ref = refs[:named_refs_count], refs[named_refs_count:-1], refs[-1]
    leaf_pos = lax.axis_index("leaf")
    pair, side = leaf_pos >> 1, leaf_pos & 1
    places = [named_place(rows, ref) for ref in named_refs]
    if pairs == 4:
        inner = jnp.logical_or(
            jnp.logical_and(pair == 1, side == 1), jnp.logical_and(pair == 2, side == 0)
        )
    else:
        inner = side == 1
    pick_block(jnp.where(inner, places[1], places[0]), blocks, out_ref)


def near_kernel(
    x_ref, mate_ref, across_ref, corner_ref, edge_ref, tiles_ref, cols_ref, count_ref, acc_ref
):
    pos = lax.axis_index("level")
    odd = pos & 1
    inner = jnp.logical_or(pos == 1, pos == 2)
    acc = dot(x_ref[...], tiles_ref[0, 0]) + dot(mate_ref[...], tiles_ref[0, 2 - odd])
    beside = jnp.where(inner, corner_ref[...], edge_ref[...])
    acc_ref[...] = acc + dot(beside, tiles_ref[0, 1 + odd])
    col = cols_ref[0, SLOT]
    turn = lax.rem(col, GROUP) ^ pos
    here = jnp.logical_and(count_ref[0] > SLOT, col // GROUP == 1)
    for at, block in enumerate((x_ref, mate_ref, across_ref, corner_ref)):
        @pl.when(jnp.logical_and(here, turn == at))
        def _(block=block):
            acc_ref[...] += dot(block[...], tiles_ref[0, SLOT])


def finish_kernel(
    acc_ref, even_ref, odd_ref, tiles_ref, w_ref, own_field, mate_field,
    cols_ref, count_ref, out_ref, total_ref, field_ref
):
    core = lax.axis_index("level") & 1
    side = lax.axis_index("leaf") & 1
    field_ref[core] = own_field[...]
    field_ref[1 - core] = mate_field[...]
    field = jnp.concatenate([field_ref[0], field_ref[1]], axis=0)
    total_ref[...] = acc_ref[...] + dot_t(field, w_ref[...])
    group = cols_ref[0, SLOT] // GROUP
    live = jnp.logical_and(count_ref[0] > SLOT, group != 1)
    from_even = (group == 0) == (side == 1)

    @pl.when(jnp.logical_and(live, from_even))
    def _():
        total_ref[...] += dot(even_ref[...], tiles_ref[0, SLOT])

    @pl.when(jnp.logical_and(live, jnp.logical_not(from_even)))
    def _():
        total_ref[...] += dot(odd_ref[...], tiles_ref[0, SLOT])

    out_ref[...] = total_ref[...].astype(BF16)


def turned(value, turn):
    return lax.ppermute(value, "level", [(i, i ^ turn) for i in range(GROUP)])


def shifted(value, steps):
    count = lax.axis_size("leaf")
    route = [(i, i + steps) for i in range(count) if 0 <= i + steps < count]
    return lax.ppermute(value, "leaf", route)


def swapped(value, distance):
    count = lax.axis_size("leaf")
    return lax.ppermute(value, "leaf", [(i, i ^ 1 << distance) for i in range(count)])


def neighbours(value, odd):
    count = lax.axis_size("leaf")
    route = [(i, i + 1) for i in range(odd, count - 1, 2)]
    return lax.ppermute(value, "leaf", route + [(b, a) for a, b in route])


def upper_field(coef, coupling, transfer, couple_mask):
    leaf_count = lax.axis_size("leaf")
    leaf_pos = lax.axis_index("leaf")
    couplings = []
    levels = range(2, min(coupling.shape[0], leaf_count.bit_length()))
    for lev in levels:
        other = swapped(coef, lev - 1)
        is_upper = (leaf_pos >> lev - 1 & 1) == 1
        total = dot(jnp.where(is_upper, other, coef), transfer[0])
        total = total + dot(jnp.where(is_upper, coef, other), transfer[1])
        coef = total.astype(BF16)
        cluster = leaf_pos >> lev
        coupled = jnp.zeros(coef.shape, F32)
        for pick, offset in enumerate((2, 3)):
            if offset < leaf_count >> lev:
                matrix = coupling[lev, pick]
                ahead = shifted(coef, -(offset << lev))
                behind = shifted(coef, offset << lev)
                ahead_mask = couple_mask[lev, cluster, pick].astype(F32)
                behind_mask = couple_mask[lev, jnp.maximum(cluster - offset, 0), pick].astype(F32)
                coupled = coupled + ahead_mask * dot(ahead, matrix)
                coupled = coupled + behind_mask * dot_t(behind, matrix)
        couplings.append(coupled)
    field = jnp.zeros(coef.shape, F32)
    for lev, coupled in zip(reversed(levels), reversed(couplings)):
        if lev + 1 in levels:
            field = dot_t(field.astype(BF16), transfer[leaf_pos >> lev & 1])
        field = field + coupled
    for lev in (1, 0):
        field = dot_t(field.astype(BF16), transfer[leaf_pos >> lev & 1])
    return field


def per_device(
    points_x, leaf_basis, near_tiles, near_cols, near_count, transfer, coupling, couple_mask
):
    assert lax.axis_size("level") == GROUP
    leaf_count = lax.axis_size("leaf")
    vectors, points = points_x.shape
    rank = leaf_basis.shape[2]
    rows = vectors // 2
    bits = GROUP.bit_length() - 1
    block = ((vectors, points), BF16)
    half = ((rows, rank), BF16)
    tailed = ((rows + TAIL, rank), BF16)

    keep, send, w, own_x, transfer_in, coupling_in = call(
        partial(up_kernel, bits), "up",
        [points_x, leaf_basis, transfer, coupling, near_cols], [],
        [tailed, tailed, ((points, rank), BF16), block, (transfer.shape, BF16),
         ((2,) + coupling.shape[1:], BF16)],
        [pltpu.VMEM((points, rank), BF16), pltpu.VMEM((2, rows, rank), BF16),
         pltpu.SMEM(near_cols.shape, jnp.int32), pltpu.SemaphoreType.DMA((5,))],
        pltpu.HBM,
    )
    coef = (keep.astype(F32) + turned(send, 1).astype(F32)).astype(BF16)
    coef = (coef.astype(F32) + turned(coef, 2).astype(F32)).astype(BF16)
    beside = swapped(coef, 0)

    joints = [(GROUP * g - 1, GROUP * g) for g in range(1, leaf_count)]
    edge = lax.ppermute(points_x, ("leaf", "level"), joints + [(b, a) for a, b in joints])
    across = turned(points_x, 2)
    mate = turned(points_x, 1)
    edge, across, beside = lax.optimization_barrier((edge, across, beside))
    corner = turned(across, 1)
    held = [own_x, mate, across, corner]

    active = min(coupling.shape[0], leaf_count.bit_length())
    pairs = leaf_count // 2
    turns = [1, 2, 3] if pairs == 4 else [1, 2, 3, -1, -2, -3]
    clusters = [lev < active and (leaf_count >> lev) > 2 for lev in (0, 1)]
    *pushes, pair_coef = call(
        partial(push_kernel, turns, pairs, clusters), "push",
        [coef, beside, coupling_in, transfer_in], [couple_mask.transpose(0, 2, 1)],
        [tailed] * len(turns) + [half], [pltpu.VMEM((2, rows, rank), BF16)],
    )
    came = {}
    for turn, push in zip(turns, pushes):
        if pairs == 4:
            came[turn] = lax.ppermute(
                push, "leaf", [(i, i ^ 2 * turn) for i in range(leaf_count)]
            )
        else:
            came[turn] = shifted(push, 2 * turn)
    field = came[1][:rows].astype(F32)
    for turn in turns[1:]:
        field = field + came[turn][:rows].astype(F32)
    if active > 2 and (leaf_count >> 2) > 2:
        field = field + upper_field(pair_coef, coupling, transfer, couple_mask)
    field = field.astype(BF16)
    mate_field = turned(field, 1)

    (to_even,) = call(partial(pick_even_kernel, rows), "pick_even", [beside] + held, [], [block])
    from_even = neighbours(to_even, 0)
    named = [came[1], came[3 if pairs == 4 else -1]]
    (to_odd,) = call(
        partial(pick_odd_kernel, rows, pairs, len(named)), "pick_odd", named + held, [], [block]
    )
    from_odd = neighbours(to_odd, 1)
    (acc,) = call(
        near_kernel, "near", held + [edge, near_tiles], [near_cols, near_count],
        [((vectors, points), F32)],
    )
    (out,) = call(
        finish_kernel, "finish",
        [acc, from_even, from_odd, near_tiles, w, field, mate_field], [near_cols, near_count],
        [block], [pltpu.VMEM((vectors, points), F32), pltpu.VMEM((2, rows, rank), BF16)],
    )
    return out


def solution(mesh):
    in_specs = (
        P(None, ("leaf", "level")),
        P(("leaf", "level"), None, None),
        P(("leaf", "level"), None, None, None),
        P(("leaf", "level"), None),
        P(("leaf", "level")),
        P(),
        P(),
        P(),
    )
    out_specs = P(None, ("leaf", "level"))
    return jax.shard_map(
        per_device, mesh=mesh, in_specs=in_specs, out_specs=out_specs, check_vma=False
    )
```

```python
from functools import partial

import jax
import jax.numpy as jnp
from jax import lax
from jax.experimental import pallas as pl
from jax.experimental.pallas import tpu as pltpu
from jax.sharding import PartitionSpec as P

VMEM_LIMIT = 32 * 1024 * 1024
F32 = jnp.float32
BF16 = jnp.bfloat16
GROUP = 4
SLOT = 3
TAIL = 16


def dot(a, b):
    return jnp.dot(a, b, preferred_element_type=F32)


def dot_t(a, b):
    return lax.dot_general(a, b, (((1,), (1,)), ((), ())), preferred_element_type=F32)


def call(kernel, name, inputs, scalars, outputs, scratch=(), inputs_in=pltpu.VMEM):
    shapes = [jax.ShapeDtypeStruct(shape, dtype) for shape, dtype in outputs]
    return pl.pallas_call(
        kernel,
        out_shape=shapes,
        in_specs=[pl.BlockSpec(memory_space=inputs_in)] * len(inputs)
        + [pl.BlockSpec(memory_space=pltpu.SMEM)] * len(scalars),
        out_specs=[pl.BlockSpec(memory_space=pltpu.VMEM)] * len(outputs),
        scratch_shapes=list(scratch),
        compiler_params=pltpu.CompilerParams(vmem_limit_bytes=VMEM_LIMIT),
        cost_estimate=pl.CostEstimate(flops=0, bytes_accessed=0, transcendentals=0),
        name=name,
    )(*(pltpu.with_memory_space_constraint(a, inputs_in) for a in inputs), *scalars)


def up_kernel(
    bits, x_hbm, basis_hbm, transfer_hbm, coupling_hbm, cols_hbm,
    keep_ref, send_ref, w_ref, x_ref, transfer_ref, coupling_ref, basis_ref, z_ref, cols_ref, sems
):
    pos = lax.axis_index("level")
    chip, core = pos >> 1, pos & 1
    pairs = (
        (basis_hbm.at[0], basis_ref), (transfer_hbm, transfer_ref), (x_hbm, x_ref),
        (coupling_hbm.at[:2], coupling_ref), (cols_hbm, cols_ref),
    )
    copies = [pltpu.make_async_copy(a, b, sems.at[i]) for i, (a, b) in enumerate(pairs)]
    for copy in copies:
        copy.start()
    copies[0].wait()
    copies[1].wait()
    w = basis_ref[...]
    for bit in range(bits):
        w = dot(w, transfer_ref[pos >> bit & 1]).astype(BF16)
    w_ref[...] = w
    copies[2].wait()
    z = dot(x_ref[...], w).astype(BF16)
    rows = z_ref.shape[1]
    for part in range(GROUP):
        z_ref[part] = z[part * rows : (part + 1) * rows]
    copies[4].wait()
    lanes = lax.broadcasted_iota(jnp.int32, (TAIL, z.shape[1]), 1)
    first = lanes < z.shape[1] // 2
    tail = jnp.where(first == (chip == 0), cols_ref[0, SLOT], 0).astype(F32).astype(BF16)
    for at, half in enumerate((chip, 1 - chip)):
        low = at * (rows + TAIL)
        keep_ref[low : low + rows] = z_ref[2 * core + half]
        send_ref[low : low + rows] = z_ref[2 * (1 - core) + half]
        keep_ref[low + rows : low + rows + TAIL] = tail
        send_ref[low + rows : low + rows + TAIL] = jnp.zeros_like(tail)
    copies[3].wait()


def push_kernel(
    turns, pairs, clusters, own_ref, mate_ref, coupling_ref, transfer_ref, mask_ref, *refs
):
    *push_refs, pair_ref, both_ref = refs
    leaf_pos = lax.axis_index("leaf")
    pair, side = leaf_pos >> 1, leaf_pos & 1
    rows = both_ref.shape[1]
    both_ref[side] = own_ref[:rows]
    both_ref[1 - side] = mate_ref[:rows]
    total = dot(both_ref[0], transfer_ref[0]) + dot(both_ref[1], transfer_ref[1])
    pair_ref[...] = total.astype(BF16)

    def term(lev, coef, gap, source, target):
        pick = abs(gap) - 2
        matrix = coupling_ref[lev, pick]
        switch = mask_ref[lev, pick, source if gap > 0 else target].astype(F32)
        return switch * (dot_t(coef, matrix) if gap > 0 else dot(coef, matrix))

    def fill(push_ref, distance, to_side):
        target_pair = pair + distance
        total = None
        if abs(distance) in (2, 3) and clusters[1]:
            coupled = term(1, pair_ref[...], distance, pair, target_pair).astype(BF16)
            total = dot_t(coupled, transfer_ref[to_side])
        for from_side in (0, 1):
            gap = 2 * distance + to_side - from_side
            if abs(gap) in (2, 3) and clusters[0]:
                more = term(
                    0, both_ref[from_side], gap, 2 * pair + from_side, 2 * target_pair + to_side
                )
                total = more if total is None else total + more
        if total is None:
            total = jnp.zeros(pair_ref.shape, F32)
        push_ref[:rows] = total.astype(BF16)

    for turn, push_ref in zip(turns, push_refs):
        push_ref[rows:] = mate_ref[rows:]
        for distance in reached(turn, pairs):
            if pairs == 4:
                inside = (pair ^ turn) == pair + distance
            else:
                inside = jnp.logical_and(pair + distance >= 0, pair + distance < pairs)
            for to_side in (0, 1):
                @pl.when(jnp.logical_and(inside, side == to_side))
                def _(push_ref=push_ref, distance=distance, to_side=to_side):
                    fill(push_ref, distance, to_side)


def reached(turn, pairs):
    return sorted({(i ^ turn) - i for i in range(pairs)}) if pairs == 4 else [turn]


def named_place(rows, ref):
    half = ref.shape[1] // 2
    cols = [jnp.max(ref[rows:, at : at + half].astype(F32)) for at in (0, half)]
    col = jnp.where(lax.axis_index("level") >> 1 == 0, cols[0], cols[1]).astype(jnp.int32)
    return lax.rem(col, GROUP)


def pick_block(place, blocks, out_ref):
    turn = place ^ lax.axis_index("level")
    for at, block in enumerate(blocks):
        @pl.when(turn == at)
        def _(block=block):
            out_ref[...] = block[...]


def pick_even_kernel(rows, named_ref, *refs):
    *blocks, out_ref = refs
    pick_block(named_place(rows, named_ref), blocks, out_ref)


def pick_odd_kernel(rows, pairs, named_refs_count, *refs):
    named_refs, blocks, out_ref = refs[:named_refs_count], refs[named_refs_count:-1], refs[-1]
    leaf_pos = lax.axis_index("leaf")
    pair, side = leaf_pos >> 1, leaf_pos & 1
    places = [named_place(rows, ref) for ref in named_refs]
    if pairs == 4:
        inner = jnp.logical_or(
            jnp.logical_and(pair == 1, side == 1), jnp.logical_and(pair == 2, side == 0)
        )
    else:
        inner = side == 1
    pick_block(jnp.where(inner, places[1], places[0]), blocks, out_ref)


def near_kernel(
    x_ref, mate_ref, across_ref, corner_ref, edge_ref, tiles_ref, w_ref, field0, field1, field2,
    field3, cols_ref, count_ref, acc_ref, field_ref
):
    pos = lax.axis_index("level")
    for turn, part_ref in enumerate((field0, field1, field2, field3)):
        field_ref[part_of(pos ^ turn)] = part_ref[...]
    field = jnp.concatenate([field_ref[part] for part in range(GROUP)], axis=0)
    odd = pos & 1
    inner = jnp.logical_or(pos == 1, pos == 2)
    acc = dot(x_ref[...], tiles_ref[0, 0]) + dot(mate_ref[...], tiles_ref[0, 2 - odd])
    beside = jnp.where(inner, corner_ref[...], edge_ref[...])
    acc = acc + dot(beside, tiles_ref[0, 1 + odd])
    acc_ref[...] = acc + dot_t(field, w_ref[...])
    col = cols_ref[0, SLOT]
    turn = lax.rem(col, GROUP) ^ pos
    here = jnp.logical_and(count_ref[0] > SLOT, col // GROUP == 1)
    for at, block in enumerate((x_ref, mate_ref, across_ref, corner_ref)):
        @pl.when(jnp.logical_and(here, turn == at))
        def _(block=block):
            acc_ref[...] += dot(block[...], tiles_ref[0, SLOT])


def finish_kernel(acc_ref, even_ref, odd_ref, tiles_ref, cols_ref, count_ref, out_ref):
    side = lax.axis_index("leaf") & 1
    group = cols_ref[0, SLOT] // GROUP
    live = jnp.logical_and(count_ref[0] > SLOT, group != 1)
    from_even = (group == 0) == (side == 1)

    @pl.when(jnp.logical_not(live))
    def _():
        out_ref[...] = acc_ref[...].astype(BF16)

    for here, block in ((from_even, even_ref), (jnp.logical_not(from_even), odd_ref)):
        @pl.when(jnp.logical_and(live, here))
        def _(block=block):
            out_ref[...] = (acc_ref[...] + dot(block[...], tiles_ref[0, SLOT])).astype(BF16)


def part_of(pos):
    return 2 * (pos & 1) + (pos >> 1)


def turned(value, turn):
    return lax.ppermute(value, "level", [(i, i ^ turn) for i in range(GROUP)])


def shifted(value, steps):
    count = lax.axis_size("leaf")
    route = [(i, i + steps) for i in range(count) if 0 <= i + steps < count]
    return lax.ppermute(value, "leaf", route)


def swapped(value, distance):
    count = lax.axis_size("leaf")
    return lax.ppermute(value, "leaf", [(i, i ^ 1 << distance) for i in range(count)])


def neighbours(value, odd):
    count = lax.axis_size("leaf")
    route = [(i, i + 1) for i in range(odd, count - 1, 2)]
    return lax.ppermute(value, "leaf", route + [(b, a) for a, b in route])


def upper_field(coef, coupling, transfer, couple_mask):
    leaf_count = lax.axis_size("leaf")
    leaf_pos = lax.axis_index("leaf")
    couplings = []
    levels = range(2, min(coupling.shape[0], leaf_count.bit_length()))
    for lev in levels:
        other = swapped(coef, lev - 1)
        is_upper = (leaf_pos >> lev - 1 & 1) == 1
        total = dot(jnp.where(is_upper, other, coef), transfer[0])
        total = total + dot(jnp.where(is_upper, coef, other), transfer[1])
        coef = total.astype(BF16)
        cluster = leaf_pos >> lev
        coupled = jnp.zeros(coef.shape, F32)
        for pick, offset in enumerate((2, 3)):
            if offset < leaf_count >> lev:
                matrix = coupling[lev, pick]
                ahead = shifted(coef, -(offset << lev))
                behind = shifted(coef, offset << lev)
                ahead_mask = couple_mask[lev, cluster, pick].astype(F32)
                behind_mask = couple_mask[lev, jnp.maximum(cluster - offset, 0), pick].astype(F32)
                coupled = coupled + ahead_mask * dot(ahead, matrix)
                coupled = coupled + behind_mask * dot_t(behind, matrix)
        couplings.append(coupled)
    field = jnp.zeros(coef.shape, F32)
    for lev, coupled in zip(reversed(levels), reversed(couplings)):
        if lev + 1 in levels:
            field = dot_t(field.astype(BF16), transfer[leaf_pos >> lev & 1])
        field = field + coupled
    for lev in (1, 0):
        field = dot_t(field.astype(BF16), transfer[leaf_pos >> lev & 1])
    return field


def per_device(
    points_x, leaf_basis, near_tiles, near_cols, near_count, transfer, coupling, couple_mask
):
    assert lax.axis_size("level") == GROUP
    leaf_count = lax.axis_size("leaf")
    vectors, points = points_x.shape
    rank = leaf_basis.shape[2]
    rows = vectors // GROUP
    bits = GROUP.bit_length() - 1
    block = ((vectors, points), BF16)
    part = ((rows, rank), BF16)
    tailed = ((rows + TAIL, rank), BF16)
    doubled = ((2 * (rows + TAIL), rank), BF16)

    keep, send, w, own_x, transfer_in, coupling_in = call(
        partial(up_kernel, bits), "up",
        [points_x, leaf_basis, transfer, coupling, near_cols], [],
        [doubled, doubled, ((points, rank), BF16), block, (transfer.shape, BF16),
         ((2,) + coupling.shape[1:], BF16)],
        [pltpu.VMEM((points, rank), BF16), pltpu.VMEM((GROUP, rows, rank), BF16),
         pltpu.SMEM(near_cols.shape, jnp.int32), pltpu.SemaphoreType.DMA((5,))],
        pltpu.HBM,
    )
    chip_sum = (keep.astype(F32) + turned(send, 1).astype(F32)).astype(BF16)
    came_half = turned(chip_sum[rows + TAIL :], 2)
    joints = [(GROUP * g - 1, GROUP * g) for g in range(1, leaf_count)]
    edge = lax.ppermute(points_x, ("leaf", "level"), joints + [(b, a) for a, b in joints])
    edge, came_half = lax.optimization_barrier((edge, came_half))
    coef = (chip_sum[: rows + TAIL].astype(F32) + came_half.astype(F32)).astype(BF16)
    beside = swapped(coef, 0)

    across = turned(points_x, 2)
    mate = turned(points_x, 1)
    across, beside = lax.optimization_barrier((across, beside))
    corner = turned(across, 1)

    active = min(coupling.shape[0], leaf_count.bit_length())
    pairs = leaf_count // 2
    turns = [1, 2, 3] if pairs == 4 else [1, 2, 3, -1, -2, -3]
    clusters = [lev < active and (leaf_count >> lev) > 2 for lev in (0, 1)]
    *pushes, pair_coef = call(
        partial(push_kernel, turns, pairs, clusters), "push",
        [coef, beside, coupling_in, transfer_in], [couple_mask.transpose(0, 2, 1)],
        [tailed] * len(turns) + [part], [pltpu.VMEM((2, rows, rank), BF16)],
    )
    mate, corner, pushes = lax.optimization_barrier((mate, corner, pushes))
    held = [own_x, mate, across, corner]
    came = {}
    for turn, push in zip(turns, pushes):
        if pairs == 4:
            came[turn] = lax.ppermute(
                push, "leaf", [(i, i ^ 2 * turn) for i in range(leaf_count)]
            )
        else:
            came[turn] = shifted(push, 2 * turn)
    field = came[1][:rows].astype(F32)
    for turn in turns[1:]:
        field = field + came[turn][:rows].astype(F32)
    if active > 2 and (leaf_count >> 2) > 2:
        field = field + upper_field(pair_coef, coupling, transfer, couple_mask)
    field = field.astype(BF16)

    (to_even,) = call(partial(pick_even_kernel, rows), "pick_even", [beside] + held, [], [block])
    from_even = neighbours(to_even, 0)
    named = [came[1], came[3 if pairs == 4 else -1]]
    (to_odd,) = call(
        partial(pick_odd_kernel, rows, pairs, len(named)), "pick_odd", named + held, [], [block]
    )
    field, to_odd = lax.optimization_barrier((field, to_odd))
    fields = [field] + [turned(field, turn) for turn in range(1, GROUP)]
    from_odd = neighbours(to_odd, 1)
    (acc,) = call(
        near_kernel, "near", held + [edge, near_tiles, w] + fields, [near_cols, near_count],
        [((vectors, points), F32)], [pltpu.VMEM((GROUP, rows, rank), BF16)],
    )
    (out,) = call(
        finish_kernel, "finish", [acc, from_even, from_odd, near_tiles], [near_cols, near_count],
        [block],
    )
    return out


def solution(mesh):
    in_specs = (
        P(None, ("leaf", "level")),
        P(("leaf", "level"), None, None),
        P(("leaf", "level"), None, None, None),
        P(("leaf", "level"), None),
        P(("leaf", "level")),
        P(),
        P(),
        P(),
    )
    out_specs = P(None, ("leaf", "level"))
    return jax.shard_map(
        per_device, mesh=mesh, in_specs=in_specs, out_specs=out_specs, check_vma=False
    )
```

```python
from functools import partial

import jax
import jax.numpy as jnp
from jax import lax
from jax.experimental import pallas as pl
from jax.experimental.pallas import tpu as pltpu
from jax.sharding import PartitionSpec as P

VMEM_LIMIT = 32 * 1024 * 1024
F32 = jnp.float32
BF16 = jnp.bfloat16
GROUP = 4
SLOT = 3
TAIL = 16


def dot(a, b):
    return jnp.dot(a, b, preferred_element_type=F32)


def dot_t(a, b):
    return lax.dot_general(a, b, (((1,), (1,)), ((), ())), preferred_element_type=F32)


def call(kernel, name, inputs, scalars, outputs, scratch=(), inputs_in=pltpu.VMEM):
    shapes = [jax.ShapeDtypeStruct(shape, dtype) for shape, dtype in outputs]
    return pl.pallas_call(
        kernel,
        out_shape=shapes,
        in_specs=[pl.BlockSpec(memory_space=inputs_in)] * len(inputs)
        + [pl.BlockSpec(memory_space=pltpu.SMEM)] * len(scalars),
        out_specs=[pl.BlockSpec(memory_space=pltpu.VMEM)] * len(outputs),
        scratch_shapes=list(scratch),
        compiler_params=pltpu.CompilerParams(vmem_limit_bytes=VMEM_LIMIT),
        cost_estimate=pl.CostEstimate(flops=0, bytes_accessed=0, transcendentals=0),
        name=name,
    )(*(pltpu.with_memory_space_constraint(a, inputs_in) for a in inputs), *scalars)


def up_kernel(
    bits, x_hbm, basis_hbm, transfer_hbm, coupling_hbm, cols_hbm,
    keep_ref, send_ref, w_ref, x_ref, transfer_ref, coupling_ref, basis_ref, z_ref, cols_ref, sems
):
    pos = lax.axis_index("level")
    chip, core = pos >> 1, pos & 1
    pairs = (
        (basis_hbm.at[0], basis_ref), (transfer_hbm, transfer_ref), (x_hbm, x_ref),
        (coupling_hbm.at[:2], coupling_ref), (cols_hbm, cols_ref),
    )
    copies = [pltpu.make_async_copy(a, b, sems.at[i]) for i, (a, b) in enumerate(pairs)]
    for copy in copies:
        copy.start()
    copies[0].wait()
    copies[1].wait()
    w = basis_ref[...]
    for bit in range(bits):
        w = dot(w, transfer_ref[pos >> bit & 1]).astype(BF16)
    w_ref[...] = w
    copies[2].wait()
    z = dot(x_ref[...], w).astype(BF16)
    rows = z_ref.shape[1]
    for part in range(GROUP):
        z_ref[part] = z[part * rows : (part + 1) * rows]
    copies[4].wait()
    lanes = lax.broadcasted_iota(jnp.int32, (TAIL, z.shape[1]), 1)
    first = lanes < z.shape[1] // 2
    tail = jnp.where(first == (chip == 0), cols_ref[0, SLOT], 0).astype(F32).astype(BF16)
    for at, half in enumerate((chip, 1 - chip)):
        low = at * (rows + TAIL)
        keep_ref[low : low + rows] = z_ref[2 * core + half]
        send_ref[low : low + rows] = z_ref[2 * (1 - core) + half]
        keep_ref[low + rows : low + rows + TAIL] = tail
        send_ref[low + rows : low + rows + TAIL] = jnp.zeros_like(tail)
    copies[3].wait()


def push_kernel(
    turns, pairs, clusters, own_ref, mate_ref, coupling_ref, transfer_ref, mask_ref, *refs
):
    *push_refs, pair_ref, both_ref = refs
    leaf_pos = lax.axis_index("leaf")
    pair, side = leaf_pos >> 1, leaf_pos & 1
    rows = both_ref.shape[1]
    both_ref[side] = own_ref[:rows]
    both_ref[1 - side] = mate_ref[:rows]
    total = dot(both_ref[0], transfer_ref[0]) + dot(both_ref[1], transfer_ref[1])
    pair_ref[...] = total.astype(BF16)

    def term(lev, coef, gap, source, target):
        pick = abs(gap) - 2
        matrix = coupling_ref[lev, pick]
        switch = mask_ref[lev, pick, source if gap > 0 else target].astype(F32)
        return switch * (dot_t(coef, matrix) if gap > 0 else dot(coef, matrix))

    def fill(push_ref, distance, to_side):
        target_pair = pair + distance
        total = None
        if abs(distance) in (2, 3) and clusters[1]:
            coupled = term(1, pair_ref[...], distance, pair, target_pair).astype(BF16)
            total = dot_t(coupled, transfer_ref[to_side])
        for from_side in (0, 1):
            gap = 2 * distance + to_side - from_side
            if abs(gap) in (2, 3) and clusters[0]:
                more = term(
                    0, both_ref[from_side], gap, 2 * pair + from_side, 2 * target_pair + to_side
                )
                total = more if total is None else total + more
        if total is None:
            total = jnp.zeros(pair_ref.shape, F32)
        push_ref[:rows] = total.astype(BF16)

    for turn, push_ref in zip(turns, push_refs):
        push_ref[rows:] = mate_ref[rows:]
        for distance in reached(turn, pairs):
            if pairs == 4:
                inside = (pair ^ turn) == pair + distance
            else:
                inside = jnp.logical_and(pair + distance >= 0, pair + distance < pairs)
            for to_side in (0, 1):
                @pl.when(jnp.logical_and(inside, side == to_side))
                def _(push_ref=push_ref, distance=distance, to_side=to_side):
                    fill(push_ref, distance, to_side)


def reached(turn, pairs):
    return sorted({(i ^ turn) - i for i in range(pairs)}) if pairs == 4 else [turn]


def named_place(rows, ref):
    half = ref.shape[1] // 2
    cols = [jnp.max(ref[rows:, at : at + half].astype(F32)) for at in (0, half)]
    col = jnp.where(lax.axis_index("level") >> 1 == 0, cols[0], cols[1]).astype(jnp.int32)
    return lax.rem(col, GROUP)


def pick_block(place, blocks, out_ref):
    turn = place ^ lax.axis_index("level")
    for at, block in enumerate(blocks):
        @pl.when(turn == at)
        def _(block=block):
            out_ref[...] = block[...]


def pick_even_kernel(rows, named_ref, *refs):
    *blocks, out_ref = refs
    pick_block(named_place(rows, named_ref), blocks, out_ref)


def pick_odd_kernel(rows, pairs, named_refs_count, *refs):
    named_refs, blocks, out_ref = refs[:named_refs_count], refs[named_refs_count:-1], refs[-1]
    leaf_pos = lax.axis_index("leaf")
    pair, side = leaf_pos >> 1, leaf_pos & 1
    places = [named_place(rows, ref) for ref in named_refs]
    if pairs == 4:
        inner = jnp.logical_or(
            jnp.logical_and(pair == 1, side == 1), jnp.logical_and(pair == 2, side == 0)
        )
    else:
        inner = side == 1
    pick_block(jnp.where(inner, places[1], places[0]), blocks, out_ref)


def near_kernel(
    x_ref, mate_ref, across_ref, corner_ref, edge_ref, tiles_ref, w_ref, field0, field1, field2,
    field3, cols_ref, count_ref, acc_ref, field_ref
):
    pos = lax.axis_index("level")
    for turn, part_ref in enumerate((field0, field1, field2, field3)):
        field_ref[part_of(pos ^ turn)] = part_ref[...]
    field = jnp.concatenate([field_ref[part] for part in range(GROUP)], axis=0)
    odd = pos & 1
    inner = jnp.logical_or(pos == 1, pos == 2)
    acc = dot(x_ref[...], tiles_ref[0, 0]) + dot(mate_ref[...], tiles_ref[0, 2 - odd])
    beside = jnp.where(inner, corner_ref[...], edge_ref[...])
    acc = acc + dot(beside, tiles_ref[0, 1 + odd])
    acc_ref[...] = acc + dot_t(field, w_ref[...])
    col = cols_ref[0, SLOT]
    turn = lax.rem(col, GROUP) ^ pos
    here = jnp.logical_and(count_ref[0] > SLOT, col // GROUP == 1)
    for at, block in enumerate((x_ref, mate_ref, across_ref, corner_ref)):
        @pl.when(jnp.logical_and(here, turn == at))
        def _(block=block):
            acc_ref[...] += dot(block[...], tiles_ref[0, SLOT])


def finish_kernel(acc_ref, even_ref, odd_ref, tiles_ref, cols_ref, count_ref, out_ref):
    side = lax.axis_index("leaf") & 1
    group = cols_ref[0, SLOT] // GROUP
    live = jnp.logical_and(count_ref[0] > SLOT, group != 1)
    from_even = (group == 0) == (side == 1)

    @pl.when(jnp.logical_not(live))
    def _():
        out_ref[...] = acc_ref[...].astype(BF16)

    for here, block in ((from_even, even_ref), (jnp.logical_not(from_even), odd_ref)):
        @pl.when(jnp.logical_and(live, here))
        def _(block=block):
            out_ref[...] = (acc_ref[...] + dot(block[...], tiles_ref[0, SLOT])).astype(BF16)


def part_of(pos):
    return 2 * (pos & 1) + (pos >> 1)


def turned(value, turn):
    return lax.ppermute(value, "level", [(i, i ^ turn) for i in range(GROUP)])


def shifted(value, steps):
    count = lax.axis_size("leaf")
    route = [(i, i + steps) for i in range(count) if 0 <= i + steps < count]
    return lax.ppermute(value, "leaf", route)


def swapped(value, distance):
    count = lax.axis_size("leaf")
    return lax.ppermute(value, "leaf", [(i, i ^ 1 << distance) for i in range(count)])


def neighbours(value, odd):
    count = lax.axis_size("leaf")
    route = [(i, i + 1) for i in range(odd, count - 1, 2)]
    return lax.ppermute(value, "leaf", route + [(b, a) for a, b in route])


def upper_field(coef, coupling, transfer, couple_mask):
    leaf_count = lax.axis_size("leaf")
    leaf_pos = lax.axis_index("leaf")
    couplings = []
    levels = range(2, min(coupling.shape[0], leaf_count.bit_length()))
    for lev in levels:
        other = swapped(coef, lev - 1)
        is_upper = (leaf_pos >> lev - 1 & 1) == 1
        total = dot(jnp.where(is_upper, other, coef), transfer[0])
        total = total + dot(jnp.where(is_upper, coef, other), transfer[1])
        coef = total.astype(BF16)
        cluster = leaf_pos >> lev
        coupled = jnp.zeros(coef.shape, F32)
        for pick, offset in enumerate((2, 3)):
            if offset < leaf_count >> lev:
                matrix = coupling[lev, pick]
                ahead = shifted(coef, -(offset << lev))
                behind = shifted(coef, offset << lev)
                ahead_mask = couple_mask[lev, cluster, pick].astype(F32)
                behind_mask = couple_mask[lev, jnp.maximum(cluster - offset, 0), pick].astype(F32)
                coupled = coupled + ahead_mask * dot(ahead, matrix)
                coupled = coupled + behind_mask * dot_t(behind, matrix)
        couplings.append(coupled)
    field = jnp.zeros(coef.shape, F32)
    for lev, coupled in zip(reversed(levels), reversed(couplings)):
        if lev + 1 in levels:
            field = dot_t(field.astype(BF16), transfer[leaf_pos >> lev & 1])
        field = field + coupled
    for lev in (1, 0):
        field = dot_t(field.astype(BF16), transfer[leaf_pos >> lev & 1])
    return field


def per_device(
    points_x, leaf_basis, near_tiles, near_cols, near_count, transfer, coupling, couple_mask
):
    assert lax.axis_size("level") == GROUP
    leaf_count = lax.axis_size("leaf")
    vectors, points = points_x.shape
    rank = leaf_basis.shape[2]
    rows = vectors // GROUP
    bits = GROUP.bit_length() - 1
    block = ((vectors, points), BF16)
    part = ((rows, rank), BF16)
    tailed = ((rows + TAIL, rank), BF16)
    doubled = ((2 * (rows + TAIL), rank), BF16)

    keep, send, w, own_x, transfer_in, coupling_in = call(
        partial(up_kernel, bits), "up",
        [points_x, leaf_basis, transfer, coupling, near_cols], [],
        [doubled, doubled, ((points, rank), BF16), block, (transfer.shape, BF16),
         ((2,) + coupling.shape[1:], BF16)],
        [pltpu.VMEM((points, rank), BF16), pltpu.VMEM((GROUP, rows, rank), BF16),
         pltpu.SMEM(near_cols.shape, jnp.int32), pltpu.SemaphoreType.DMA((5,))],
        pltpu.HBM,
    )
    chip_sum = (keep.astype(F32) + turned(send, 1).astype(F32)).astype(BF16)
    came_half = turned(chip_sum[rows + TAIL :], 2)
    coef = (chip_sum[: rows + TAIL].astype(F32) + came_half.astype(F32)).astype(BF16)
    sent, coef = lax.optimization_barrier((points_x, coef))
    joints = [(GROUP * g - 1, GROUP * g) for g in range(1, leaf_count)]
    edge = lax.ppermute(sent, ("leaf", "level"), joints + [(b, a) for a, b in joints])
    beside = swapped(coef, 0)

    across = turned(points_x, 2)
    mate = turned(points_x, 1)
    across, beside = lax.optimization_barrier((across, beside))
    corner = turned(across, 1)

    active = min(coupling.shape[0], leaf_count.bit_length())
    pairs = leaf_count // 2
    turns = [1, 2, 3] if pairs == 4 else [1, 2, 3, -1, -2, -3]
    clusters = [lev < active and (leaf_count >> lev) > 2 for lev in (0, 1)]
    *pushes, pair_coef = call(
        partial(push_kernel, turns, pairs, clusters), "push",
        [coef, beside, coupling_in, transfer_in], [couple_mask.transpose(0, 2, 1)],
        [tailed] * len(turns) + [part], [pltpu.VMEM((2, rows, rank), BF16)],
    )
    edge, mate, corner, pushes = lax.optimization_barrier((edge, mate, corner, pushes))
    held = [own_x, mate, across, corner]
    came = {}
    for turn, push in zip(turns, pushes):
        if pairs == 4:
            came[turn] = lax.ppermute(
                push, "leaf", [(i, i ^ 2 * turn) for i in range(leaf_count)]
            )
        else:
            came[turn] = shifted(push, 2 * turn)
    field = came[1][:rows].astype(F32)
    for turn in turns[1:]:
        field = field + came[turn][:rows].astype(F32)
    if active > 2 and (leaf_count >> 2) > 2:
        field = field + upper_field(pair_coef, coupling, transfer, couple_mask)
    field = field.astype(BF16)

    (to_even,) = call(partial(pick_even_kernel, rows), "pick_even", [beside] + held, [], [block])
    from_even = neighbours(to_even, 0)
    named = [came[1], came[3 if pairs == 4 else -1]]
    (to_odd,) = call(
        partial(pick_odd_kernel, rows, pairs, len(named)), "pick_odd", named + held, [], [block]
    )
    field, to_odd = lax.optimization_barrier((field, to_odd))
    fields = [field] + [turned(field, turn) for turn in range(1, GROUP)]
    from_odd = neighbours(to_odd, 1)
    (acc,) = call(
        near_kernel, "near", held + [edge, near_tiles, w] + fields, [near_cols, near_count],
        [((vectors, points), F32)], [pltpu.VMEM((GROUP, rows, rank), BF16)],
    )
    (out,) = call(
        finish_kernel, "finish", [acc, from_even, from_odd, near_tiles], [near_cols, near_count],
        [block],
    )
    return out


def solution(mesh):
    in_specs = (
        P(None, ("leaf", "level")),
        P(("leaf", "level"), None, None),
        P(("leaf", "level"), None, None, None),
        P(("leaf", "level"), None),
        P(("leaf", "level")),
        P(),
        P(),
        P(),
    )
    out_specs = P(None, ("leaf", "level"))
    return jax.shard_map(
        per_device, mesh=mesh, in_specs=in_specs, out_specs=out_specs, check_vma=False
    )
```

```python
from functools import partial

import jax
import jax.numpy as jnp
from jax import lax
from jax.experimental import pallas as pl
from jax.experimental.pallas import tpu as pltpu
from jax.sharding import PartitionSpec as P

VMEM_LIMIT = 32 * 1024 * 1024
F32 = jnp.float32
BF16 = jnp.bfloat16
GROUP = 4
SLOT = 3
TAIL = 16


def dot(a, b):
    return jnp.dot(a, b, preferred_element_type=F32)


def dot_t(a, b):
    return lax.dot_general(a, b, (((1,), (1,)), ((), ())), preferred_element_type=F32)


def call(kernel, name, inputs, scalars, outputs, scratch=(), inputs_in=pltpu.VMEM):
    shapes = [jax.ShapeDtypeStruct(shape, dtype) for shape, dtype in outputs]
    return pl.pallas_call(
        kernel,
        out_shape=shapes,
        in_specs=[pl.BlockSpec(memory_space=inputs_in)] * len(inputs)
        + [pl.BlockSpec(memory_space=pltpu.SMEM)] * len(scalars),
        out_specs=[pl.BlockSpec(memory_space=pltpu.VMEM)] * len(outputs),
        scratch_shapes=list(scratch),
        compiler_params=pltpu.CompilerParams(vmem_limit_bytes=VMEM_LIMIT),
        cost_estimate=pl.CostEstimate(flops=0, bytes_accessed=0, transcendentals=0),
        name=name,
    )(*(pltpu.with_memory_space_constraint(a, inputs_in) for a in inputs), *scalars)


def up_kernel(
    bits, x_hbm, basis_hbm, transfer_hbm, coupling_hbm, cols_hbm,
    keep_ref, send_ref, w_ref, x_ref, transfer_ref, coupling_ref, basis_ref, z_ref, cols_ref, sems
):
    pos = lax.axis_index("level")
    chip, core = pos >> 1, pos & 1
    pairs = (
        (basis_hbm.at[0], basis_ref), (transfer_hbm, transfer_ref), (x_hbm, x_ref),
        (coupling_hbm.at[:2], coupling_ref), (cols_hbm, cols_ref),
    )
    copies = [pltpu.make_async_copy(a, b, sems.at[i]) for i, (a, b) in enumerate(pairs)]
    for copy in copies:
        copy.start()
    copies[0].wait()
    copies[1].wait()
    w = basis_ref[...]
    for bit in range(bits):
        w = dot(w, transfer_ref[pos >> bit & 1]).astype(BF16)
    w_ref[...] = w
    copies[2].wait()
    z = dot(x_ref[...], w).astype(BF16)
    rows = z_ref.shape[1]
    for part in range(GROUP):
        z_ref[part] = z[part * rows : (part + 1) * rows]
    copies[4].wait()
    lanes = lax.broadcasted_iota(jnp.int32, (TAIL, z.shape[1]), 1)
    first = lanes < z.shape[1] // 2
    tail = jnp.where(first == (chip == 0), cols_ref[0, SLOT], 0).astype(F32).astype(BF16)
    for at, half in enumerate((chip, 1 - chip)):
        low = at * (rows + TAIL)
        keep_ref[low : low + rows] = z_ref[2 * core + half]
        send_ref[low : low + rows] = z_ref[2 * (1 - core) + half]
        keep_ref[low + rows : low + rows + TAIL] = tail
        send_ref[low + rows : low + rows + TAIL] = jnp.zeros_like(tail)
    copies[3].wait()


def push_kernel(
    turns, pairs, clusters, own_ref, mate_ref, coupling_ref, transfer_ref, mask_ref, *refs
):
    *push_refs, pair_ref, both_ref = refs
    leaf_pos = lax.axis_index("leaf")
    pair, side = leaf_pos >> 1, leaf_pos & 1
    rows = both_ref.shape[1]
    both_ref[side] = own_ref[:rows]
    both_ref[1 - side] = mate_ref[:rows]
    total = dot(both_ref[0], transfer_ref[0]) + dot(both_ref[1], transfer_ref[1])
    pair_ref[...] = total.astype(BF16)

    def term(lev, coef, gap, source, target):
        pick = abs(gap) - 2
        matrix = coupling_ref[lev, pick]
        switch = mask_ref[lev, pick, source if gap > 0 else target].astype(F32)
        return switch * (dot_t(coef, matrix) if gap > 0 else dot(coef, matrix))

    def fill(push_ref, distance, to_side):
        target_pair = pair + distance
        total = None
        if abs(distance) in (2, 3) and clusters[1]:
            coupled = term(1, pair_ref[...], distance, pair, target_pair).astype(BF16)
            total = dot_t(coupled, transfer_ref[to_side])
        for from_side in (0, 1):
            gap = 2 * distance + to_side - from_side
            if abs(gap) in (2, 3) and clusters[0]:
                more = term(
                    0, both_ref[from_side], gap, 2 * pair + from_side, 2 * target_pair + to_side
                )
                total = more if total is None else total + more
        if total is None:
            total = jnp.zeros(pair_ref.shape, F32)
        push_ref[:rows] = total.astype(BF16)

    for turn, push_ref in zip(turns, push_refs):
        push_ref[rows:] = mate_ref[rows:]
        for distance in reached(turn, pairs):
            if pairs == 4:
                inside = (pair ^ turn) == pair + distance
            else:
                inside = jnp.logical_and(pair + distance >= 0, pair + distance < pairs)
            for to_side in (0, 1):
                @pl.when(jnp.logical_and(inside, side == to_side))
                def _(push_ref=push_ref, distance=distance, to_side=to_side):
                    fill(push_ref, distance, to_side)


def reached(turn, pairs):
    return sorted({(i ^ turn) - i for i in range(pairs)}) if pairs == 4 else [turn]


def named_place(rows, ref):
    half = ref.shape[1] // 2
    cols = [jnp.max(ref[rows:, at : at + half].astype(F32)) for at in (0, half)]
    col = jnp.where(lax.axis_index("level") >> 1 == 0, cols[0], cols[1]).astype(jnp.int32)
    return lax.rem(col, GROUP)


def pick_block(place, blocks, out_ref):
    turn = place ^ lax.axis_index("level")
    for at, block in enumerate(blocks):
        @pl.when(turn == at)
        def _(block=block):
            out_ref[...] = block[...]


def pick_even_kernel(rows, named_ref, *refs):
    *blocks, out_ref = refs
    pick_block(named_place(rows, named_ref), blocks, out_ref)


def pick_odd_kernel(rows, pairs, named_refs_count, *refs):
    named_refs, blocks, out_ref = refs[:named_refs_count], refs[named_refs_count:-1], refs[-1]
    leaf_pos = lax.axis_index("leaf")
    pair, side = leaf_pos >> 1, leaf_pos & 1
    places = [named_place(rows, ref) for ref in named_refs]
    if pairs == 4:
        inner = jnp.logical_or(
            jnp.logical_and(pair == 1, side == 1), jnp.logical_and(pair == 2, side == 0)
        )
    else:
        inner = side == 1
    pick_block(jnp.where(inner, places[1], places[0]), blocks, out_ref)


def near_kernel(
    x_ref, mate_ref, across_ref, corner_ref, edge_ref, tiles_ref, w_ref, field0, field1, field2,
    field3, cols_ref, count_ref, acc_ref, field_ref
):
    pos = lax.axis_index("level")
    for turn, part_ref in enumerate((field0, field1, field2, field3)):
        field_ref[part_of(pos ^ turn)] = part_ref[...]
    field = jnp.concatenate([field_ref[part] for part in range(GROUP)], axis=0)
    odd = pos & 1
    inner = jnp.logical_or(pos == 1, pos == 2)
    acc = dot(x_ref[...], tiles_ref[0, 0]) + dot(mate_ref[...], tiles_ref[0, 2 - odd])
    beside = jnp.where(inner, corner_ref[...], edge_ref[...])
    acc = acc + dot(beside, tiles_ref[0, 1 + odd])
    acc_ref[...] = acc + dot_t(field, w_ref[...])
    col = cols_ref[0, SLOT]
    turn = lax.rem(col, GROUP) ^ pos
    here = jnp.logical_and(count_ref[0] > SLOT, col // GROUP == 1)
    for at, block in enumerate((x_ref, mate_ref, across_ref, corner_ref)):
        @pl.when(jnp.logical_and(here, turn == at))
        def _(block=block):
            acc_ref[...] += dot(block[...], tiles_ref[0, SLOT])


def finish_kernel(acc_ref, even_ref, odd_ref, tiles_ref, cols_ref, count_ref, out_ref):
    side = lax.axis_index("leaf") & 1
    group = cols_ref[0, SLOT] // GROUP
    live = jnp.logical_and(count_ref[0] > SLOT, group != 1)
    from_even = (group == 0) == (side == 1)

    @pl.when(jnp.logical_not(live))
    def _():
        out_ref[...] = acc_ref[...].astype(BF16)

    for here, block in ((from_even, even_ref), (jnp.logical_not(from_even), odd_ref)):
        @pl.when(jnp.logical_and(live, here))
        def _(block=block):
            out_ref[...] = (acc_ref[...] + dot(block[...], tiles_ref[0, SLOT])).astype(BF16)


def part_of(pos):
    return 2 * (pos & 1) + (pos >> 1)


def turned(value, turn):
    return lax.ppermute(value, "level", [(i, i ^ turn) for i in range(GROUP)])


def shifted(value, steps):
    count = lax.axis_size("leaf")
    route = [(i, i + steps) for i in range(count) if 0 <= i + steps < count]
    return lax.ppermute(value, "leaf", route)


def swapped(value, distance):
    count = lax.axis_size("leaf")
    return lax.ppermute(value, "leaf", [(i, i ^ 1 << distance) for i in range(count)])


def neighbours(value, odd):
    count = lax.axis_size("leaf")
    route = [(i, i + 1) for i in range(odd, count - 1, 2)]
    return lax.ppermute(value, "leaf", route + [(b, a) for a, b in route])


def upper_field(coef, coupling, transfer, couple_mask):
    leaf_count = lax.axis_size("leaf")
    leaf_pos = lax.axis_index("leaf")
    couplings = []
    levels = range(2, min(coupling.shape[0], leaf_count.bit_length()))
    for lev in levels:
        other = swapped(coef, lev - 1)
        is_upper = (leaf_pos >> lev - 1 & 1) == 1
        total = dot(jnp.where(is_upper, other, coef), transfer[0])
        total = total + dot(jnp.where(is_upper, coef, other), transfer[1])
        coef = total.astype(BF16)
        cluster = leaf_pos >> lev
        coupled = jnp.zeros(coef.shape, F32)
        for pick, offset in enumerate((2, 3)):
            if offset < leaf_count >> lev:
                matrix = coupling[lev, pick]
                ahead = shifted(coef, -(offset << lev))
                behind = shifted(coef, offset << lev)
                ahead_mask = couple_mask[lev, cluster, pick].astype(F32)
                behind_mask = couple_mask[lev, jnp.maximum(cluster - offset, 0), pick].astype(F32)
                coupled = coupled + ahead_mask * dot(ahead, matrix)
                coupled = coupled + behind_mask * dot_t(behind, matrix)
        couplings.append(coupled)
    field = jnp.zeros(coef.shape, F32)
    for lev, coupled in zip(reversed(levels), reversed(couplings)):
        if lev + 1 in levels:
            field = dot_t(field.astype(BF16), transfer[leaf_pos >> lev & 1])
        field = field + coupled
    for lev in (1, 0):
        field = dot_t(field.astype(BF16), transfer[leaf_pos >> lev & 1])
    return field


def per_device(
    points_x, leaf_basis, near_tiles, near_cols, near_count, transfer, coupling, couple_mask
):
    assert lax.axis_size("level") == GROUP
    leaf_count = lax.axis_size("leaf")
    vectors, points = points_x.shape
    rank = leaf_basis.shape[2]
    rows = vectors // GROUP
    bits = GROUP.bit_length() - 1
    block = ((vectors, points), BF16)
    part = ((rows, rank), BF16)
    tailed = ((rows + TAIL, rank), BF16)
    doubled = ((2 * (rows + TAIL), rank), BF16)

    keep, send, w, own_x, transfer_in, coupling_in = call(
        partial(up_kernel, bits), "up",
        [points_x, leaf_basis, transfer, coupling, near_cols], [],
        [doubled, doubled, ((points, rank), BF16), block, (transfer.shape, BF16),
         ((2,) + coupling.shape[1:], BF16)],
        [pltpu.VMEM((points, rank), BF16), pltpu.VMEM((GROUP, rows, rank), BF16),
         pltpu.SMEM(near_cols.shape, jnp.int32), pltpu.SemaphoreType.DMA((5,))],
        pltpu.HBM,
    )
    chip_sum = (keep.astype(F32) + turned(send, 1).astype(F32)).astype(BF16)
    came_half = turned(chip_sum[rows + TAIL :], 2)
    coef = (chip_sum[: rows + TAIL].astype(F32) + came_half.astype(F32)).astype(BF16)
    sent, coef = lax.optimization_barrier((points_x, coef))
    joints = [(GROUP * g - 1, GROUP * g) for g in range(1, leaf_count)]
    edge = lax.ppermute(sent, ("leaf", "level"), joints + [(b, a) for a, b in joints])
    beside = swapped(coef, 0)

    across = turned(points_x, 2)
    mate = turned(points_x, 1)

    active = min(coupling.shape[0], leaf_count.bit_length())
    pairs = leaf_count // 2
    turns = [1, 3, 2] if pairs == 4 else [1, 2, 3, -1, -2, -3]
    clusters = [lev < active and (leaf_count >> lev) > 2 for lev in (0, 1)]
    *pushes, pair_coef = call(
        partial(push_kernel, turns, pairs, clusters), "push",
        [coef, beside, coupling_in, transfer_in], [couple_mask.transpose(0, 2, 1)],
        [tailed] * len(turns) + [part], [pltpu.VMEM((2, rows, rank), BF16)],
    )
    across, pushes = lax.optimization_barrier((across, pushes))
    corner = turned(across, 1)
    edge, mate, corner, pushes[0] = lax.optimization_barrier((edge, mate, corner, pushes[0]))
    held = [own_x, mate, across, corner]
    came = {}
    for turn, push in zip(turns, pushes):
        if pairs == 4:
            came[turn] = lax.ppermute(
                push, "leaf", [(i, i ^ 2 * turn) for i in range(leaf_count)]
            )
        else:
            came[turn] = shifted(push, 2 * turn)
    came = dict(zip(came, lax.optimization_barrier(list(came.values()))))
    field = came[1][:rows].astype(F32)
    for turn in turns[1:]:
        field = field + came[turn][:rows].astype(F32)
    if active > 2 and (leaf_count >> 2) > 2:
        field = field + upper_field(pair_coef, coupling, transfer, couple_mask)
    field = field.astype(BF16)

    (to_even,) = call(partial(pick_even_kernel, rows), "pick_even", [beside] + held, [], [block])
    from_even = neighbours(to_even, 0)
    named = [came[1], came[3 if pairs == 4 else -1]]
    (to_odd,) = call(
        partial(pick_odd_kernel, rows, pairs, len(named)), "pick_odd", named + held, [], [block]
    )
    field, to_odd = lax.optimization_barrier((field, to_odd))
    fields = [field] + [turned(field, turn) for turn in range(1, GROUP)]
    from_odd = neighbours(to_odd, 1)
    (acc,) = call(
        near_kernel, "near", held + [edge, near_tiles, w] + fields, [near_cols, near_count],
        [((vectors, points), F32)], [pltpu.VMEM((GROUP, rows, rank), BF16)],
    )
    (out,) = call(
        finish_kernel, "finish", [acc, from_even, from_odd, near_tiles], [near_cols, near_count],
        [block],
    )
    return out


def solution(mesh):
    in_specs = (
        P(None, ("leaf", "level")),
        P(("leaf", "level"), None, None),
        P(("leaf", "level"), None, None, None),
        P(("leaf", "level"), None),
        P(("leaf", "level")),
        P(),
        P(),
        P(),
    )
    out_specs = P(None, ("leaf", "level"))
    return jax.shard_map(
        per_device, mesh=mesh, in_specs=in_specs, out_specs=out_specs, check_vma=False
    )
```

```python
from functools import partial

import jax
import jax.numpy as jnp
from jax import lax
from jax.experimental import pallas as pl
from jax.experimental.pallas import tpu as pltpu
from jax.sharding import PartitionSpec as P

VMEM_LIMIT = 32 * 1024 * 1024
F32 = jnp.float32
BF16 = jnp.bfloat16
GROUP = 4
SLOT = 3
TAIL = 16


def dot(a, b):
    return jnp.dot(a, b, preferred_element_type=F32)


def dot_t(a, b):
    return lax.dot_general(a, b, (((1,), (1,)), ((), ())), preferred_element_type=F32)


def call(kernel, name, inputs, scalars, outputs, scratch=(), inputs_in=pltpu.VMEM):
    shapes = [jax.ShapeDtypeStruct(shape, dtype) for shape, dtype in outputs]
    return pl.pallas_call(
        kernel,
        out_shape=shapes,
        in_specs=[pl.BlockSpec(memory_space=inputs_in)] * len(inputs)
        + [pl.BlockSpec(memory_space=pltpu.SMEM)] * len(scalars),
        out_specs=[pl.BlockSpec(memory_space=pltpu.VMEM)] * len(outputs),
        scratch_shapes=list(scratch),
        compiler_params=pltpu.CompilerParams(vmem_limit_bytes=VMEM_LIMIT),
        cost_estimate=pl.CostEstimate(flops=0, bytes_accessed=0, transcendentals=0),
        name=name,
    )(*(pltpu.with_memory_space_constraint(a, inputs_in) for a in inputs), *scalars)


def up_kernel(
    bits, x_hbm, basis_hbm, transfer_hbm, coupling_hbm, cols_hbm,
    keep_ref, send_ref, w_ref, x_ref, transfer_ref, coupling_ref, basis_ref, z_ref, cols_ref, sems
):
    pos = lax.axis_index("level")
    chip, core = pos >> 1, pos & 1
    pairs = (
        (basis_hbm.at[0], basis_ref), (transfer_hbm, transfer_ref), (x_hbm, x_ref),
        (coupling_hbm.at[:2], coupling_ref), (cols_hbm, cols_ref),
    )
    copies = [pltpu.make_async_copy(a, b, sems.at[i]) for i, (a, b) in enumerate(pairs)]
    for copy in copies:
        copy.start()
    copies[0].wait()
    copies[1].wait()
    w = basis_ref[...]
    for bit in range(bits):
        w = dot(w, transfer_ref[pos >> bit & 1]).astype(BF16)
    w_ref[...] = w
    copies[2].wait()
    z = dot(x_ref[...], w).astype(BF16)
    rows = z_ref.shape[1]
    for part in range(GROUP):
        z_ref[part] = z[part * rows : (part + 1) * rows]
    copies[4].wait()
    lanes = lax.broadcasted_iota(jnp.int32, (TAIL, z.shape[1]), 1)
    first = lanes < z.shape[1] // 2
    tail = jnp.where(first == (chip == 0), cols_ref[0, SLOT], 0).astype(F32).astype(BF16)
    for at, half in enumerate((chip, 1 - chip)):
        low = at * (rows + TAIL)
        keep_ref[low : low + rows] = z_ref[2 * core + half]
        send_ref[low : low + rows] = z_ref[2 * (1 - core) + half]
        keep_ref[low + rows : low + rows + TAIL] = tail
        send_ref[low + rows : low + rows + TAIL] = jnp.zeros_like(tail)
    copies[3].wait()


def push_kernel(
    turns, pairs, clusters, own_ref, mate_ref, coupling_ref, transfer_ref, mask_ref, *refs
):
    *push_refs, pair_ref, both_ref = refs
    leaf_pos = lax.axis_index("leaf")
    pair, side = leaf_pos >> 1, leaf_pos & 1
    rows = both_ref.shape[1]
    both_ref[side] = own_ref[:rows]
    both_ref[1 - side] = mate_ref[:rows]
    total = dot(both_ref[0], transfer_ref[0]) + dot(both_ref[1], transfer_ref[1])
    pair_ref[...] = total.astype(BF16)

    def term(lev, coef, gap, source, target):
        pick = abs(gap) - 2
        matrix = coupling_ref[lev, pick]
        switch = mask_ref[lev, pick, source if gap > 0 else target].astype(F32)
        return switch * (dot_t(coef, matrix) if gap > 0 else dot(coef, matrix))

    def fill(push_ref, distance, to_side):
        target_pair = pair + distance
        total = None
        if abs(distance) in (2, 3) and clusters[1]:
            coupled = term(1, pair_ref[...], distance, pair, target_pair).astype(BF16)
            total = dot_t(coupled, transfer_ref[to_side])
        for from_side in (0, 1):
            gap = 2 * distance + to_side - from_side
            if abs(gap) in (2, 3) and clusters[0]:
                more = term(
                    0, both_ref[from_side], gap, 2 * pair + from_side, 2 * target_pair + to_side
                )
                total = more if total is None else total + more
        if total is None:
            total = jnp.zeros(pair_ref.shape, F32)
        push_ref[:rows] = total.astype(BF16)

    for turn, push_ref in zip(turns, push_refs):
        push_ref[rows:] = mate_ref[rows:]
        for distance in reached(turn, pairs):
            if pairs == 4:
                inside = (pair ^ turn) == pair + distance
            else:
                inside = jnp.logical_and(pair + distance >= 0, pair + distance < pairs)
            for to_side in (0, 1):
                @pl.when(jnp.logical_and(inside, side == to_side))
                def _(push_ref=push_ref, distance=distance, to_side=to_side):
                    fill(push_ref, distance, to_side)


def reached(turn, pairs):
    return sorted({(i ^ turn) - i for i in range(pairs)}) if pairs == 4 else [turn]


def named_place(rows, ref):
    half = ref.shape[1] // 2
    cols = [jnp.max(ref[rows:, at : at + half].astype(F32)) for at in (0, half)]
    col = jnp.where(lax.axis_index("level") >> 1 == 0, cols[0], cols[1]).astype(jnp.int32)
    return lax.rem(col, GROUP)


def pick_block(place, blocks, out_ref):
    turn = place ^ lax.axis_index("level")
    for at, block in enumerate(blocks):
        @pl.when(turn == at)
        def _(block=block):
            out_ref[...] = block[...]


def pick_even_kernel(rows, named_ref, *refs):
    *blocks, out_ref = refs
    pick_block(named_place(rows, named_ref), blocks, out_ref)


def pick_odd_kernel(rows, pairs, named_refs_count, *refs):
    named_refs, blocks, out_ref = refs[:named_refs_count], refs[named_refs_count:-1], refs[-1]
    leaf_pos = lax.axis_index("leaf")
    pair, side = leaf_pos >> 1, leaf_pos & 1
    places = [named_place(rows, ref) for ref in named_refs]
    if pairs == 4:
        inner = jnp.logical_or(
            jnp.logical_and(pair == 1, side == 1), jnp.logical_and(pair == 2, side == 0)
        )
    else:
        inner = side == 1
    pick_block(jnp.where(inner, places[1], places[0]), blocks, out_ref)


def near_kernel(
    x_ref, mate_ref, across_ref, corner_ref, edge_ref, tiles_ref, w_ref, own_field, mate_field,
    cols_ref, count_ref, acc_ref, field_ref
):
    pos = lax.axis_index("level")
    rows = field_ref.shape[1]
    for flip, came_ref in enumerate((own_field, mate_field)):
        field_ref[part_of(pos ^ flip)] = came_ref[:rows]
        field_ref[part_of(pos ^ flip ^ 2)] = came_ref[rows:]
    field = jnp.concatenate([field_ref[part] for part in range(GROUP)], axis=0)
    odd = pos & 1
    inner = jnp.logical_or(pos == 1, pos == 2)
    acc = dot(x_ref[...], tiles_ref[0, 0]) + dot(mate_ref[...], tiles_ref[0, 2 - odd])
    beside = jnp.where(inner, corner_ref[...], edge_ref[...])
    acc = acc + dot(beside, tiles_ref[0, 1 + odd])
    acc_ref[...] = acc + dot_t(field, w_ref[...])
    col = cols_ref[0, SLOT]
    turn = lax.rem(col, GROUP) ^ pos
    here = jnp.logical_and(count_ref[0] > SLOT, col // GROUP == 1)
    for at, block in enumerate((x_ref, mate_ref, across_ref, corner_ref)):
        @pl.when(jnp.logical_and(here, turn == at))
        def _(block=block):
            acc_ref[...] += dot(block[...], tiles_ref[0, SLOT])


def finish_kernel(acc_ref, even_ref, odd_ref, tiles_ref, cols_ref, count_ref, out_ref):
    side = lax.axis_index("leaf") & 1
    group = cols_ref[0, SLOT] // GROUP
    live = jnp.logical_and(count_ref[0] > SLOT, group != 1)
    from_even = (group == 0) == (side == 1)

    @pl.when(jnp.logical_not(live))
    def _():
        out_ref[...] = acc_ref[...].astype(BF16)

    for here, block in ((from_even, even_ref), (jnp.logical_not(from_even), odd_ref)):
        @pl.when(jnp.logical_and(live, here))
        def _(block=block):
            out_ref[...] = (acc_ref[...] + dot(block[...], tiles_ref[0, SLOT])).astype(BF16)


def part_of(pos):
    return 2 * (pos & 1) + (pos >> 1)


def turned(value, turn):
    return lax.ppermute(value, "level", [(i, i ^ turn) for i in range(GROUP)])


def shifted(value, steps):
    count = lax.axis_size("leaf")
    route = [(i, i + steps) for i in range(count) if 0 <= i + steps < count]
    return lax.ppermute(value, "leaf", route)


def swapped(value, distance):
    count = lax.axis_size("leaf")
    return lax.ppermute(value, "leaf", [(i, i ^ 1 << distance) for i in range(count)])


def neighbours(value, odd):
    count = lax.axis_size("leaf")
    route = [(i, i + 1) for i in range(odd, count - 1, 2)]
    return lax.ppermute(value, "leaf", route + [(b, a) for a, b in route])


def upper_field(coef, coupling, transfer, couple_mask):
    leaf_count = lax.axis_size("leaf")
    leaf_pos = lax.axis_index("leaf")
    couplings = []
    levels = range(2, min(coupling.shape[0], leaf_count.bit_length()))
    for lev in levels:
        other = swapped(coef, lev - 1)
        is_upper = (leaf_pos >> lev - 1 & 1) == 1
        total = dot(jnp.where(is_upper, other, coef), transfer[0])
        total = total + dot(jnp.where(is_upper, coef, other), transfer[1])
        coef = total.astype(BF16)
        cluster = leaf_pos >> lev
        coupled = jnp.zeros(coef.shape, F32)
        for pick, offset in enumerate((2, 3)):
            if offset < leaf_count >> lev:
                matrix = coupling[lev, pick]
                ahead = shifted(coef, -(offset << lev))
                behind = shifted(coef, offset << lev)
                ahead_mask = couple_mask[lev, cluster, pick].astype(F32)
                behind_mask = couple_mask[lev, jnp.maximum(cluster - offset, 0), pick].astype(F32)
                coupled = coupled + ahead_mask * dot(ahead, matrix)
                coupled = coupled + behind_mask * dot_t(behind, matrix)
        couplings.append(coupled)
    field = jnp.zeros(coef.shape, F32)
    for lev, coupled in zip(reversed(levels), reversed(couplings)):
        if lev + 1 in levels:
            field = dot_t(field.astype(BF16), transfer[leaf_pos >> lev & 1])
        field = field + coupled
    for lev in (1, 0):
        field = dot_t(field.astype(BF16), transfer[leaf_pos >> lev & 1])
    return field


def per_device(
    points_x, leaf_basis, near_tiles, near_cols, near_count, transfer, coupling, couple_mask
):
    assert lax.axis_size("level") == GROUP
    leaf_count = lax.axis_size("leaf")
    vectors, points = points_x.shape
    rank = leaf_basis.shape[2]
    rows = vectors // GROUP
    bits = GROUP.bit_length() - 1
    block = ((vectors, points), BF16)
    part = ((rows, rank), BF16)
    tailed = ((rows + TAIL, rank), BF16)
    doubled = ((2 * (rows + TAIL), rank), BF16)

    keep, send, w, own_x, transfer_in, coupling_in = call(
        partial(up_kernel, bits), "up",
        [points_x, leaf_basis, transfer, coupling, near_cols], [],
        [doubled, doubled, ((points, rank), BF16), block, (transfer.shape, BF16),
         ((2,) + coupling.shape[1:], BF16)],
        [pltpu.VMEM((points, rank), BF16), pltpu.VMEM((GROUP, rows, rank), BF16),
         pltpu.SMEM(near_cols.shape, jnp.int32), pltpu.SemaphoreType.DMA((5,))],
        pltpu.HBM,
    )
    chip_sum = (keep.astype(F32) + turned(send, 1).astype(F32)).astype(BF16)
    came_half = turned(chip_sum[rows + TAIL :], 2)
    mate = turned(points_x, 1)
    mate, came_half = lax.optimization_barrier((mate, came_half))
    coef = (chip_sum[: rows + TAIL].astype(F32) + came_half.astype(F32)).astype(BF16)
    sent, coef = lax.optimization_barrier((points_x, coef))
    joints = [(GROUP * g - 1, GROUP * g) for g in range(1, leaf_count)]
    edge = lax.ppermute(sent, ("leaf", "level"), joints + [(b, a) for a, b in joints])
    beside = swapped(coef, 0)

    across = turned(points_x, 2)

    active = min(coupling.shape[0], leaf_count.bit_length())
    pairs = leaf_count // 2
    turns = [2, 1, 3] if pairs == 4 else [2, 1, 3, -1, -2, -3]
    clusters = [lev < active and (leaf_count >> lev) > 2 for lev in (0, 1)]
    *pushes, pair_coef = call(
        partial(push_kernel, turns, pairs, clusters), "push",
        [coef, beside, coupling_in, transfer_in], [couple_mask.transpose(0, 2, 1)],
        [tailed] * len(turns) + [part], [pltpu.VMEM((2, rows, rank), BF16)],
    )
    across, pushes = lax.optimization_barrier((across, pushes))
    corner = turned(across, 1)
    edge, corner, pushes[0] = lax.optimization_barrier((edge, corner, pushes[0]))
    held = [own_x, mate, across, corner]
    came = {}
    for turn, push in zip(turns, pushes):
        if pairs == 4:
            came[turn] = lax.ppermute(
                push, "leaf", [(i, i ^ 2 * turn) for i in range(leaf_count)]
            )
        else:
            came[turn] = shifted(push, 2 * turn)
    field = came[turns[0]][:rows].astype(F32)
    for turn in turns[1:]:
        field = field + came[turn][:rows].astype(F32)
    if active > 2 and (leaf_count >> 2) > 2:
        field = field + upper_field(pair_coef, coupling, transfer, couple_mask)
    field = field.astype(BF16)

    (to_even,) = call(partial(pick_even_kernel, rows), "pick_even", [beside] + held, [], [block])
    from_even = neighbours(to_even, 0)
    named = [came[1], came[3 if pairs == 4 else -1]]
    (to_odd,) = call(
        partial(pick_odd_kernel, rows, pairs, len(named)), "pick_odd", named + held, [], [block]
    )
    field, to_odd = lax.optimization_barrier((field, to_odd))
    chip_field = jnp.concatenate([field, turned(field, 2)])
    fields = [chip_field, turned(chip_field, 1)]
    from_odd = neighbours(to_odd, 1)
    (acc,) = call(
        near_kernel, "near", held + [edge, near_tiles, w] + fields, [near_cols, near_count],
        [((vectors, points), F32)], [pltpu.VMEM((GROUP, rows, rank), BF16)],
    )
    (out,) = call(
        finish_kernel, "finish", [acc, from_even, from_odd, near_tiles], [near_cols, near_count],
        [block],
    )
    return out


def solution(mesh):
    in_specs = (
        P(None, ("leaf", "level")),
        P(("leaf", "level"), None, None),
        P(("leaf", "level"), None, None, None),
        P(("leaf", "level"), None),
        P(("leaf", "level")),
        P(),
        P(),
        P(),
    )
    out_specs = P(None, ("leaf", "level"))
    return jax.shard_map(
        per_device, mesh=mesh, in_specs=in_specs, out_specs=out_specs, check_vma=False
    )
```

```python
from functools import partial

import jax
import jax.numpy as jnp
from jax import lax
from jax.experimental import pallas as pl
from jax.experimental.pallas import tpu as pltpu
from jax.sharding import PartitionSpec as P

VMEM_LIMIT = 32 * 1024 * 1024
F32 = jnp.float32
BF16 = jnp.bfloat16
GROUP = 4
SLOT = 3
TAIL = 16


def dot(a, b):
    return jnp.dot(a, b, preferred_element_type=F32)


def dot_t(a, b):
    return lax.dot_general(a, b, (((1,), (1,)), ((), ())), preferred_element_type=F32)


def call(kernel, name, inputs, scalars, outputs, scratch=(), inputs_in=pltpu.VMEM):
    shapes = [jax.ShapeDtypeStruct(shape, dtype) for shape, dtype in outputs]
    return pl.pallas_call(
        kernel,
        out_shape=shapes,
        in_specs=[pl.BlockSpec(memory_space=inputs_in)] * len(inputs)
        + [pl.BlockSpec(memory_space=pltpu.SMEM)] * len(scalars),
        out_specs=[pl.BlockSpec(memory_space=pltpu.VMEM)] * len(outputs),
        scratch_shapes=list(scratch),
        compiler_params=pltpu.CompilerParams(vmem_limit_bytes=VMEM_LIMIT),
        cost_estimate=pl.CostEstimate(flops=0, bytes_accessed=0, transcendentals=0),
        name=name,
    )(*(pltpu.with_memory_space_constraint(a, inputs_in) for a in inputs), *scalars)


def up_kernel(
    bits, x_hbm, basis_hbm, transfer_hbm, coupling_hbm,
    keep_ref, send_ref, w_ref, x_ref, transfer_ref, coupling_ref, basis_ref, z_ref, sems
):
    pos = lax.axis_index("level")
    chip, core = pos >> 1, pos & 1
    pairs = (
        (basis_hbm.at[0], basis_ref), (transfer_hbm, transfer_ref), (x_hbm, x_ref),
        (coupling_hbm.at[:2], coupling_ref),
    )
    copies = [pltpu.make_async_copy(a, b, sems.at[i]) for i, (a, b) in enumerate(pairs)]
    for copy in copies:
        copy.start()
    copies[0].wait()
    copies[1].wait()
    w = basis_ref[...]
    for bit in range(bits):
        w = dot(w, transfer_ref[pos >> bit & 1]).astype(BF16)
    w_ref[...] = w
    copies[2].wait()
    z = dot(x_ref[...], w).astype(BF16)
    rows = z_ref.shape[1]
    for part in range(GROUP):
        z_ref[part] = z[part * rows : (part + 1) * rows]
    for at, half in enumerate((chip, 1 - chip)):
        keep_ref[at * rows : (at + 1) * rows] = z_ref[2 * core + half]
        send_ref[at * rows : (at + 1) * rows] = z_ref[2 * (1 - core) + half]
    copies[3].wait()


def join_kernel(rows, chip_ref, came_ref, cols_ref, next_ref, out_ref):
    out_ref[:rows] = (chip_ref[:rows].astype(F32) + came_ref[...].astype(F32)).astype(BF16)
    shape = (TAIL, out_ref.shape[1])
    lanes = lax.broadcasted_iota(jnp.int32, shape, 1)
    here, further = (
        jnp.broadcast_to(ref[:, SLOT : SLOT + 1], shape) for ref in (cols_ref, next_ref)
    )
    out_ref[rows:] = jnp.where(lanes < shape[1] // 2, here, further).astype(F32).astype(BF16)


def push_kernel(
    turns, pairs, clusters, own_ref, mate_ref, coupling_ref, transfer_ref, mask_ref, *refs
):
    *push_refs, pair_ref, both_ref = refs
    leaf_pos = lax.axis_index("leaf")
    pair, side = leaf_pos >> 1, leaf_pos & 1
    rows = both_ref.shape[1]
    both_ref[side] = own_ref[:rows]
    both_ref[1 - side] = mate_ref[:rows]
    total = dot(both_ref[0], transfer_ref[0]) + dot(both_ref[1], transfer_ref[1])
    pair_ref[...] = total.astype(BF16)

    def term(lev, coef, gap, source, target):
        pick = abs(gap) - 2
        matrix = coupling_ref[lev, pick]
        switch = mask_ref[lev, pick, source if gap > 0 else target].astype(F32)
        return switch * (dot_t(coef, matrix) if gap > 0 else dot(coef, matrix))

    def fill(push_ref, distance, to_side):
        target_pair = pair + distance
        total = None
        if abs(distance) in (2, 3) and clusters[1]:
            coupled = term(1, pair_ref[...], distance, pair, target_pair).astype(BF16)
            total = dot_t(coupled, transfer_ref[to_side])
        for from_side in (0, 1):
            gap = 2 * distance + to_side - from_side
            if abs(gap) in (2, 3) and clusters[0]:
                more = term(
                    0, both_ref[from_side], gap, 2 * pair + from_side, 2 * target_pair + to_side
                )
                total = more if total is None else total + more
        if total is None:
            total = jnp.zeros(pair_ref.shape, F32)
        push_ref[...] = total.astype(BF16)

    for turn, push_ref in zip(turns, push_refs):
        for distance in reached(turn, pairs):
            if pairs == 4:
                inside = (pair ^ turn) == pair + distance
            else:
                inside = jnp.logical_and(pair + distance >= 0, pair + distance < pairs)
            for to_side in (0, 1):
                @pl.when(jnp.logical_and(inside, side == to_side))
                def _(push_ref=push_ref, distance=distance, to_side=to_side):
                    fill(push_ref, distance, to_side)


def reached(turn, pairs):
    return sorted({(i ^ turn) - i for i in range(pairs)}) if pairs == 4 else [turn]


def pick_kernel(rows, named_ref, *refs):
    *blocks, even_ref, odd_ref = refs
    half = named_ref.shape[1] // 2
    for lane, out_ref in ((0, even_ref), (half, odd_ref)):
        col = jnp.max(named_ref[rows:, lane : lane + half].astype(F32)).astype(jnp.int32)
        turn = lax.rem(col, GROUP) ^ lax.axis_index("level")
        for at, block in enumerate(blocks):
            @pl.when(turn == at)
            def _(block=block, out_ref=out_ref):
                out_ref[...] = block[...]


def near_kernel(
    x_ref, mate_ref, across_ref, corner_ref, edge_ref, tiles_ref, w_ref, own_field, mate_field,
    cols_ref, count_ref, acc_ref, field_ref
):
    pos = lax.axis_index("level")
    rows = field_ref.shape[1]
    for flip, came_ref in enumerate((own_field, mate_field)):
        field_ref[part_of(pos ^ flip)] = came_ref[:rows]
        field_ref[part_of(pos ^ flip ^ 2)] = came_ref[rows:]
    field = jnp.concatenate([field_ref[part] for part in range(GROUP)], axis=0)
    odd = pos & 1
    inner = jnp.logical_or(pos == 1, pos == 2)
    acc = dot(x_ref[...], tiles_ref[0, 0]) + dot(mate_ref[...], tiles_ref[0, 2 - odd])
    beside = jnp.where(inner, corner_ref[...], edge_ref[...])
    acc = acc + dot(beside, tiles_ref[0, 1 + odd])
    acc_ref[...] = acc + dot_t(field, w_ref[...])
    col = cols_ref[0, SLOT]
    turn = lax.rem(col, GROUP) ^ pos
    here = jnp.logical_and(count_ref[0] > SLOT, col // GROUP == 1)
    for at, block in enumerate((x_ref, mate_ref, across_ref, corner_ref)):
        @pl.when(jnp.logical_and(here, turn == at))
        def _(block=block):
            acc_ref[...] += dot(block[...], tiles_ref[0, SLOT])


def finish_kernel(acc_ref, even_ref, odd_ref, tiles_ref, cols_ref, count_ref, out_ref):
    side = lax.axis_index("leaf") & 1
    group = cols_ref[0, SLOT] // GROUP
    live = jnp.logical_and(count_ref[0] > SLOT, group != 1)
    from_even = (group == 0) == (side == 1)

    @pl.when(jnp.logical_not(live))
    def _():
        out_ref[...] = acc_ref[...].astype(BF16)

    for here, block in ((from_even, even_ref), (jnp.logical_not(from_even), odd_ref)):
        @pl.when(jnp.logical_and(live, here))
        def _(block=block):
            out_ref[...] = (acc_ref[...] + dot(block[...], tiles_ref[0, SLOT])).astype(BF16)


def part_of(pos):
    return 2 * (pos & 1) + (pos >> 1)


def turned(value, turn):
    return lax.ppermute(value, "level", [(i, i ^ turn) for i in range(GROUP)])


def shifted(value, steps):
    count = lax.axis_size("leaf")
    route = [(i, i + steps) for i in range(count) if 0 <= i + steps < count]
    return lax.ppermute(value, "leaf", route)


def swapped(value, distance):
    count = lax.axis_size("leaf")
    return lax.ppermute(value, "leaf", [(i, i ^ 1 << distance) for i in range(count)])


def neighbours(value, odd):
    count = lax.axis_size("leaf")
    route = [(i, i + 1) for i in range(odd, count - 1, 2)]
    return lax.ppermute(value, "leaf", route + [(b, a) for a, b in route])


def upper_field(coef, coupling, transfer, couple_mask):
    leaf_count = lax.axis_size("leaf")
    leaf_pos = lax.axis_index("leaf")
    couplings = []
    levels = range(2, min(coupling.shape[0], leaf_count.bit_length()))
    for lev in levels:
        other = swapped(coef, lev - 1)
        is_upper = (leaf_pos >> lev - 1 & 1) == 1
        total = dot(jnp.where(is_upper, other, coef), transfer[0])
        total = total + dot(jnp.where(is_upper, coef, other), transfer[1])
        coef = total.astype(BF16)
        cluster = leaf_pos >> lev
        coupled = jnp.zeros(coef.shape, F32)
        for pick, offset in enumerate((2, 3)):
            if offset < leaf_count >> lev:
                matrix = coupling[lev, pick]
                ahead = shifted(coef, -(offset << lev))
                behind = shifted(coef, offset << lev)
                ahead_mask = couple_mask[lev, cluster, pick].astype(F32)
                behind_mask = couple_mask[lev, jnp.maximum(cluster - offset, 0), pick].astype(F32)
                coupled = coupled + ahead_mask * dot(ahead, matrix)
                coupled = coupled + behind_mask * dot_t(behind, matrix)
        couplings.append(coupled)
    field = jnp.zeros(coef.shape, F32)
    for lev, coupled in zip(reversed(levels), reversed(couplings)):
        if lev + 1 in levels:
            field = dot_t(field.astype(BF16), transfer[leaf_pos >> lev & 1])
        field = field + coupled
    for lev in (1, 0):
        field = dot_t(field.astype(BF16), transfer[leaf_pos >> lev & 1])
    return field


def per_device(
    points_x, leaf_basis, near_tiles, near_cols, near_count, transfer, coupling, couple_mask
):
    assert lax.axis_size("level") == GROUP
    leaf_count = lax.axis_size("leaf")
    vectors, points = points_x.shape
    rank = leaf_basis.shape[2]
    rows = vectors // GROUP
    bits = GROUP.bit_length() - 1
    block = ((vectors, points), BF16)
    part = ((rows, rank), BF16)
    pair_rows = ((2 * rows, rank), BF16)

    keep, send, w, own_x, transfer_in, coupling_in = call(
        partial(up_kernel, bits), "up", [points_x, leaf_basis, transfer, coupling], [],
        [pair_rows, pair_rows, ((points, rank), BF16), block, (transfer.shape, BF16),
         ((2,) + coupling.shape[1:], BF16)],
        [pltpu.VMEM((points, rank), BF16), pltpu.VMEM((GROUP, rows, rank), BF16),
         pltpu.SemaphoreType.DMA((4,))],
        pltpu.HBM,
    )
    chip_sum = (keep.astype(F32) + turned(send, 1).astype(F32)).astype(BF16)
    came_half = turned(chip_sum[rows:], 2)
    mate = turned(points_x, 1)
    hops = [(i, i + (2 if i & 1 else -2)) for i in range(leaf_count)]
    next_cols = lax.ppermute(near_cols, "leaf", [h for h in hops if 0 <= h[1] < leaf_count])
    sent, mate, came_half, next_cols = lax.optimization_barrier(
        (points_x, mate, came_half, next_cols)
    )
    across = turned(sent, 2)
    (tailed,) = call(
        partial(join_kernel, rows), "join", [chip_sum, came_half, near_cols, next_cols], [],
        [((rows + TAIL, rank), BF16)],
    )
    sent, tailed = lax.optimization_barrier((points_x, tailed))
    joints = [(GROUP * g - 1, GROUP * g) for g in range(1, leaf_count)]
    edge = lax.ppermute(sent, ("leaf", "level"), joints + [(b, a) for a, b in joints])
    beside = swapped(tailed, 0)


    active = min(coupling.shape[0], leaf_count.bit_length())
    pairs = leaf_count // 2
    turns = [1, 3, 2] if pairs == 4 else [1, 3, 2, -1, -2, -3]
    clusters = [lev < active and (leaf_count >> lev) > 2 for lev in (0, 1)]
    *pushes, pair_coef = call(
        partial(push_kernel, turns, pairs, clusters), "push",
        [tailed, beside, coupling_in, transfer_in], [couple_mask.transpose(0, 2, 1)],
        [part] * (len(turns) + 1), [pltpu.VMEM((2, rows, rank), BF16)],
    )
    across, pushes = lax.optimization_barrier((across, pushes))
    corner = turned(across, 1)
    edge, corner, pushes[0] = lax.optimization_barrier((edge, corner, pushes[0]))
    held = [own_x, mate, across, corner]
    came = {}
    for turn, push in zip(turns, pushes):
        if pairs == 4:
            came[turn] = lax.ppermute(
                push, "leaf", [(i, i ^ 2 * turn) for i in range(leaf_count)]
            )
        else:
            came[turn] = shifted(push, 2 * turn)
    field = came[turns[0]].astype(F32)
    for turn in turns[1:]:
        field = field + came[turn].astype(F32)
    if active > 2 and (leaf_count >> 2) > 2:
        field = field + upper_field(pair_coef, coupling, transfer, couple_mask)
    field = field.astype(BF16)

    to_even, to_odd = call(partial(pick_kernel, rows), "pick", [beside] + held, [], [block] * 2)
    from_even = neighbours(to_even, 0)
    chip_field = jnp.concatenate([field, turned(field, 2)])
    fields = [chip_field, turned(chip_field, 1)]
    from_odd = neighbours(to_odd, 1)
    (acc,) = call(
        near_kernel, "near", held + [edge, near_tiles, w] + fields, [near_cols, near_count],
        [((vectors, points), F32)], [pltpu.VMEM((GROUP, rows, rank), BF16)],
    )
    (out,) = call(
        finish_kernel, "finish", [acc, from_even, from_odd, near_tiles], [near_cols, near_count],
        [block],
    )
    return out


def solution(mesh):
    in_specs = (
        P(None, ("leaf", "level")),
        P(("leaf", "level"), None, None),
        P(("leaf", "level"), None, None, None),
        P(("leaf", "level"), None),
        P(("leaf", "level")),
        P(),
        P(),
        P(),
    )
    out_specs = P(None, ("leaf", "level"))
    return jax.shard_map(
        per_device, mesh=mesh, in_specs=in_specs, out_specs=out_specs, check_vma=False
    )
```

```python
from functools import partial

import jax
import jax.numpy as jnp
from jax import lax
from jax.experimental import pallas as pl
from jax.experimental.pallas import tpu as pltpu
from jax.sharding import PartitionSpec as P

VMEM_LIMIT = 32 * 1024 * 1024
F32 = jnp.float32
BF16 = jnp.bfloat16
GROUP = 4
SLOT = 3
TAIL = 16


def dot(a, b):
    return jnp.dot(a, b, preferred_element_type=F32)


def dot_t(a, b):
    return lax.dot_general(a, b, (((1,), (1,)), ((), ())), preferred_element_type=F32)


def call(kernel, name, inputs, scalars, outputs, scratch=(), inputs_in=pltpu.VMEM):
    shapes = [jax.ShapeDtypeStruct(shape, dtype) for shape, dtype in outputs]
    return pl.pallas_call(
        kernel,
        out_shape=shapes,
        in_specs=[pl.BlockSpec(memory_space=inputs_in)] * len(inputs)
        + [pl.BlockSpec(memory_space=pltpu.SMEM)] * len(scalars),
        out_specs=[pl.BlockSpec(memory_space=pltpu.VMEM)] * len(outputs),
        scratch_shapes=list(scratch),
        compiler_params=pltpu.CompilerParams(vmem_limit_bytes=VMEM_LIMIT),
        cost_estimate=pl.CostEstimate(flops=0, bytes_accessed=0, transcendentals=0),
        name=name,
    )(*(pltpu.with_memory_space_constraint(a, inputs_in) for a in inputs), *scalars)


def up_kernel(
    bits, x_hbm, basis_hbm, transfer_hbm, coupling_hbm, cols_hbm,
    keep_ref, send_ref, w_ref, x_ref, transfer_ref, coupling_ref, basis_ref, z_ref, cols_ref, sems
):
    pos = lax.axis_index("level")
    chip, core = pos >> 1, pos & 1
    pairs = (
        (basis_hbm.at[0], basis_ref), (transfer_hbm, transfer_ref), (x_hbm, x_ref),
        (coupling_hbm.at[:2], coupling_ref), (cols_hbm, cols_ref),
    )
    copies = [pltpu.make_async_copy(a, b, sems.at[i]) for i, (a, b) in enumerate(pairs)]
    for copy in copies:
        copy.start()
    copies[0].wait()
    copies[1].wait()
    w = basis_ref[...]
    for bit in range(bits):
        w = dot(w, transfer_ref[pos >> bit & 1]).astype(BF16)
    w_ref[...] = w
    copies[2].wait()
    z = dot(x_ref[...], w).astype(BF16)
    rows = z_ref.shape[1]
    for part in range(GROUP):
        z_ref[part] = z[part * rows : (part + 1) * rows]
    copies[4].wait()
    lanes = lax.broadcasted_iota(jnp.int32, (TAIL, z.shape[1]), 1)
    first = lanes < z.shape[1] // 2
    tail = jnp.where(first == (chip == 0), cols_ref[0, SLOT], 0).astype(F32).astype(BF16)
    for at, half in enumerate((chip, 1 - chip)):
        low = at * (rows + TAIL)
        keep_ref[low : low + rows] = z_ref[2 * core + half]
        send_ref[low : low + rows] = z_ref[2 * (1 - core) + half]
        keep_ref[low + rows : low + rows + TAIL] = tail
        send_ref[low + rows : low + rows + TAIL] = jnp.zeros_like(tail)
    copies[3].wait()


def push_kernel(
    turns, pairs, clusters, own_ref, mate_ref, coupling_ref, transfer_ref, mask_ref, *refs
):
    *push_refs, pair_ref, both_ref = refs
    leaf_pos = lax.axis_index("leaf")
    pair, side = leaf_pos >> 1, leaf_pos & 1
    rows = both_ref.shape[1]
    both_ref[side] = own_ref[:rows]
    both_ref[1 - side] = mate_ref[:rows]
    total = dot(both_ref[0], transfer_ref[0]) + dot(both_ref[1], transfer_ref[1])
    pair_ref[...] = total.astype(BF16)

    def term(lev, coef, gap, source, target):
        pick = abs(gap) - 2
        matrix = coupling_ref[lev, pick]
        switch = mask_ref[lev, pick, source if gap > 0 else target].astype(F32)
        return switch * (dot_t(coef, matrix) if gap > 0 else dot(coef, matrix))

    def fill(push_ref, distance, to_side):
        target_pair = pair + distance
        total = None
        if abs(distance) in (2, 3) and clusters[1]:
            coupled = term(1, pair_ref[...], distance, pair, target_pair).astype(BF16)
            total = dot_t(coupled, transfer_ref[to_side])
        for from_side in (0, 1):
            gap = 2 * distance + to_side - from_side
            if abs(gap) in (2, 3) and clusters[0]:
                more = term(
                    0, both_ref[from_side], gap, 2 * pair + from_side, 2 * target_pair + to_side
                )
                total = more if total is None else total + more
        if total is None:
            total = jnp.zeros(pair_ref.shape, F32)
        push_ref[:rows] = total.astype(BF16)

    for turn, push_ref in zip(turns, push_refs):
        push_ref[rows:] = mate_ref[rows:]
        for distance in reached(turn, pairs):
            if pairs == 4:
                inside = (pair ^ turn) == pair + distance
            else:
                inside = jnp.logical_and(pair + distance >= 0, pair + distance < pairs)
            for to_side in (0, 1):
                @pl.when(jnp.logical_and(inside, side == to_side))
                def _(push_ref=push_ref, distance=distance, to_side=to_side):
                    fill(push_ref, distance, to_side)


def reached(turn, pairs):
    return sorted({(i ^ turn) - i for i in range(pairs)}) if pairs == 4 else [turn]


def named_place(rows, ref):
    half = ref.shape[1] // 2
    cols = [jnp.max(ref[rows:, at : at + half].astype(F32)) for at in (0, half)]
    col = jnp.where(lax.axis_index("level") >> 1 == 0, cols[0], cols[1]).astype(jnp.int32)
    return lax.rem(col, GROUP)


def pick_block(place, blocks, out_ref):
    turn = place ^ lax.axis_index("level")
    for at, block in enumerate(blocks):
        @pl.when(turn == at)
        def _(block=block):
            out_ref[...] = block[...]


def pick_even_kernel(rows, named_ref, *refs):
    *blocks, out_ref = refs
    pick_block(named_place(rows, named_ref), blocks, out_ref)


def pick_odd_kernel(rows, pairs, named_refs_count, *refs):
    named_refs, blocks, out_ref = refs[:named_refs_count], refs[named_refs_count:-1], refs[-1]
    leaf_pos = lax.axis_index("leaf")
    pair, side = leaf_pos >> 1, leaf_pos & 1
    places = [named_place(rows, ref) for ref in named_refs]
    if pairs == 4:
        inner = jnp.logical_or(
            jnp.logical_and(pair == 1, side == 1), jnp.logical_and(pair == 2, side == 0)
        )
    else:
        inner = side == 1
    pick_block(jnp.where(inner, places[1], places[0]), blocks, out_ref)


def near_kernel(
    x_ref, mate_ref, across_ref, corner_ref, tiles_ref, w_ref, field0, field1, field2,
    field3, cols_ref, count_ref, acc_ref, field_ref
):
    pos = lax.axis_index("level")
    for turn, part_ref in enumerate((field0, field1, field2, field3)):
        field_ref[part_of(pos ^ turn)] = part_ref[...]
    field = jnp.concatenate([field_ref[part] for part in range(GROUP)], axis=0)
    odd = pos & 1
    acc = dot(x_ref[...], tiles_ref[0, 0]) + dot(mate_ref[...], tiles_ref[0, 2 - odd])
    acc_ref[...] = acc + dot_t(field, w_ref[...])

    @pl.when(is_inner(pos))
    def _():
        acc_ref[...] += dot(corner_ref[...], tiles_ref[0, 1 + odd])

    col = cols_ref[0, SLOT]
    turn = lax.rem(col, GROUP) ^ pos
    here = jnp.logical_and(count_ref[0] > SLOT, col // GROUP == 1)
    for at, block in enumerate((x_ref, mate_ref, across_ref, corner_ref)):
        @pl.when(jnp.logical_and(here, turn == at))
        def _(block=block):
            acc_ref[...] += dot(block[...], tiles_ref[0, SLOT])


def finish_kernel(
    acc_ref, even_ref, odd_ref, edge_ref, tiles_ref, cols_ref, count_ref, out_ref, total_ref
):
    side = lax.axis_index("leaf") & 1
    pos = lax.axis_index("level")
    group = cols_ref[0, SLOT] // GROUP
    live = jnp.logical_and(count_ref[0] > SLOT, group != 1)
    from_even = (group == 0) == (side == 1)

    outer = jnp.logical_not(is_inner(pos))

    @pl.when(outer)
    def _():
        total_ref[...] = acc_ref[...] + dot(edge_ref[...], tiles_ref[0, 1 + (pos & 1)])

    @pl.when(jnp.logical_not(outer))
    def _():
        total_ref[...] = acc_ref[...]

    @pl.when(jnp.logical_not(live))
    def _():
        out_ref[...] = total_ref[...].astype(BF16)

    for here, block in ((from_even, even_ref), (jnp.logical_not(from_even), odd_ref)):
        @pl.when(jnp.logical_and(live, here))
        def _(block=block):
            out_ref[...] = (total_ref[...] + dot(block[...], tiles_ref[0, SLOT])).astype(BF16)


def is_inner(pos):
    return jnp.logical_and(pos > 0, pos < GROUP - 1)


def part_of(pos):
    return 2 * (pos & 1) + (pos >> 1)


def turned(value, turn):
    return lax.ppermute(value, "level", [(i, i ^ turn) for i in range(GROUP)])


def shifted(value, steps):
    count = lax.axis_size("leaf")
    route = [(i, i + steps) for i in range(count) if 0 <= i + steps < count]
    return lax.ppermute(value, "leaf", route)


def swapped(value, distance):
    count = lax.axis_size("leaf")
    return lax.ppermute(value, "leaf", [(i, i ^ 1 << distance) for i in range(count)])


def neighbours(value, odd):
    count = lax.axis_size("leaf")
    route = [(i, i + 1) for i in range(odd, count - 1, 2)]
    return lax.ppermute(value, "leaf", route + [(b, a) for a, b in route])


def upper_field(coef, coupling, transfer, couple_mask):
    leaf_count = lax.axis_size("leaf")
    leaf_pos = lax.axis_index("leaf")
    couplings = []
    levels = range(2, min(coupling.shape[0], leaf_count.bit_length()))
    for lev in levels:
        other = swapped(coef, lev - 1)
        is_upper = (leaf_pos >> lev - 1 & 1) == 1
        total = dot(jnp.where(is_upper, other, coef), transfer[0])
        total = total + dot(jnp.where(is_upper, coef, other), transfer[1])
        coef = total.astype(BF16)
        cluster = leaf_pos >> lev
        coupled = jnp.zeros(coef.shape, F32)
        for pick, offset in enumerate((2, 3)):
            if offset < leaf_count >> lev:
                matrix = coupling[lev, pick]
                ahead = shifted(coef, -(offset << lev))
                behind = shifted(coef, offset << lev)
                ahead_mask = couple_mask[lev, cluster, pick].astype(F32)
                behind_mask = couple_mask[lev, jnp.maximum(cluster - offset, 0), pick].astype(F32)
                coupled = coupled + ahead_mask * dot(ahead, matrix)
                coupled = coupled + behind_mask * dot_t(behind, matrix)
        couplings.append(coupled)
    field = jnp.zeros(coef.shape, F32)
    for lev, coupled in zip(reversed(levels), reversed(couplings)):
        if lev + 1 in levels:
            field = dot_t(field.astype(BF16), transfer[leaf_pos >> lev & 1])
        field = field + coupled
    for lev in (1, 0):
        field = dot_t(field.astype(BF16), transfer[leaf_pos >> lev & 1])
    return field


def per_device(
    points_x, leaf_basis, near_tiles, near_cols, near_count, transfer, coupling, couple_mask
):
    assert lax.axis_size("level") == GROUP
    leaf_count = lax.axis_size("leaf")
    vectors, points = points_x.shape
    rank = leaf_basis.shape[2]
    rows = vectors // GROUP
    bits = GROUP.bit_length() - 1
    block = ((vectors, points), BF16)
    part = ((rows, rank), BF16)
    tailed = ((rows + TAIL, rank), BF16)
    doubled = ((2 * (rows + TAIL), rank), BF16)

    keep, send, w, own_x, transfer_in, coupling_in = call(
        partial(up_kernel, bits), "up",
        [points_x, leaf_basis, transfer, coupling, near_cols], [],
        [doubled, doubled, ((points, rank), BF16), block, (transfer.shape, BF16),
         ((2,) + coupling.shape[1:], BF16)],
        [pltpu.VMEM((points, rank), BF16), pltpu.VMEM((GROUP, rows, rank), BF16),
         pltpu.SMEM(near_cols.shape, jnp.int32), pltpu.SemaphoreType.DMA((5,))],
        pltpu.HBM,
    )
    chip_sum = (keep.astype(F32) + turned(send, 1).astype(F32)).astype(BF16)
    came_half = turned(chip_sum[rows + TAIL :], 2)
    mate = turned(points_x, 1)
    mate, came_half = lax.optimization_barrier((mate, came_half))
    coef = (chip_sum[: rows + TAIL].astype(F32) + came_half.astype(F32)).astype(BF16)
    beside = swapped(coef, 0)

    across = turned(points_x, 2)

    active = min(coupling.shape[0], leaf_count.bit_length())
    pairs = leaf_count // 2
    turns = [1, 3, 2] if pairs == 4 else [1, 2, 3, -1, -2, -3]
    clusters = [lev < active and (leaf_count >> lev) > 2 for lev in (0, 1)]
    *pushes, pair_coef = call(
        partial(push_kernel, turns, pairs, clusters), "push",
        [coef, beside, coupling_in, transfer_in], [couple_mask.transpose(0, 2, 1)],
        [tailed] * len(turns) + [part], [pltpu.VMEM((2, rows, rank), BF16)],
    )
    across, pushes = lax.optimization_barrier((across, pushes))
    corner = turned(across, 1)
    corner, pushes[0] = lax.optimization_barrier((corner, pushes[0]))
    held = [own_x, mate, across, corner]
    came = {}
    for turn, push in zip(turns, pushes):
        if pairs == 4:
            came[turn] = lax.ppermute(
                push, "leaf", [(i, i ^ 2 * turn) for i in range(leaf_count)]
            )
        else:
            came[turn] = shifted(push, 2 * turn)
    came = dict(zip(came, lax.optimization_barrier(list(came.values()))))
    field = came[1][:rows].astype(F32)
    for turn in turns[1:]:
        field = field + came[turn][:rows].astype(F32)
    if active > 2 and (leaf_count >> 2) > 2:
        field = field + upper_field(pair_coef, coupling, transfer, couple_mask)
    field = field.astype(BF16)

    (to_even,) = call(partial(pick_even_kernel, rows), "pick_even", [beside] + held, [], [block])
    from_even = neighbours(to_even, 0)
    named = [came[1], came[3 if pairs == 4 else -1]]
    (to_odd,) = call(
        partial(pick_odd_kernel, rows, pairs, len(named)), "pick_odd", named + held, [], [block]
    )
    sent, field, to_odd = lax.optimization_barrier((points_x, field, to_odd))
    joints = [(GROUP * g - 1, GROUP * g) for g in range(1, leaf_count)]
    edge = lax.ppermute(sent, ("leaf", "level"), joints + [(b, a) for a, b in joints])
    fields = [field] + [turned(field, turn) for turn in range(1, GROUP)]
    from_odd = neighbours(to_odd, 1)
    (acc,) = call(
        near_kernel, "near", held + [near_tiles, w] + fields, [near_cols, near_count],
        [((vectors, points), F32)], [pltpu.VMEM((GROUP, rows, rank), BF16)],
    )
    (out,) = call(
        finish_kernel, "finish", [acc, from_even, from_odd, edge, near_tiles],
        [near_cols, near_count], [block], [pltpu.VMEM((vectors, points), F32)],
    )
    return out


def solution(mesh):
    in_specs = (
        P(None, ("leaf", "level")),
        P(("leaf", "level"), None, None),
        P(("leaf", "level"), None, None, None),
        P(("leaf", "level"), None),
        P(("leaf", "level")),
        P(),
        P(),
        P(),
    )
    out_specs = P(None, ("leaf", "level"))
    return jax.shard_map(
        per_device, mesh=mesh, in_specs=in_specs, out_specs=out_specs, check_vma=False
    )
```

```python
from functools import partial

import jax
import jax.numpy as jnp
from jax import lax
from jax.experimental import pallas as pl
from jax.experimental.pallas import tpu as pltpu
from jax.sharding import PartitionSpec as P

VMEM_LIMIT = 32 * 1024 * 1024
F32 = jnp.float32
BF16 = jnp.bfloat16
GROUP = 4
SLOT = 3
TAIL = 16


def dot(a, b):
    return jnp.dot(a, b, preferred_element_type=F32)


def dot_t(a, b):
    return lax.dot_general(a, b, (((1,), (1,)), ((), ())), preferred_element_type=F32)


def call(kernel, name, inputs, scalars, outputs, scratch=(), inputs_in=pltpu.VMEM):
    shapes = [jax.ShapeDtypeStruct(shape, dtype) for shape, dtype in outputs]
    return pl.pallas_call(
        kernel,
        out_shape=shapes,
        in_specs=[pl.BlockSpec(memory_space=inputs_in)] * len(inputs)
        + [pl.BlockSpec(memory_space=pltpu.SMEM)] * len(scalars),
        out_specs=[pl.BlockSpec(memory_space=pltpu.VMEM)] * len(outputs),
        scratch_shapes=list(scratch),
        compiler_params=pltpu.CompilerParams(vmem_limit_bytes=VMEM_LIMIT),
        cost_estimate=pl.CostEstimate(flops=0, bytes_accessed=0, transcendentals=0),
        name=name,
    )(*(pltpu.with_memory_space_constraint(a, inputs_in) for a in inputs), *scalars)


def up_kernel(
    bits, x_hbm, basis_hbm, transfer_hbm, coupling_hbm, cols_hbm,
    keep_ref, send_ref, w_ref, x_ref, transfer_ref, coupling_ref, basis_ref, z_ref, cols_ref, sems
):
    pos = lax.axis_index("level")
    chip, core = pos >> 1, pos & 1
    pairs = (
        (basis_hbm.at[0], basis_ref), (transfer_hbm, transfer_ref), (x_hbm, x_ref),
        (coupling_hbm.at[:2], coupling_ref), (cols_hbm, cols_ref),
    )
    copies = [pltpu.make_async_copy(a, b, sems.at[i]) for i, (a, b) in enumerate(pairs)]
    for copy in copies:
        copy.start()
    copies[0].wait()
    copies[1].wait()
    w = basis_ref[...]
    for bit in range(bits):
        w = dot(w, transfer_ref[pos >> bit & 1]).astype(BF16)
    w_ref[...] = w
    copies[2].wait()
    z = dot(x_ref[...], w).astype(BF16)
    rows = z_ref.shape[1]
    for part in range(GROUP):
        z_ref[part] = z[part * rows : (part + 1) * rows]
    copies[4].wait()
    lanes = lax.broadcasted_iota(jnp.int32, (TAIL, z.shape[1]), 1)
    first = lanes < z.shape[1] // 2
    tail = jnp.where(first == (chip == 0), cols_ref[0, SLOT], 0).astype(F32).astype(BF16)
    for at, half in enumerate((chip, 1 - chip)):
        low = at * (rows + TAIL)
        keep_ref[low : low + rows] = z_ref[2 * core + half]
        send_ref[low : low + rows] = z_ref[2 * (1 - core) + half]
        keep_ref[low + rows : low + rows + TAIL] = tail
        send_ref[low + rows : low + rows + TAIL] = jnp.zeros_like(tail)
    copies[3].wait()


def fold_kernel(turns, pairs, clusters, coupling_ref, transfer_ref, mask_ref, *fold_refs):
    leaf_pos = lax.axis_index("leaf")
    pair, side = leaf_pos >> 1, leaf_pos & 1

    def switch(lev, gap, source, target):
        return mask_ref[lev, abs(gap) - 2, source if gap > 0 else target].astype(F32)

    def fill(fold_ref, distance, to_side):
        other = pair + distance
        through = None
        if abs(distance) in (2, 3) and clusters[1]:
            matrix = coupling_ref[1, abs(distance) - 2]
            on = switch(1, distance, pair, other)
            if distance > 0:
                through = dot(transfer_ref[to_side], matrix)
            else:
                through = dot_t(matrix, transfer_ref[to_side])
            through = (on * through).astype(BF16)
        for from_side in (0, 1):
            total = jnp.zeros(fold_ref.shape[1:], F32)
            if through is not None:
                product = dot_t if distance > 0 else dot
                total = product(transfer_ref[from_side], through)
            gap = 2 * distance + to_side - from_side
            if abs(gap) in (2, 3) and clusters[0]:
                matrix = coupling_ref[0, abs(gap) - 2].astype(F32)
                on = switch(0, gap, 2 * pair + from_side, 2 * other + to_side)
                total = total + on * (matrix.T if gap > 0 else matrix)
            fold_ref[from_side] = total.astype(BF16)

    for turn, fold_ref in zip(turns, fold_refs):
        for distance in reached(turn, pairs):
            if pairs == 4:
                inside = (pair ^ turn) == pair + distance
            else:
                inside = jnp.logical_and(pair + distance >= 0, pair + distance < pairs)
            for to_side in (0, 1):
                @pl.when(jnp.logical_and(inside, side == to_side))
                def _(fold_ref=fold_ref, distance=distance, to_side=to_side):
                    fill(fold_ref, distance, to_side)


def push_kernel(rows, count, own_ref, mate_ref, *refs):
    fold_refs, push_refs = refs[:count], refs[count:]
    side = lax.axis_index("leaf") & 1
    for fold_ref, push_ref in zip(fold_refs, push_refs):
        total = dot(own_ref[:rows], fold_ref[side]) + dot(mate_ref[:rows], fold_ref[1 - side])
        push_ref[:rows] = total.astype(BF16)
        push_ref[rows:] = mate_ref[rows:]


def reached(turn, pairs):
    return sorted({(i ^ turn) - i for i in range(pairs)}) if pairs == 4 else [turn]


def named_place(rows, ref):
    half = ref.shape[1] // 2
    cols = [jnp.max(ref[rows:, at : at + half].astype(F32)) for at in (0, half)]
    col = jnp.where(lax.axis_index("level") >> 1 == 0, cols[0], cols[1]).astype(jnp.int32)
    return lax.rem(col, GROUP)


def pick_block(place, blocks, out_ref):
    turn = place ^ lax.axis_index("level")
    for at, block in enumerate(blocks):
        @pl.when(turn == at)
        def _(block=block):
            out_ref[...] = block[...]


def pick_even_kernel(rows, named_ref, *refs):
    *blocks, out_ref = refs
    pick_block(named_place(rows, named_ref), blocks, out_ref)


def pick_odd_kernel(rows, pairs, named_refs_count, *refs):
    named_refs, blocks, out_ref = refs[:named_refs_count], refs[named_refs_count:-1], refs[-1]
    leaf_pos = lax.axis_index("leaf")
    pair, side = leaf_pos >> 1, leaf_pos & 1
    places = [named_place(rows, ref) for ref in named_refs]
    if pairs == 4:
        inner = jnp.logical_or(
            jnp.logical_and(pair == 1, side == 1), jnp.logical_and(pair == 2, side == 0)
        )
    else:
        inner = side == 1
    pick_block(jnp.where(inner, places[1], places[0]), blocks, out_ref)


def near_kernel(
    x_ref, mate_ref, across_ref, corner_ref, edge_ref, tiles_ref, w_ref, field0, field1, field2,
    field3, cols_ref, count_ref, acc_ref, field_ref
):
    pos = lax.axis_index("level")
    for turn, part_ref in enumerate((field0, field1, field2, field3)):
        field_ref[part_of(pos ^ turn)] = part_ref[...]
    field = jnp.concatenate([field_ref[part] for part in range(GROUP)], axis=0)
    odd = pos & 1
    inner = jnp.logical_or(pos == 1, pos == 2)
    acc = dot(x_ref[...], tiles_ref[0, 0]) + dot(mate_ref[...], tiles_ref[0, 2 - odd])
    beside = jnp.where(inner, corner_ref[...], edge_ref[...])
    acc = acc + dot(beside, tiles_ref[0, 1 + odd])
    acc_ref[...] = acc + dot_t(field, w_ref[...])
    col = cols_ref[0, SLOT]
    turn = lax.rem(col, GROUP) ^ pos
    here = jnp.logical_and(count_ref[0] > SLOT, col // GROUP == 1)
    for at, block in enumerate((x_ref, mate_ref, across_ref, corner_ref)):
        @pl.when(jnp.logical_and(here, turn == at))
        def _(block=block):
            acc_ref[...] += dot(block[...], tiles_ref[0, SLOT])


def finish_kernel(acc_ref, even_ref, odd_ref, tiles_ref, cols_ref, count_ref, out_ref):
    side = lax.axis_index("leaf") & 1
    group = cols_ref[0, SLOT] // GROUP
    live = jnp.logical_and(count_ref[0] > SLOT, group != 1)
    from_even = (group == 0) == (side == 1)

    @pl.when(jnp.logical_not(live))
    def _():
        out_ref[...] = acc_ref[...].astype(BF16)

    for here, block in ((from_even, even_ref), (jnp.logical_not(from_even), odd_ref)):
        @pl.when(jnp.logical_and(live, here))
        def _(block=block):
            out_ref[...] = (acc_ref[...] + dot(block[...], tiles_ref[0, SLOT])).astype(BF16)


def part_of(pos):
    return 2 * (pos & 1) + (pos >> 1)


def turned(value, turn):
    return lax.ppermute(value, "level", [(i, i ^ turn) for i in range(GROUP)])


def shifted(value, steps):
    count = lax.axis_size("leaf")
    route = [(i, i + steps) for i in range(count) if 0 <= i + steps < count]
    return lax.ppermute(value, "leaf", route)


def swapped(value, distance):
    count = lax.axis_size("leaf")
    return lax.ppermute(value, "leaf", [(i, i ^ 1 << distance) for i in range(count)])


def neighbours(value, odd):
    count = lax.axis_size("leaf")
    route = [(i, i + 1) for i in range(odd, count - 1, 2)]
    return lax.ppermute(value, "leaf", route + [(b, a) for a, b in route])


def upper_field(coef, coupling, transfer, couple_mask):
    leaf_count = lax.axis_size("leaf")
    leaf_pos = lax.axis_index("leaf")
    couplings = []
    levels = range(2, min(coupling.shape[0], leaf_count.bit_length()))
    for lev in range(1, levels.stop):
        other = swapped(coef, lev - 1)
        is_upper = (leaf_pos >> lev - 1 & 1) == 1
        total = dot(jnp.where(is_upper, other, coef), transfer[0])
        total = total + dot(jnp.where(is_upper, coef, other), transfer[1])
        coef = total.astype(BF16)
        if lev not in levels:
            continue
        cluster = leaf_pos >> lev
        coupled = jnp.zeros(coef.shape, F32)
        for pick, offset in enumerate((2, 3)):
            if offset < leaf_count >> lev:
                matrix = coupling[lev, pick]
                ahead = shifted(coef, -(offset << lev))
                behind = shifted(coef, offset << lev)
                ahead_mask = couple_mask[lev, cluster, pick].astype(F32)
                behind_mask = couple_mask[lev, jnp.maximum(cluster - offset, 0), pick].astype(F32)
                coupled = coupled + ahead_mask * dot(ahead, matrix)
                coupled = coupled + behind_mask * dot_t(behind, matrix)
        couplings.append(coupled)
    field = jnp.zeros(coef.shape, F32)
    for lev, coupled in zip(reversed(levels), reversed(couplings)):
        if lev + 1 in levels:
            field = dot_t(field.astype(BF16), transfer[leaf_pos >> lev & 1])
        field = field + coupled
    for lev in (1, 0):
        field = dot_t(field.astype(BF16), transfer[leaf_pos >> lev & 1])
    return field


def per_device(
    points_x, leaf_basis, near_tiles, near_cols, near_count, transfer, coupling, couple_mask
):
    assert lax.axis_size("level") == GROUP
    leaf_count = lax.axis_size("leaf")
    vectors, points = points_x.shape
    rank = leaf_basis.shape[2]
    rows = vectors // GROUP
    bits = GROUP.bit_length() - 1
    block = ((vectors, points), BF16)
    part = ((rows, rank), BF16)
    tailed = ((rows + TAIL, rank), BF16)
    doubled = ((2 * (rows + TAIL), rank), BF16)

    keep, send, w, own_x, transfer_in, coupling_in = call(
        partial(up_kernel, bits), "up",
        [points_x, leaf_basis, transfer, coupling, near_cols], [],
        [doubled, doubled, ((points, rank), BF16), block, (transfer.shape, BF16),
         ((2,) + coupling.shape[1:], BF16)],
        [pltpu.VMEM((points, rank), BF16), pltpu.VMEM((GROUP, rows, rank), BF16),
         pltpu.SMEM(near_cols.shape, jnp.int32), pltpu.SemaphoreType.DMA((5,))],
        pltpu.HBM,
    )
    chip_sum = (keep.astype(F32) + turned(send, 1).astype(F32)).astype(BF16)
    came_half = turned(chip_sum[rows + TAIL :], 2)
    mate = turned(points_x, 1)
    active = min(coupling.shape[0], leaf_count.bit_length())
    pairs = leaf_count // 2
    turns = [2, 1, 3] if pairs == 4 else [2, 1, 3, -1, -2, -3]
    clusters = [lev < active and (leaf_count >> lev) > 2 for lev in (0, 1)]
    folds = call(
        partial(fold_kernel, turns, pairs, clusters), "fold", [coupling_in, transfer_in],
        [couple_mask.transpose(0, 2, 1)], [((2, rank, rank), BF16)] * len(turns),
    )
    mate, came_half, folds = lax.optimization_barrier((mate, came_half, folds))
    coef = (chip_sum[: rows + TAIL].astype(F32) + came_half.astype(F32)).astype(BF16)
    sent, coef = lax.optimization_barrier((points_x, coef))
    joints = [(GROUP * g - 1, GROUP * g) for g in range(1, leaf_count)]
    edge = lax.ppermute(sent, ("leaf", "level"), joints + [(b, a) for a, b in joints])
    beside = swapped(coef, 0)

    across = turned(points_x, 2)

    pushes = call(
        partial(push_kernel, rows, len(turns)), "push", [coef, beside, *folds], [],
        [tailed] * len(turns),
    )
    pushes = list(pushes)
    across, pushes = lax.optimization_barrier((across, pushes))
    corner = turned(across, 1)
    edge, corner, pushes[0] = lax.optimization_barrier((edge, corner, pushes[0]))
    held = [own_x, mate, across, corner]
    came = {}
    for turn, push in zip(turns, pushes):
        if pairs == 4:
            came[turn] = lax.ppermute(
                push, "leaf", [(i, i ^ 2 * turn) for i in range(leaf_count)]
            )
        else:
            came[turn] = shifted(push, 2 * turn)
    field = came[turns[0]][:rows].astype(F32)
    for turn in turns[1:]:
        field = field + came[turn][:rows].astype(F32)
    if active > 2 and (leaf_count >> 2) > 2:
        field = field + upper_field(coef[:rows], coupling, transfer, couple_mask)
    field = field.astype(BF16)

    (to_even,) = call(partial(pick_even_kernel, rows), "pick_even", [beside] + held, [], [block])
    from_even = neighbours(to_even, 0)
    named = [came[1], came[3 if pairs == 4 else -1]]
    (to_odd,) = call(
        partial(pick_odd_kernel, rows, pairs, len(named)), "pick_odd", named + held, [], [block]
    )
    field, to_odd = lax.optimization_barrier((field, to_odd))
    fields = [field] + [turned(field, turn) for turn in range(1, GROUP)]
    from_odd = neighbours(to_odd, 1)
    (acc,) = call(
        near_kernel, "near", held + [edge, near_tiles, w] + fields, [near_cols, near_count],
        [((vectors, points), F32)], [pltpu.VMEM((GROUP, rows, rank), BF16)],
    )
    (out,) = call(
        finish_kernel, "finish", [acc, from_even, from_odd, near_tiles], [near_cols, near_count],
        [block],
    )
    return out


def solution(mesh):
    in_specs = (
        P(None, ("leaf", "level")),
        P(("leaf", "level"), None, None),
        P(("leaf", "level"), None, None, None),
        P(("leaf", "level"), None),
        P(("leaf", "level")),
        P(),
        P(),
        P(),
    )
    out_specs = P(None, ("leaf", "level"))
    return jax.shard_map(
        per_device, mesh=mesh, in_specs=in_specs, out_specs=out_specs, check_vma=False
    )
```

```python
from functools import partial

import jax
import jax.numpy as jnp
from jax import lax
from jax.experimental import pallas as pl
from jax.experimental.pallas import tpu as pltpu
from jax.sharding import PartitionSpec as P

VMEM_LIMIT = 32 * 1024 * 1024
F32 = jnp.float32
BF16 = jnp.bfloat16
GROUP = 4
SLOT = 3
TAIL = 16


def dot(a, b):
    return jnp.dot(a, b, preferred_element_type=F32)


def dot_t(a, b):
    return lax.dot_general(a, b, (((1,), (1,)), ((), ())), preferred_element_type=F32)


def call(kernel, name, inputs, scalars, outputs, scratch=(), inputs_in=pltpu.VMEM):
    shapes = [jax.ShapeDtypeStruct(shape, dtype) for shape, dtype in outputs]
    return pl.pallas_call(
        kernel,
        out_shape=shapes,
        in_specs=[pl.BlockSpec(memory_space=inputs_in)] * len(inputs)
        + [pl.BlockSpec(memory_space=pltpu.SMEM)] * len(scalars),
        out_specs=[pl.BlockSpec(memory_space=pltpu.VMEM)] * len(outputs),
        scratch_shapes=list(scratch),
        compiler_params=pltpu.CompilerParams(vmem_limit_bytes=VMEM_LIMIT),
        cost_estimate=pl.CostEstimate(flops=0, bytes_accessed=0, transcendentals=0),
        name=name,
    )(*(pltpu.with_memory_space_constraint(a, inputs_in) for a in inputs), *scalars)


def up_kernel(
    bits, x_hbm, basis_hbm, transfer_hbm, coupling_hbm, cols_hbm,
    keep_ref, send_ref, w_ref, x_ref, transfer_ref, coupling_ref, basis_ref, z_ref, cols_ref, sems
):
    pos = lax.axis_index("level")
    chip, core = pos >> 1, pos & 1
    pairs = (
        (basis_hbm.at[0], basis_ref), (transfer_hbm, transfer_ref), (x_hbm, x_ref),
        (coupling_hbm.at[:2], coupling_ref), (cols_hbm, cols_ref),
    )
    copies = [pltpu.make_async_copy(a, b, sems.at[i]) for i, (a, b) in enumerate(pairs)]
    for copy in copies:
        copy.start()
    copies[0].wait()
    copies[1].wait()
    w = basis_ref[...]
    for bit in range(bits):
        w = dot(w, transfer_ref[pos >> bit & 1]).astype(BF16)
    w_ref[...] = w
    copies[2].wait()
    z = dot(x_ref[...], w).astype(BF16)
    rows = z_ref.shape[1]
    for part in range(GROUP):
        z_ref[part] = z[part * rows : (part + 1) * rows]
    copies[4].wait()
    lanes = lax.broadcasted_iota(jnp.int32, (TAIL, z.shape[1]), 1)
    first = lanes < z.shape[1] // 2
    tail = jnp.where(first == (chip == 0), cols_ref[0, SLOT], 0).astype(F32).astype(BF16)
    for at, half in enumerate((chip, 1 - chip)):
        low = at * (rows + TAIL)
        keep_ref[low : low + rows] = z_ref[2 * core + half]
        send_ref[low : low + rows] = z_ref[2 * (1 - core) + half]
        keep_ref[low + rows : low + rows + TAIL] = tail
        send_ref[low + rows : low + rows + TAIL] = jnp.zeros_like(tail)
    copies[3].wait()


def fold_kernel(turns, pairs, clusters, coupling_ref, transfer_ref, mask_ref, *fold_refs):
    leaf_pos = lax.axis_index("leaf")
    pair, side = leaf_pos >> 1, leaf_pos & 1

    def switch(lev, gap, source, target):
        return mask_ref[lev, abs(gap) - 2, source if gap > 0 else target].astype(F32)

    def fill(fold_ref, distance, to_side):
        other = pair + distance
        through = None
        if abs(distance) in (2, 3) and clusters[1]:
            matrix = coupling_ref[1, abs(distance) - 2]
            on = switch(1, distance, pair, other)
            if distance > 0:
                through = dot(transfer_ref[to_side], matrix)
            else:
                through = dot_t(matrix, transfer_ref[to_side])
            through = (on * through).astype(BF16)
        for from_side in (0, 1):
            total = jnp.zeros(fold_ref.shape[1:], F32)
            if through is not None:
                product = dot_t if distance > 0 else dot
                total = product(transfer_ref[from_side], through)
            gap = 2 * distance + to_side - from_side
            if abs(gap) in (2, 3) and clusters[0]:
                matrix = coupling_ref[0, abs(gap) - 2].astype(F32)
                on = switch(0, gap, 2 * pair + from_side, 2 * other + to_side)
                total = total + on * (matrix.T if gap > 0 else matrix)
            fold_ref[from_side] = total.astype(BF16)

    for turn, fold_ref in zip(turns, fold_refs):
        for distance in reached(turn, pairs):
            if pairs == 4:
                inside = (pair ^ turn) == pair + distance
            else:
                inside = jnp.logical_and(pair + distance >= 0, pair + distance < pairs)
            for to_side in (0, 1):
                @pl.when(jnp.logical_and(inside, side == to_side))
                def _(fold_ref=fold_ref, distance=distance, to_side=to_side):
                    fill(fold_ref, distance, to_side)


def push_kernel(rows, count, own_ref, mate_ref, *refs):
    fold_refs, push_refs = refs[:count], refs[count:]
    side = lax.axis_index("leaf") & 1
    for fold_ref, push_ref in zip(fold_refs, push_refs):
        total = dot(own_ref[:rows], fold_ref[side]) + dot(mate_ref[:rows], fold_ref[1 - side])
        push_ref[:rows] = total.astype(BF16)
        push_ref[rows:] = mate_ref[rows:]


def reached(turn, pairs):
    return sorted({(i ^ turn) - i for i in range(pairs)}) if pairs == 4 else [turn]


def named_place(rows, ref):
    half = ref.shape[1] // 2
    cols = [jnp.max(ref[rows:, at : at + half].astype(F32)) for at in (0, half)]
    col = jnp.where(lax.axis_index("level") >> 1 == 0, cols[0], cols[1]).astype(jnp.int32)
    return lax.rem(col, GROUP)


def pick_block(place, blocks, out_ref):
    turn = place ^ lax.axis_index("level")
    for at, block in enumerate(blocks):
        @pl.when(turn == at)
        def _(block=block):
            out_ref[...] = block[...]


def pick_even_kernel(rows, named_ref, *refs):
    *blocks, out_ref = refs
    pick_block(named_place(rows, named_ref), blocks, out_ref)


def pick_odd_kernel(rows, pairs, named_refs_count, *refs):
    named_refs, blocks, out_ref = refs[:named_refs_count], refs[named_refs_count:-1], refs[-1]
    leaf_pos = lax.axis_index("leaf")
    pair, side = leaf_pos >> 1, leaf_pos & 1
    places = [named_place(rows, ref) for ref in named_refs]
    if pairs == 4:
        inner = jnp.logical_or(
            jnp.logical_and(pair == 1, side == 1), jnp.logical_and(pair == 2, side == 0)
        )
    else:
        inner = side == 1
    pick_block(jnp.where(inner, places[1], places[0]), blocks, out_ref)


def near_kernel(
    x_ref, mate_ref, across_ref, corner_ref, edge_ref, tiles_ref, cols_ref, count_ref, acc_ref
):
    pos = lax.axis_index("level")
    odd = pos & 1
    inner = jnp.logical_or(pos == 1, pos == 2)
    acc = dot(x_ref[...], tiles_ref[0, 0]) + dot(mate_ref[...], tiles_ref[0, 2 - odd])
    beside = jnp.where(inner, corner_ref[...], edge_ref[...])
    acc_ref[...] = acc + dot(beside, tiles_ref[0, 1 + odd])
    col = cols_ref[0, SLOT]
    turn = lax.rem(col, GROUP) ^ pos
    here = jnp.logical_and(count_ref[0] > SLOT, col // GROUP == 1)
    for at, block in enumerate((x_ref, mate_ref, across_ref, corner_ref)):
        @pl.when(jnp.logical_and(here, turn == at))
        def _(block=block):
            acc_ref[...] += dot(block[...], tiles_ref[0, SLOT])


def finish_kernel(
    acc_ref, even_ref, odd_ref, tiles_ref, w_ref, field0, field1, field2, field3,
    cols_ref, count_ref, out_ref, total_ref, field_ref
):
    pos = lax.axis_index("level")
    side = lax.axis_index("leaf") & 1
    for turn, part_ref in enumerate((field0, field1, field2, field3)):
        field_ref[part_of(pos ^ turn)] = part_ref[...]
    field = jnp.concatenate([field_ref[part] for part in range(GROUP)], axis=0)
    group = cols_ref[0, SLOT] // GROUP
    live = jnp.logical_and(count_ref[0] > SLOT, group != 1)
    from_even = (group == 0) == (side == 1)
    total = acc_ref[...] + dot_t(field, w_ref[...])

    @pl.when(jnp.logical_not(live))
    def _():
        out_ref[...] = total.astype(BF16)

    @pl.when(live)
    def _():
        total_ref[...] = total

    for here, block in ((from_even, even_ref), (jnp.logical_not(from_even), odd_ref)):
        @pl.when(jnp.logical_and(live, here))
        def _(block=block):
            out_ref[...] = (total_ref[...] + dot(block[...], tiles_ref[0, SLOT])).astype(BF16)


def part_of(pos):
    return 2 * (pos & 1) + (pos >> 1)


def turned(value, turn):
    return lax.ppermute(value, "level", [(i, i ^ turn) for i in range(GROUP)])


def shifted(value, steps):
    count = lax.axis_size("leaf")
    route = [(i, i + steps) for i in range(count) if 0 <= i + steps < count]
    return lax.ppermute(value, "leaf", route)


def swapped(value, distance):
    count = lax.axis_size("leaf")
    return lax.ppermute(value, "leaf", [(i, i ^ 1 << distance) for i in range(count)])


def neighbours(value, odd):
    count = lax.axis_size("leaf")
    route = [(i, i + 1) for i in range(odd, count - 1, 2)]
    return lax.ppermute(value, "leaf", route + [(b, a) for a, b in route])


def upper_field(coef, coupling, transfer, couple_mask):
    leaf_count = lax.axis_size("leaf")
    leaf_pos = lax.axis_index("leaf")
    couplings = []
    levels = range(2, min(coupling.shape[0], leaf_count.bit_length()))
    for lev in range(1, levels.stop):
        other = swapped(coef, lev - 1)
        is_upper = (leaf_pos >> lev - 1 & 1) == 1
        total = dot(jnp.where(is_upper, other, coef), transfer[0])
        total = total + dot(jnp.where(is_upper, coef, other), transfer[1])
        coef = total.astype(BF16)
        if lev not in levels:
            continue
        cluster = leaf_pos >> lev
        coupled = jnp.zeros(coef.shape, F32)
        for pick, offset in enumerate((2, 3)):
            if offset < leaf_count >> lev:
                matrix = coupling[lev, pick]
                ahead = shifted(coef, -(offset << lev))
                behind = shifted(coef, offset << lev)
                ahead_mask = couple_mask[lev, cluster, pick].astype(F32)
                behind_mask = couple_mask[lev, jnp.maximum(cluster - offset, 0), pick].astype(F32)
                coupled = coupled + ahead_mask * dot(ahead, matrix)
                coupled = coupled + behind_mask * dot_t(behind, matrix)
        couplings.append(coupled)
    field = jnp.zeros(coef.shape, F32)
    for lev, coupled in zip(reversed(levels), reversed(couplings)):
        if lev + 1 in levels:
            field = dot_t(field.astype(BF16), transfer[leaf_pos >> lev & 1])
        field = field + coupled
    for lev in (1, 0):
        field = dot_t(field.astype(BF16), transfer[leaf_pos >> lev & 1])
    return field


def per_device(
    points_x, leaf_basis, near_tiles, near_cols, near_count, transfer, coupling, couple_mask
):
    assert lax.axis_size("level") == GROUP
    leaf_count = lax.axis_size("leaf")
    vectors, points = points_x.shape
    rank = leaf_basis.shape[2]
    rows = vectors // GROUP
    bits = GROUP.bit_length() - 1
    block = ((vectors, points), BF16)
    part = ((rows, rank), BF16)
    tailed = ((rows + TAIL, rank), BF16)
    doubled = ((2 * (rows + TAIL), rank), BF16)

    keep, send, w, own_x, transfer_in, coupling_in = call(
        partial(up_kernel, bits), "up",
        [points_x, leaf_basis, transfer, coupling, near_cols], [],
        [doubled, doubled, ((points, rank), BF16), block, (transfer.shape, BF16),
         ((2,) + coupling.shape[1:], BF16)],
        [pltpu.VMEM((points, rank), BF16), pltpu.VMEM((GROUP, rows, rank), BF16),
         pltpu.SMEM(near_cols.shape, jnp.int32), pltpu.SemaphoreType.DMA((5,))],
        pltpu.HBM,
    )
    chip_sum = (keep.astype(F32) + turned(send, 1).astype(F32)).astype(BF16)
    came_half = turned(chip_sum[rows + TAIL :], 2)
    mate = turned(points_x, 1)
    active = min(coupling.shape[0], leaf_count.bit_length())
    pairs = leaf_count // 2
    turns = [2, 1, 3] if pairs == 4 else [2, 1, 3, -1, -2, -3]
    clusters = [lev < active and (leaf_count >> lev) > 2 for lev in (0, 1)]
    folds = call(
        partial(fold_kernel, turns, pairs, clusters), "fold", [coupling_in, transfer_in],
        [couple_mask.transpose(0, 2, 1)], [((2, rank, rank), BF16)] * len(turns),
    )
    mate, came_half, folds = lax.optimization_barrier((mate, came_half, folds))
    coef = (chip_sum[: rows + TAIL].astype(F32) + came_half.astype(F32)).astype(BF16)
    sent, coef = lax.optimization_barrier((points_x, coef))
    joints = [(GROUP * g - 1, GROUP * g) for g in range(1, leaf_count)]
    edge = lax.ppermute(sent, ("leaf", "level"), joints + [(b, a) for a, b in joints])
    beside = swapped(coef, 0)

    across = turned(points_x, 2)

    pushes = call(
        partial(push_kernel, rows, len(turns)), "push", [coef, beside, *folds], [],
        [tailed] * len(turns),
    )
    pushes = list(pushes)
    across, pushes = lax.optimization_barrier((across, pushes))
    corner = turned(across, 1)
    edge, corner, pushes[0] = lax.optimization_barrier((edge, corner, pushes[0]))
    held = [own_x, mate, across, corner]
    came = {}
    for turn, push in zip(turns, pushes):
        if pairs == 4:
            came[turn] = lax.ppermute(
                push, "leaf", [(i, i ^ 2 * turn) for i in range(leaf_count)]
            )
        else:
            came[turn] = shifted(push, 2 * turn)
    field = came[turns[0]][:rows].astype(F32)
    for turn in turns[1:]:
        field = field + came[turn][:rows].astype(F32)
    if active > 2 and (leaf_count >> 2) > 2:
        field = field + upper_field(coef[:rows], coupling, transfer, couple_mask)
    field = field.astype(BF16)

    (to_even,) = call(partial(pick_even_kernel, rows), "pick_even", [beside] + held, [], [block])
    from_even = neighbours(to_even, 0)
    named = [came[1], came[3 if pairs == 4 else -1]]
    (to_odd,) = call(
        partial(pick_odd_kernel, rows, pairs, len(named)), "pick_odd", named + held, [], [block]
    )
    (acc,) = call(
        near_kernel, "near", held + [edge, near_tiles], [near_cols, near_count],
        [((vectors, points), F32)],
    )
    field, to_odd, acc = lax.optimization_barrier((field, to_odd, acc))
    fields = [field] + [turned(field, turn) for turn in range(1, GROUP)]
    from_odd = neighbours(to_odd, 1)
    (out,) = call(
        finish_kernel, "finish", [acc, from_even, from_odd, near_tiles, w] + fields,
        [near_cols, near_count], [block],
        [pltpu.VMEM((vectors, points), F32), pltpu.VMEM((GROUP, rows, rank), BF16)],
    )
    return out


def solution(mesh):
    in_specs = (
        P(None, ("leaf", "level")),
        P(("leaf", "level"), None, None),
        P(("leaf", "level"), None, None, None),
        P(("leaf", "level"), None),
        P(("leaf", "level")),
        P(),
        P(),
        P(),
    )
    out_specs = P(None, ("leaf", "level"))
    return jax.shard_map(
        per_device, mesh=mesh, in_specs=in_specs, out_specs=out_specs, check_vma=False
    )
```

```python
from functools import partial

import jax
import jax.numpy as jnp
from jax import lax
from jax.experimental import pallas as pl
from jax.experimental.pallas import tpu as pltpu
from jax.sharding import PartitionSpec as P

VMEM_LIMIT = 32 * 1024 * 1024
F32 = jnp.float32
BF16 = jnp.bfloat16
GROUP = 4
SLOT = 3
TAIL = 16


def dot(a, b):
    return jnp.dot(a, b, preferred_element_type=F32)


def dot_t(a, b):
    return lax.dot_general(a, b, (((1,), (1,)), ((), ())), preferred_element_type=F32)


def call(kernel, name, inputs, scalars, outputs, scratch=(), inputs_in=pltpu.VMEM):
    shapes = [jax.ShapeDtypeStruct(shape, dtype) for shape, dtype in outputs]
    return pl.pallas_call(
        kernel,
        out_shape=shapes,
        in_specs=[pl.BlockSpec(memory_space=inputs_in)] * len(inputs)
        + [pl.BlockSpec(memory_space=pltpu.SMEM)] * len(scalars),
        out_specs=[pl.BlockSpec(memory_space=pltpu.VMEM)] * len(outputs),
        scratch_shapes=list(scratch),
        compiler_params=pltpu.CompilerParams(vmem_limit_bytes=VMEM_LIMIT),
        cost_estimate=pl.CostEstimate(flops=0, bytes_accessed=0, transcendentals=0),
        name=name,
    )(*(pltpu.with_memory_space_constraint(a, inputs_in) for a in inputs), *scalars)


def up_kernel(
    bits, x_hbm, basis_hbm, transfer_hbm, coupling_hbm, cols_hbm,
    keep_ref, send_ref, w_ref, x_ref, transfer_ref, coupling_ref, basis_ref, z_ref, cols_ref, sems
):
    pos = lax.axis_index("level")
    chip, core = pos >> 1, pos & 1
    pairs = (
        (basis_hbm.at[0], basis_ref), (transfer_hbm, transfer_ref), (x_hbm, x_ref),
        (coupling_hbm.at[:2], coupling_ref), (cols_hbm, cols_ref),
    )
    copies = [pltpu.make_async_copy(a, b, sems.at[i]) for i, (a, b) in enumerate(pairs)]
    for copy in copies:
        copy.start()
    copies[0].wait()
    copies[1].wait()
    w = basis_ref[...]
    for bit in range(bits):
        w = dot(w, transfer_ref[pos >> bit & 1]).astype(BF16)
    w_ref[...] = w
    copies[2].wait()
    z = dot(x_ref[...], w).astype(BF16)
    rows = z_ref.shape[1]
    for part in range(GROUP):
        z_ref[part] = z[part * rows : (part + 1) * rows]
    copies[4].wait()
    lanes = lax.broadcasted_iota(jnp.int32, (TAIL, z.shape[1]), 1)
    first = lanes < z.shape[1] // 2
    tail = jnp.where(first == (chip == 0), cols_ref[0, SLOT], 0).astype(F32).astype(BF16)
    for at, half in enumerate((chip, 1 - chip)):
        low = at * (rows + TAIL)
        keep_ref[low : low + rows] = z_ref[2 * core + half]
        send_ref[low : low + rows] = z_ref[2 * (1 - core) + half]
        keep_ref[low + rows : low + rows + TAIL] = tail
        send_ref[low + rows : low + rows + TAIL] = jnp.zeros_like(tail)
    copies[3].wait()


def fold_kernel(turns, pairs, clusters, coupling_ref, transfer_ref, mask_ref, *fold_refs):
    leaf_pos = lax.axis_index("leaf")
    pair, side = leaf_pos >> 1, leaf_pos & 1

    def switch(lev, gap, source, target):
        return mask_ref[lev, abs(gap) - 2, source if gap > 0 else target].astype(F32)

    def fill(fold_ref, distance, to_side):
        other = pair + distance
        through = None
        if abs(distance) in (2, 3) and clusters[1]:
            matrix = coupling_ref[1, abs(distance) - 2]
            on = switch(1, distance, pair, other)
            if distance > 0:
                through = dot(transfer_ref[to_side], matrix)
            else:
                through = dot_t(matrix, transfer_ref[to_side])
            through = (on * through).astype(BF16)
        for from_side in (0, 1):
            total = jnp.zeros(fold_ref.shape[1:], F32)
            if through is not None:
                product = dot_t if distance > 0 else dot
                total = product(transfer_ref[from_side], through)
            gap = 2 * distance + to_side - from_side
            if abs(gap) in (2, 3) and clusters[0]:
                matrix = coupling_ref[0, abs(gap) - 2].astype(F32)
                on = switch(0, gap, 2 * pair + from_side, 2 * other + to_side)
                total = total + on * (matrix.T if gap > 0 else matrix)
            fold_ref[from_side] = total.astype(BF16)

    for turn, fold_ref in zip(turns, fold_refs):
        for distance in reached(turn, pairs):
            if pairs == 4:
                inside = (pair ^ turn) == pair + distance
            else:
                inside = jnp.logical_and(pair + distance >= 0, pair + distance < pairs)
            for to_side in (0, 1):
                @pl.when(jnp.logical_and(inside, side == to_side))
                def _(fold_ref=fold_ref, distance=distance, to_side=to_side):
                    fill(fold_ref, distance, to_side)


def push_kernel(rows, count, own_ref, mate_ref, *refs):
    fold_refs, push_refs = refs[:count], refs[count:]
    side = lax.axis_index("leaf") & 1
    for fold_ref, push_ref in zip(fold_refs, push_refs):
        total = dot(own_ref[:rows], fold_ref[side]) + dot(mate_ref[:rows], fold_ref[1 - side])
        push_ref[:rows] = total.astype(BF16)
        push_ref[rows:] = mate_ref[rows:]


def reached(turn, pairs):
    return sorted({(i ^ turn) - i for i in range(pairs)}) if pairs == 4 else [turn]


def named_place(rows, ref):
    half = ref.shape[1] // 2
    cols = [jnp.max(ref[rows:, at : at + half].astype(F32)) for at in (0, half)]
    col = jnp.where(lax.axis_index("level") >> 1 == 0, cols[0], cols[1]).astype(jnp.int32)
    return lax.rem(col, GROUP)


def pick_block(place, blocks, out_ref):
    turn = place ^ lax.axis_index("level")
    for at, block in enumerate(blocks):
        @pl.when(turn == at)
        def _(block=block):
            out_ref[...] = block[...]


def pick_even_kernel(rows, named_ref, *refs):
    *blocks, out_ref = refs
    pick_block(named_place(rows, named_ref), blocks, out_ref)


def pick_odd_kernel(rows, pairs, named_refs_count, *refs):
    named_refs, blocks, out_ref = refs[:named_refs_count], refs[named_refs_count:-1], refs[-1]
    leaf_pos = lax.axis_index("leaf")
    pair, side = leaf_pos >> 1, leaf_pos & 1
    places = [named_place(rows, ref) for ref in named_refs]
    if pairs == 4:
        inner = jnp.logical_or(
            jnp.logical_and(pair == 1, side == 1), jnp.logical_and(pair == 2, side == 0)
        )
    else:
        inner = side == 1
    pick_block(jnp.where(inner, places[1], places[0]), blocks, out_ref)


def near_kernel(
    x_ref, mate_ref, across_ref, corner_ref, edge_ref, even_ref, odd_ref, tiles_ref,
    cols_ref, count_ref, acc_ref
):
    pos = lax.axis_index("level")
    side = lax.axis_index("leaf") & 1
    odd = pos & 1
    inner = jnp.logical_or(pos == 1, pos == 2)
    acc = dot(x_ref[...], tiles_ref[0, 0]) + dot(mate_ref[...], tiles_ref[0, 2 - odd])
    beside = jnp.where(inner, corner_ref[...], edge_ref[...])
    acc_ref[...] = acc + dot(beside, tiles_ref[0, 1 + odd])
    col = cols_ref[0, SLOT]
    group, turn = col // GROUP, lax.rem(col, GROUP) ^ pos
    live = count_ref[0] > SLOT
    from_even = (group == 0) == (side == 1)
    sources = [
        (jnp.logical_and(group == 1, turn == at), block)
        for at, block in enumerate((x_ref, mate_ref, across_ref, corner_ref))
    ] + [
        (jnp.logical_and(group != 1, from_even), even_ref),
        (jnp.logical_and(group != 1, jnp.logical_not(from_even)), odd_ref),
    ]
    for here, block in sources:
        @pl.when(jnp.logical_and(live, here))
        def _(block=block):
            acc_ref[...] += dot(block[...], tiles_ref[0, SLOT])


def finish_kernel(acc_ref, w_ref, field0, field1, field2, field3, out_ref, field_ref):
    pos = lax.axis_index("level")
    for turn, part_ref in enumerate((field0, field1, field2, field3)):
        field_ref[part_of(pos ^ turn)] = part_ref[...]
    field = jnp.concatenate([field_ref[part] for part in range(GROUP)], axis=0)
    out_ref[...] = (acc_ref[...] + dot_t(field, w_ref[...])).astype(BF16)


def part_of(pos):
    return 2 * (pos & 1) + (pos >> 1)


def turned(value, turn):
    return lax.ppermute(value, "level", [(i, i ^ turn) for i in range(GROUP)])


def shifted(value, steps):
    count = lax.axis_size("leaf")
    route = [(i, i + steps) for i in range(count) if 0 <= i + steps < count]
    return lax.ppermute(value, "leaf", route)


def swapped(value, distance):
    count = lax.axis_size("leaf")
    return lax.ppermute(value, "leaf", [(i, i ^ 1 << distance) for i in range(count)])


def neighbours(value, odd):
    count = lax.axis_size("leaf")
    route = [(i, i + 1) for i in range(odd, count - 1, 2)]
    return lax.ppermute(value, "leaf", route + [(b, a) for a, b in route])


def upper_field(coef, coupling, transfer, couple_mask):
    leaf_count = lax.axis_size("leaf")
    leaf_pos = lax.axis_index("leaf")
    couplings = []
    levels = range(2, min(coupling.shape[0], leaf_count.bit_length()))
    for lev in range(1, levels.stop):
        other = swapped(coef, lev - 1)
        is_upper = (leaf_pos >> lev - 1 & 1) == 1
        total = dot(jnp.where(is_upper, other, coef), transfer[0])
        total = total + dot(jnp.where(is_upper, coef, other), transfer[1])
        coef = total.astype(BF16)
        if lev not in levels:
            continue
        cluster = leaf_pos >> lev
        coupled = jnp.zeros(coef.shape, F32)
        for pick, offset in enumerate((2, 3)):
            if offset < leaf_count >> lev:
                matrix = coupling[lev, pick]
                ahead = shifted(coef, -(offset << lev))
                behind = shifted(coef, offset << lev)
                ahead_mask = couple_mask[lev, cluster, pick].astype(F32)
                behind_mask = couple_mask[lev, jnp.maximum(cluster - offset, 0), pick].astype(F32)
                coupled = coupled + ahead_mask * dot(ahead, matrix)
                coupled = coupled + behind_mask * dot_t(behind, matrix)
        couplings.append(coupled)
    field = jnp.zeros(coef.shape, F32)
    for lev, coupled in zip(reversed(levels), reversed(couplings)):
        if lev + 1 in levels:
            field = dot_t(field.astype(BF16), transfer[leaf_pos >> lev & 1])
        field = field + coupled
    for lev in (1, 0):
        field = dot_t(field.astype(BF16), transfer[leaf_pos >> lev & 1])
    return field


def per_device(
    points_x, leaf_basis, near_tiles, near_cols, near_count, transfer, coupling, couple_mask
):
    assert lax.axis_size("level") == GROUP
    leaf_count = lax.axis_size("leaf")
    vectors, points = points_x.shape
    rank = leaf_basis.shape[2]
    rows = vectors // GROUP
    bits = GROUP.bit_length() - 1
    block = ((vectors, points), BF16)
    part = ((rows, rank), BF16)
    tailed = ((rows + TAIL, rank), BF16)
    doubled = ((2 * (rows + TAIL), rank), BF16)

    keep, send, w, own_x, transfer_in, coupling_in = call(
        partial(up_kernel, bits), "up",
        [points_x, leaf_basis, transfer, coupling, near_cols], [],
        [doubled, doubled, ((points, rank), BF16), block, (transfer.shape, BF16),
         ((2,) + coupling.shape[1:], BF16)],
        [pltpu.VMEM((points, rank), BF16), pltpu.VMEM((GROUP, rows, rank), BF16),
         pltpu.SMEM(near_cols.shape, jnp.int32), pltpu.SemaphoreType.DMA((5,))],
        pltpu.HBM,
    )
    chip_sum = (keep.astype(F32) + turned(send, 1).astype(F32)).astype(BF16)
    came_half = turned(chip_sum[rows + TAIL :], 2)
    mate = turned(points_x, 1)
    active = min(coupling.shape[0], leaf_count.bit_length())
    pairs = leaf_count // 2
    turns = [2, 1, 3] if pairs == 4 else [2, 1, 3, -1, -2, -3]
    clusters = [lev < active and (leaf_count >> lev) > 2 for lev in (0, 1)]
    folds = call(
        partial(fold_kernel, turns, pairs, clusters), "fold", [coupling_in, transfer_in],
        [couple_mask.transpose(0, 2, 1)], [((2, rank, rank), BF16)] * len(turns),
    )
    mate, came_half, folds = lax.optimization_barrier((mate, came_half, folds))
    coef = (chip_sum[: rows + TAIL].astype(F32) + came_half.astype(F32)).astype(BF16)
    sent, coef = lax.optimization_barrier((points_x, coef))
    joints = [(GROUP * g - 1, GROUP * g) for g in range(1, leaf_count)]
    edge = lax.ppermute(sent, ("leaf", "level"), joints + [(b, a) for a, b in joints])
    beside = swapped(coef, 0)

    across = turned(points_x, 2)

    pushes = call(
        partial(push_kernel, rows, len(turns)), "push", [coef, beside, *folds], [],
        [tailed] * len(turns),
    )
    pushes = list(pushes)
    across, pushes = lax.optimization_barrier((across, pushes))
    corner = turned(across, 1)
    edge, corner, pushes[0] = lax.optimization_barrier((edge, corner, pushes[0]))
    held = [own_x, mate, across, corner]
    came = {}
    for turn, push in zip(turns, pushes):
        if pairs == 4:
            came[turn] = lax.ppermute(
                push, "leaf", [(i, i ^ 2 * turn) for i in range(leaf_count)]
            )
        else:
            came[turn] = shifted(push, 2 * turn)
    field = came[turns[0]][:rows].astype(F32)
    for turn in turns[1:]:
        field = field + came[turn][:rows].astype(F32)
    if active > 2 and (leaf_count >> 2) > 2:
        field = field + upper_field(coef[:rows], coupling, transfer, couple_mask)
    field = field.astype(BF16)

    (to_even,) = call(partial(pick_even_kernel, rows), "pick_even", [beside] + held, [], [block])
    from_even = neighbours(to_even, 0)
    named = [came[1], came[3 if pairs == 4 else -1]]
    (to_odd,) = call(
        partial(pick_odd_kernel, rows, pairs, len(named)), "pick_odd", named + held, [], [block]
    )

    fields = [field] + [turned(field, turn) for turn in range(1, GROUP)]
    from_odd = neighbours(to_odd, 1)
    (acc,) = call(
        near_kernel, "near", held + [edge, from_even, from_odd, near_tiles],
        [near_cols, near_count], [((vectors, points), F32)],
    )
    (out,) = call(
        finish_kernel, "finish", [acc, w] + fields, [], [block],
        [pltpu.VMEM((GROUP, rows, rank), BF16)],
    )
    return out


def solution(mesh):
    in_specs = (
        P(None, ("leaf", "level")),
        P(("leaf", "level"), None, None),
        P(("leaf", "level"), None, None, None),
        P(("leaf", "level"), None),
        P(("leaf", "level")),
        P(),
        P(),
        P(),
    )
    out_specs = P(None, ("leaf", "level"))
    return jax.shard_map(
        per_device, mesh=mesh, in_specs=in_specs, out_specs=out_specs, check_vma=False
    )
```

```python
from functools import partial

import jax
import jax.numpy as jnp
from jax import lax
from jax.experimental import pallas as pl
from jax.experimental.pallas import tpu as pltpu
from jax.sharding import PartitionSpec as P

VMEM_LIMIT = 32 * 1024 * 1024
F32 = jnp.float32
BF16 = jnp.bfloat16
GROUP = 4
SLOT = 3
TAIL = 16


def dot(a, b):
    return jnp.dot(a, b, preferred_element_type=F32)


def dot_t(a, b):
    return lax.dot_general(a, b, (((1,), (1,)), ((), ())), preferred_element_type=F32)


def call(kernel, name, inputs, scalars, outputs, scratch=(), inputs_in=pltpu.VMEM):
    shapes = [jax.ShapeDtypeStruct(shape, dtype) for shape, dtype in outputs]
    return pl.pallas_call(
        kernel,
        out_shape=shapes,
        in_specs=[pl.BlockSpec(memory_space=inputs_in)] * len(inputs)
        + [pl.BlockSpec(memory_space=pltpu.SMEM)] * len(scalars),
        out_specs=[pl.BlockSpec(memory_space=pltpu.VMEM)] * len(outputs),
        scratch_shapes=list(scratch),
        compiler_params=pltpu.CompilerParams(vmem_limit_bytes=VMEM_LIMIT),
        cost_estimate=pl.CostEstimate(flops=0, bytes_accessed=0, transcendentals=0),
        name=name,
    )(*(pltpu.with_memory_space_constraint(a, inputs_in) for a in inputs), *scalars)


def up_kernel(
    bits, x_hbm, basis_hbm, transfer_hbm, coupling_hbm, cols_hbm,
    keep_ref, send_ref, w_ref, x_ref, transfer_ref, coupling_ref, basis_ref, z_ref, cols_ref, sems
):
    pos = lax.axis_index("level")
    chip, core = pos >> 1, pos & 1
    pairs = (
        (basis_hbm.at[0], basis_ref), (transfer_hbm, transfer_ref), (x_hbm, x_ref),
        (coupling_hbm.at[:2], coupling_ref), (cols_hbm, cols_ref),
    )
    copies = [pltpu.make_async_copy(a, b, sems.at[i]) for i, (a, b) in enumerate(pairs)]
    for copy in copies:
        copy.start()
    copies[0].wait()
    copies[1].wait()
    w = basis_ref[...]
    for bit in range(bits):
        w = dot(w, transfer_ref[pos >> bit & 1]).astype(BF16)
    w_ref[...] = w
    copies[2].wait()
    z = dot(x_ref[...], w).astype(BF16)
    rows = z_ref.shape[1]
    for part in range(GROUP):
        z_ref[part] = z[part * rows : (part + 1) * rows]
    copies[4].wait()
    lanes = lax.broadcasted_iota(jnp.int32, (TAIL, z.shape[1]), 1)
    first = lanes < z.shape[1] // 2
    tail = jnp.where(first == (chip == 0), cols_ref[0, SLOT], 0).astype(F32).astype(BF16)
    for at, half in enumerate((chip, 1 - chip)):
        low = at * (rows + TAIL)
        keep_ref[low : low + rows] = z_ref[2 * core + half]
        send_ref[low : low + rows] = z_ref[2 * (1 - core) + half]
        keep_ref[low + rows : low + rows + TAIL] = tail
        send_ref[low + rows : low + rows + TAIL] = jnp.zeros_like(tail)
    copies[3].wait()


def fold_kernel(turns, pairs, clusters, coupling_ref, transfer_ref, mask_ref, *fold_refs):
    leaf_pos = lax.axis_index("leaf")
    pair, side = leaf_pos >> 1, leaf_pos & 1

    def switch(lev, gap, source, target):
        return mask_ref[lev, abs(gap) - 2, source if gap > 0 else target].astype(F32)

    def fill(fold_ref, distance, to_side):
        other = pair + distance
        through = None
        if abs(distance) in (2, 3) and clusters[1]:
            matrix = coupling_ref[1, abs(distance) - 2]
            on = switch(1, distance, pair, other)
            if distance > 0:
                through = dot(transfer_ref[to_side], matrix)
            else:
                through = dot_t(matrix, transfer_ref[to_side])
            through = (on * through).astype(BF16)
        for from_side in (0, 1):
            total = jnp.zeros(fold_ref.shape[1:], F32)
            if through is not None:
                product = dot_t if distance > 0 else dot
                total = product(transfer_ref[from_side], through)
            gap = 2 * distance + to_side - from_side
            if abs(gap) in (2, 3) and clusters[0]:
                matrix = coupling_ref[0, abs(gap) - 2].astype(F32)
                on = switch(0, gap, 2 * pair + from_side, 2 * other + to_side)
                total = total + on * (matrix.T if gap > 0 else matrix)
            fold_ref[from_side] = total.astype(BF16)

    for turn, fold_ref in zip(turns, fold_refs):
        for distance in reached(turn, pairs):
            if pairs == 4:
                inside = (pair ^ turn) == pair + distance
            else:
                inside = jnp.logical_and(pair + distance >= 0, pair + distance < pairs)
            for to_side in (0, 1):
                @pl.when(jnp.logical_and(inside, side == to_side))
                def _(fold_ref=fold_ref, distance=distance, to_side=to_side):
                    fill(fold_ref, distance, to_side)


def push_kernel(rows, count, own_ref, mate_ref, *refs):
    fold_refs, push_refs = refs[:count], refs[count:]
    side = lax.axis_index("leaf") & 1
    for fold_ref, push_ref in zip(fold_refs, push_refs):
        total = dot(own_ref[:rows], fold_ref[side]) + dot(mate_ref[:rows], fold_ref[1 - side])
        push_ref[:rows] = total.astype(BF16)
        push_ref[rows:] = mate_ref[rows:]


def reached(turn, pairs):
    return sorted({(i ^ turn) - i for i in range(pairs)}) if pairs == 4 else [turn]


def named_place(rows, ref):
    half = ref.shape[1] // 2
    cols = [jnp.max(ref[rows:, at : at + half].astype(F32)) for at in (0, half)]
    col = jnp.where(lax.axis_index("level") >> 1 == 0, cols[0], cols[1]).astype(jnp.int32)
    return lax.rem(col, GROUP)


def pick_block(place, blocks, out_ref):
    turn = place ^ lax.axis_index("level")
    for at, block in enumerate(blocks):
        @pl.when(turn == at)
        def _(block=block):
            out_ref[...] = block[...]


def pick_even_kernel(rows, named_ref, *refs):
    *blocks, out_ref = refs
    pick_block(named_place(rows, named_ref), blocks, out_ref)


def pick_odd_kernel(rows, pairs, named_refs_count, *refs):
    named_refs, blocks, out_ref = refs[:named_refs_count], refs[named_refs_count:-1], refs[-1]
    leaf_pos = lax.axis_index("leaf")
    pair, side = leaf_pos >> 1, leaf_pos & 1
    places = [named_place(rows, ref) for ref in named_refs]
    if pairs == 4:
        inner = jnp.logical_or(
            jnp.logical_and(pair == 1, side == 1), jnp.logical_and(pair == 2, side == 0)
        )
    else:
        inner = side == 1
    pick_block(jnp.where(inner, places[1], places[0]), blocks, out_ref)


def near_kernel(
    x_ref, mate_ref, across_ref, corner_ref, edge_ref, tiles_ref, cols_ref, count_ref, acc_ref
):
    pos = lax.axis_index("level")
    odd = pos & 1
    inner = jnp.logical_or(pos == 1, pos == 2)
    acc = dot(x_ref[...], tiles_ref[0, 0]) + dot(mate_ref[...], tiles_ref[0, 2 - odd])
    beside = jnp.where(inner, corner_ref[...], edge_ref[...])
    acc_ref[...] = acc + dot(beside, tiles_ref[0, 1 + odd])
    col = cols_ref[0, SLOT]
    turn = lax.rem(col, GROUP) ^ pos
    here = jnp.logical_and(count_ref[0] > SLOT, col // GROUP == 1)
    for at, block in enumerate((x_ref, mate_ref, across_ref, corner_ref)):
        @pl.when(jnp.logical_and(here, turn == at))
        def _(block=block):
            acc_ref[...] += dot(block[...], tiles_ref[0, SLOT])


def finish_kernel(
    acc_ref, even_ref, odd_ref, tiles_ref, w_ref, field0, field1, field2, field3,
    cols_ref, count_ref, out_ref, total_ref, field_ref
):
    pos = lax.axis_index("level")
    side = lax.axis_index("leaf") & 1
    for turn, part_ref in enumerate((field0, field1, field2, field3)):
        field_ref[part_of(pos ^ turn)] = part_ref[...]
    field = jnp.concatenate([field_ref[part] for part in range(GROUP)], axis=0)
    group = cols_ref[0, SLOT] // GROUP
    live = jnp.logical_and(count_ref[0] > SLOT, group != 1)
    from_even = (group == 0) == (side == 1)
    total = acc_ref[...] + dot_t(field, w_ref[...])

    @pl.when(jnp.logical_not(live))
    def _():
        out_ref[...] = total.astype(BF16)

    @pl.when(live)
    def _():
        total_ref[...] = total

    for here, block in ((from_even, even_ref), (jnp.logical_not(from_even), odd_ref)):
        @pl.when(jnp.logical_and(live, here))
        def _(block=block):
            out_ref[...] = (total_ref[...] + dot(block[...], tiles_ref[0, SLOT])).astype(BF16)


def part_of(pos):
    return 2 * (pos & 1) + (pos >> 1)


def turned(value, turn):
    return lax.ppermute(value, "level", [(i, i ^ turn) for i in range(GROUP)])


def shifted(value, steps):
    count = lax.axis_size("leaf")
    route = [(i, i + steps) for i in range(count) if 0 <= i + steps < count]
    return lax.ppermute(value, "leaf", route)


def swapped(value, distance):
    count = lax.axis_size("leaf")
    return lax.ppermute(value, "leaf", [(i, i ^ 1 << distance) for i in range(count)])


def neighbours(value, odd):
    count = lax.axis_size("leaf")
    route = [(i, i + 1) for i in range(odd, count - 1, 2)]
    return lax.ppermute(value, "leaf", route + [(b, a) for a, b in route])


def upper_field(coef, coupling, transfer, couple_mask):
    leaf_count = lax.axis_size("leaf")
    leaf_pos = lax.axis_index("leaf")
    couplings = []
    levels = range(2, min(coupling.shape[0], leaf_count.bit_length()))
    for lev in range(1, levels.stop):
        other = swapped(coef, lev - 1)
        is_upper = (leaf_pos >> lev - 1 & 1) == 1
        total = dot(jnp.where(is_upper, other, coef), transfer[0])
        total = total + dot(jnp.where(is_upper, coef, other), transfer[1])
        coef = total.astype(BF16)
        if lev not in levels:
            continue
        cluster = leaf_pos >> lev
        coupled = jnp.zeros(coef.shape, F32)
        for pick, offset in enumerate((2, 3)):
            if offset < leaf_count >> lev:
                matrix = coupling[lev, pick]
                ahead = shifted(coef, -(offset << lev))
                behind = shifted(coef, offset << lev)
                ahead_mask = couple_mask[lev, cluster, pick].astype(F32)
                behind_mask = couple_mask[lev, jnp.maximum(cluster - offset, 0), pick].astype(F32)
                coupled = coupled + ahead_mask * dot(ahead, matrix)
                coupled = coupled + behind_mask * dot_t(behind, matrix)
        couplings.append(coupled)
    field = jnp.zeros(coef.shape, F32)
    for lev, coupled in zip(reversed(levels), reversed(couplings)):
        if lev + 1 in levels:
            field = dot_t(field.astype(BF16), transfer[leaf_pos >> lev & 1])
        field = field + coupled
    for lev in (1, 0):
        field = dot_t(field.astype(BF16), transfer[leaf_pos >> lev & 1])
    return field


def per_device(
    points_x, leaf_basis, near_tiles, near_cols, near_count, transfer, coupling, couple_mask
):
    assert lax.axis_size("level") == GROUP
    leaf_count = lax.axis_size("leaf")
    vectors, points = points_x.shape
    rank = leaf_basis.shape[2]
    rows = vectors // GROUP
    bits = GROUP.bit_length() - 1
    block = ((vectors, points), BF16)
    part = ((rows, rank), BF16)
    tailed = ((rows + TAIL, rank), BF16)
    doubled = ((2 * (rows + TAIL), rank), BF16)

    keep, send, w, own_x, transfer_in, coupling_in = call(
        partial(up_kernel, bits), "up",
        [points_x, leaf_basis, transfer, coupling, near_cols], [],
        [doubled, doubled, ((points, rank), BF16), block, (transfer.shape, BF16),
         ((2,) + coupling.shape[1:], BF16)],
        [pltpu.VMEM((points, rank), BF16), pltpu.VMEM((GROUP, rows, rank), BF16),
         pltpu.SMEM(near_cols.shape, jnp.int32), pltpu.SemaphoreType.DMA((5,))],
        pltpu.HBM,
    )
    chip_sum = (keep.astype(F32) + turned(send, 1).astype(F32)).astype(BF16)
    came_half = turned(chip_sum[rows + TAIL :], 2)
    mate = turned(points_x, 1)
    active = min(coupling.shape[0], leaf_count.bit_length())
    pairs = leaf_count // 2
    turns = [2, 1, 3] if pairs == 4 else [2, 1, 3, -1, -2, -3]
    clusters = [lev < active and (leaf_count >> lev) > 2 for lev in (0, 1)]
    folds = call(
        partial(fold_kernel, turns, pairs, clusters), "fold", [coupling_in, transfer_in],
        [couple_mask.transpose(0, 2, 1)], [((2, rank, rank), BF16)] * len(turns),
    )
    mate, came_half, folds = lax.optimization_barrier((mate, came_half, folds))
    coef = (chip_sum[: rows + TAIL].astype(F32) + came_half.astype(F32)).astype(BF16)
    sent, coef = lax.optimization_barrier((points_x, coef))
    joints = [(GROUP * g - 1, GROUP * g) for g in range(1, leaf_count)]
    edge = lax.ppermute(sent, ("leaf", "level"), joints + [(b, a) for a, b in joints])
    beside = swapped(coef, 0)

    across = turned(points_x, 2)

    pushes = call(
        partial(push_kernel, rows, len(turns)), "push", [coef, beside, *folds], [],
        [tailed] * len(turns),
    )
    pushes = list(pushes)
    across, pushes = lax.optimization_barrier((across, pushes))
    corner = turned(across, 1)
    edge, corner, pushes[0] = lax.optimization_barrier((edge, corner, pushes[0]))
    held = [own_x, mate, across, corner]
    came = {}
    for turn, push in zip(turns, pushes):
        if pairs == 4:
            came[turn] = lax.ppermute(
                push, "leaf", [(i, i ^ 2 * turn) for i in range(leaf_count)]
            )
        else:
            came[turn] = shifted(push, 2 * turn)
    field = came[turns[0]][:rows].astype(F32)
    for turn in turns[1:]:
        field = field + came[turn][:rows].astype(F32)
    if active > 2 and (leaf_count >> 2) > 2:
        field = field + upper_field(coef[:rows], coupling, transfer, couple_mask)
    field = field.astype(BF16)

    (to_even,) = call(partial(pick_even_kernel, rows), "pick_even", [beside] + held, [], [block])
    from_even = neighbours(to_even, 0)
    named = [came[1], came[3 if pairs == 4 else -1]]
    (to_odd,) = call(
        partial(pick_odd_kernel, rows, pairs, len(named)), "pick_odd", named + held, [], [block]
    )
    (acc,) = call(
        near_kernel, "near", held + [edge, near_tiles], [near_cols, near_count],
        [((vectors, points), F32)],
    )
    fields = [field] + [turned(field, turn) for turn in range(1, GROUP)]
    from_odd = neighbours(to_odd, 1)
    (out,) = call(
        finish_kernel, "finish", [acc, from_even, from_odd, near_tiles, w] + fields,
        [near_cols, near_count], [block],
        [pltpu.VMEM((vectors, points), F32), pltpu.VMEM((GROUP, rows, rank), BF16)],
    )
    return out


def solution(mesh):
    in_specs = (
        P(None, ("leaf", "level")),
        P(("leaf", "level"), None, None),
        P(("leaf", "level"), None, None, None),
        P(("leaf", "level"), None),
        P(("leaf", "level")),
        P(),
        P(),
        P(),
    )
    out_specs = P(None, ("leaf", "level"))
    return jax.shard_map(
        per_device, mesh=mesh, in_specs=in_specs, out_specs=out_specs, check_vma=False
    )
```
